512 devices in a mesh: grp: 8 (over y, core), dev: 64 (over x, z).
Axes of the slice: x: 4, y: 4, z: 16, core: 2. Of those that a mesh axis runs over, the one named last changes fastest.
Arguments:
- tiles: bfloat16 [8, 3456, 64, 64], P('grp', 'dev'), may hold values from -0.15625 to 0.15625
- owner: int32 [8, 3456, 1], P('grp', 'dev'), may hold values from 0 to 63; in each aligned block of 54 rows (0 to 53, 54 to 107, ..., all dimensions but the last counted through in order) at most 2 rows name the same one
- tile_rows: int32 [8, 3456], P('grp', 'dev'), may hold values from 0 to 1
- tile_cols: int32 [8, 3456], P('grp', 'dev'), may hold values from 0 to 3
- ghost_rows: int32 [8, 128], P('grp', 'dev'), may hold values from 0 to 1
- rhs: float32 [8, 32, 8192], P('grp', None, 'dev')
- start: float32 [8, 32, 8192], P('grp', None, 'dev'), may hold values from -3 to 3
- diag: float32 [8, 8192], P('grp', 'dev'), may hold values from 2 to 20
Outputs:
- smoothed: float32 [8, 32, 8192], P('grp', None, 'dev')
- residual_rms: float32 [32], replicated
The draws below stay inside these ranges and needn't reach their ends.
Inputs may be any that keep to these rules, and one draw needn't show every extreme that they name: Among the 54 tiles held by one device, no owner is named more than 2 times, a bound that some block reaches.
All inputs are finite; a program needn't handle non-finite values.
Results may differ from the reference program's by a relative error of at most 0.0013.
Values may be sent and summed in bfloat16 or wider, within the bound.
A program may use at most 64 MiB of HBM per device.

```python
import math
import jax
import jax.numpy as jnp
import numpy as np
from jax import lax

BS = 64
RHS = 32
RB = 2
TILES_ROW = 27
STEPS = 3
TT = 54
GH = 1
CAP = 2
NDOF = 8192
N_GRP = 8
N_DEV = 64


def draw_rhs(key, part):
    key = jax.random.fold_in(key, 11)
    key_base, key_rows = jax.random.split(key)
    shape = (N_GRP, RHS, NDOF)
    position = (jnp.arange(N_GRP)[:, None] * NDOF + jnp.arange(NDOF)[None, :]).astype(jnp.float32) / (N_GRP * NDOF)
    rising = 1.0 + 2.0 * position
    row_scale = jnp.exp(jax.random.uniform(key_rows, (N_GRP, NDOF), jnp.float32, 0.0, math.log(10.0)))
    base = jax.random.normal(key_base, shape, jnp.float32)
    return (0.3 * base * row_scale[:, None, :] * rising[:, None, :]).astype(jnp.float32)


def set_ends(entries, key, least, top_value):
    shape = entries.shape
    spot = [jax.random.randint(jax.random.fold_in(key, axis), (), 0, shape[axis]) for axis in range(len(shape))]
    entries = entries.at[tuple(spot)].set(least)
    longest = shape.index(max(shape))
    spot[longest] = (spot[longest] + 1) % shape[longest]
    return entries.at[tuple(spot)].set(top_value)


def shard_levels(rng, extent, cuts, smallest, largest):
    loudness = 1.0
    for dim, blocks in cuts:
        heights = jax.random.uniform(jax.random.fold_in(jax.random.fold_in(rng, 6), dim), (blocks,), jnp.float32, smallest / len(cuts), largest / len(cuts))
        loudness = loudness * jnp.repeat(jnp.exp(heights), extent[dim] // blocks).reshape((-1,) + (1,) * (len(extent) - 1 - dim))
    return loudness


def routed_block(stream_key, own, number, rows, count, top, bound, lean):
    order = jax.random.permutation(stream_key, count)
    crowded, common = shares(count, rows * top, bound, lean, True), shares(count, rows * top, bound, lean, False)
    places = jnp.arange(count)

    def named(lengths, turn):
        used = int((lengths > 0).sum())
        fixed = max(1, used // 4)
        shifted = fixed + (places - fixed + turn * (used - fixed)) % max(1, count - fixed)
        return jnp.zeros((count,), jnp.int32).at[order[jnp.where(places < fixed, places, shifted)]].set(jnp.asarray(lengths, jnp.int32))

    lengths = jnp.where(number % 4 == 0, named(crowded, number // 4), named(common, number - number // 4 - 1))
    mixed = jax.random.permutation(jax.random.fold_in(own, 3), count)
    source_of, sink = mixed[0:count // 2 * 2:2], mixed[1:count // 2 * 2:2]
    slack = jnp.minimum(lengths[source_of] - 1, bound - lengths[sink]) // 2
    slack = jnp.where((source_of == order[0]) | (sink == order[0]) | (lengths[sink] == 0), 0, jnp.maximum(slack, 0))
    shifted = jax.random.randint(jax.random.fold_in(own, 4), (count // 2,), 0, 1 << 20) % (slack + 1)
    lengths = lengths.at[source_of].add(-shifted).at[sink].add(shifted)
    members = jnp.searchsorted(jnp.cumsum(lengths), jnp.arange(rows * top), side="right").astype(jnp.int32)
    listing = members.reshape(top, rows).T
    listing = listing[jax.random.permutation(jax.random.fold_in(own, 1), rows)]
    turn = jax.random.randint(jax.random.fold_in(own, 2), (rows, 1), 0, top)
    return jnp.take_along_axis(listing, (jnp.arange(top)[None, :] + turn) % top, axis=1)


def shares(number_of, total, reach, lean, full):
    portions = [(1 << 20) // math.isqrt(standing ** lean) + 1 for standing in range(1, number_of + 1)]
    largest = reach if full else min(reach, max(-(-total // number_of), total * portions[0] // sum(portions)))
    least = 1 if total - largest >= number_of - 1 else 0
    counts, rest = [largest] + [least] * (number_of - 1), total - largest - least * (number_of - 1)
    while rest > 0:
        movable = [i for i in range(1, number_of) if counts[i] < largest] or [i for i in range(1, number_of) if counts[i] < reach]
        whole, remaining = sum([portions[i] for i in movable]), rest
        for i in movable:
            extra = min(reach - counts[i], max(1, remaining * portions[i] // whole), rest)
            counts[i] = counts[i] + extra
            rest = rest - extra
    return np.array(counts)


def noise(key, shape, scale, most, cuts=(), held_as=jnp.bfloat16):
    level = shard_levels(key, shape, cuts, -0.22, 0.18) if cuts else 1.0
    entries = jax.random.normal(key, shape, jnp.float32) * scale * level
    return jnp.minimum(jnp.maximum(entries, -most), most).astype(held_as)


def setup_inputs(seed: int = 0) -> dict:
    seeds = jax.random.split(jax.random.key(seed), 9)
    tiles = noise(seeds[0], (N_GRP, N_DEV * TT, BS, BS), (BS * TILES_ROW) ** -0.5, 0.15625, ((0, 8), (1, 64)))
    owner_keys = jax.random.split(jax.random.fold_in(seeds[1], 1), N_GRP * (N_DEV * TT) // TT)
    owner_turns = jax.random.permutation(jax.random.fold_in(seeds[1], 3), N_GRP * (N_DEV * TT) // TT)
    owner = jax.vmap(lambda own, number: routed_block(jax.random.fold_in(seeds[1], 2), own, number, TT, N_DEV, 1, CAP, 2))(owner_keys, owner_turns).reshape((N_GRP, N_DEV * TT, 1))
    tile_rows = set_ends(jax.random.randint(seeds[2], (N_GRP, N_DEV * TT), 0, RB), jax.random.fold_in(seeds[2], 1), 0, RB - 1).astype(jnp.int32)
    tile_cols = set_ends(jax.random.randint(seeds[3], (N_GRP, N_DEV * TT), 0, RB + 2 * GH), jax.random.fold_in(seeds[3], 1), 0, (RB + 2 * GH) - 1).astype(jnp.int32)
    ghost_rows = set_ends(jax.random.randint(seeds[4], (N_GRP, N_DEV * 2 * GH), 0, RB), jax.random.fold_in(seeds[4], 1), 0, RB - 1).astype(jnp.int32)
    rhs = draw_rhs(jax.random.fold_in(seeds[8], 71), 0)
    start = noise(seeds[6], (N_GRP, RHS, NDOF), 0.5, 3.0, ((0, 8), (2, 64)), jnp.float32)
    diag = jnp.clip(jnp.exp(math.log(20.0) - 2.3025851 * jax.random.uniform(seeds[7], (N_GRP, NDOF), jnp.float32) ** shard_levels(seeds[7], (N_GRP, NDOF), ((0, 8), (1, 64)), -0.2, 0.2)), 2.0, 20.0)
    return dict(tiles=tiles, owner=owner, tile_rows=tile_rows, tile_cols=tile_cols, ghost_rows=ghost_rows, rhs=rhs, start=start, diag=diag)


def ghost_extend(low, ghosts):
    dev_ix = jnp.arange(N_DEV)[:, None]
    packed = low[:, dev_ix, ghosts]
    lower_part = packed[:, :, :GH]
    upper_part = packed[:, :, GH:]
    blank = jnp.zeros_like(upper_part[:, :1])
    from_lower = jnp.concatenate([blank, upper_part[:, :-1]], axis=1)
    from_upper = jnp.concatenate([lower_part[:, 1:], blank], axis=1)
    return jnp.concatenate([low, from_lower, from_upper], axis=2)

def apply_group(vec, tiles_g, owner_g, rows_g, cols_g, ghosts_g, diag_g):
    low = vec.astype(jnp.bfloat16)
    extended = ghost_extend(low, ghosts_g)
    gathered = extended[:, owner_g, cols_g]
    prod = jnp.einsum('tij,rtj->rti', tiles_g.astype(jnp.float32), gathered.astype(jnp.float32), precision=lax.Precision.HIGHEST)
    flat = owner_g * RB + rows_g
    summed = jnp.zeros((RHS, N_DEV * RB, BS), jnp.float32).at[:, flat].add(prod)
    return diag_g * vec + summed.reshape(RHS, N_DEV, RB, BS)

def reference(tiles, owner, tile_rows, tile_cols, ghost_rows, rhs, start, diag):
    lmax = 2.0
    lmin = 0.2
    theta = (lmax + lmin) / 2.0
    delta = (lmax - lmin) / 2.0
    sigma = theta / delta
    outs = []
    total = jnp.zeros((RHS,), jnp.float32)
    for group in range(N_GRP):
        tiles_g = tiles[group]
        owner_g = owner[group, :, 0]
        rows_g = tile_rows[group]
        cols_g = tile_cols[group]
        ghosts_g = ghost_rows[group].reshape(N_DEV, 2 * GH)
        diag_g = diag[group].reshape(1, N_DEV, RB, BS)

        def apply_op(vec):
            return apply_group(vec, tiles_g, owner_g, rows_g, cols_g, ghosts_g, diag_g)
        right = rhs[group].reshape(RHS, N_DEV, RB, BS)
        iterate = start[group].reshape(RHS, N_DEV, RB, BS)
        residual = right - apply_op(iterate)
        direction = residual / (theta * diag_g)
        rho = 1.0 / sigma
        for step in range(STEPS):
            iterate = iterate + direction
            residual = residual - apply_op(direction)
            if step + 1 < STEPS:
                rho_new = 1.0 / (2.0 * sigma - rho)
                direction = rho_new * rho * direction + 2.0 * rho_new / delta * residual / diag_g
                rho = rho_new
        outs.append(iterate.reshape(RHS, NDOF))
        total = total + lax.optimization_barrier(jnp.sum(residual * residual, axis=(1, 2, 3)))
    smoothed = jnp.stack(outs)
    residual_rms = jnp.sqrt(total / (N_GRP * NDOF))
    return (smoothed, residual_rms)
```

```python
import functools

import jax
import jax.numpy as jnp
from jax import lax
from jax.experimental import pallas as pl
from jax.experimental.pallas import tpu as pltpu
from jax.sharding import PartitionSpec as P

STEPS = 3
NZ = 16
CH = 4
MESH = pl.DeviceIdType.MESH


def kernel(
    ng, nx, nz,
    owner_s, rows_s, cols_s, ghost_s, tiles_hbm, rhs_ref, start_ref, diag_ref,
    out_ref, rms_ref,
    tiles_v, tab_v, tab_s, plc_send, plc, xsend, xbuf, rsend, rrecv, wmat,
    gsend, grecv, red_g, red_x, red_z,
    tile_sem, tab_sem, plc_ss, plc_rs, x_ss, x_rs, r_ss, r_rs, g_ss, g_rs,
    red_g_ss, red_g_rs, red_x_ss, red_x_rs, red_z_ss, red_z_rs,
):
    half = nz // 2
    ndev = nx * nz
    tcount = tiles_v.shape[0]
    dev = lax.axis_index("dev")
    grp = lax.axis_index("grp")
    x = lax.div(dev, nz)
    z = lax.rem(dev, nz)

    def x_peer(j):
        return {"dev": lax.rem(x + j, nx) * nz + z}

    def z_peer(k):
        return {"dev": x * nz + lax.rem(z + k, nz)}

    def g_peer(k):
        return {"grp": lax.rem(grp + k, ng)}

    upper = {"dev": lax.rem(dev + 1, ndev)}
    lower = {"dev": lax.rem(dev + ndev - 1, ndev)}

    tile_copy = pltpu.make_async_copy(tiles_hbm.at[0], tiles_v, tile_sem)
    tile_copy.start()

    barrier = pltpu.get_barrier_semaphore()
    peers = [x_peer(j) for j in range(1, nx)] + [z_peer(k) for k in range(1, nz)]
    peers += [g_peer(k) for k in range(1, ng)] + [upper, lower]
    for peer in peers:
        pl.semaphore_signal(barrier, inc=1, device_id=peer, device_id_type=MESH)

    lane = lax.broadcasted_iota(jnp.int32, (1, 128), 1)
    none = jnp.full((1, 128), -1, jnp.int32)

    def find(t, held):
        i0, i1, p0, p1 = held
        hit = lane == owner_s[0, t]
        place = rows_s[0, t] * 4 + cols_s[0, t]
        first = jnp.logical_and(hit, i0 < 0)
        second = jnp.logical_and(hit, i0 >= 0)
        return (
            jnp.where(first, t, i0), jnp.where(second, t, i1),
            jnp.where(first, place, p0), jnp.where(second, place, p1),
        )

    i0, i1, p0, p1 = lax.fori_loop(0, tcount, find, (none,) * 4, unroll=True)
    tab_v[0:1, :] = jnp.maximum(i0, 0)
    tab_v[1:2, :] = jnp.maximum(i1, 0)
    tab_v[2:3, :] = p0
    tab_v[3:4, :] = p1
    tab_copy = pltpu.make_async_copy(tab_v, tab_s, tab_sem)
    tab_copy.start()

    wide = lax.broadcasted_iota(jnp.int32, (rhs_ref.shape[1], 128), 1)
    left = wide < 64
    stay = jnp.where(left, ghost_s[0, 1], 1 - ghost_s[0, 0]) == 0

    def ghost_copies(n):
        return [
            pltpu.make_async_remote_copy(
                src_ref=gsend.at[n], dst_ref=grecv.at[n, way],
                send_sem=g_ss.at[n, way], recv_sem=g_rs.at[n, way],
                device_id=peer, device_id_type=MESH,
            )
            for way, peer in enumerate((upper, lower))
        ]

    def send_ghosts(n, vec):
        gsend[n] = jnp.where(stay, vec, pltpu.roll(vec, 64, 1)).astype(jnp.bfloat16)
        for copy in ghost_copies(n):
            copy.start()

    pl.semaphore_wait(barrier, len(peers))

    start = start_ref[0]
    send_ghosts(0, start)

    tab_copy.wait()

    def owner_of(j, fam, m):
        step = half - m if fam == 0 else m + nz - (half - 1)
        return lax.rem(x + j, nx) * nz + lax.rem(z + step, nz)

    def set_places(m, _):
        for j in range(nx):
            for fam in range(2):
                o = owner_of(j, fam, m)
                row = jnp.where(lane < 64, tab_s[2, o], tab_s[3, o])
                if j == 0:
                    plc[0, pl.ds(m * 2 + fam, 1), :] = row
                else:
                    plc_send[j, pl.ds(m * 2 + fam, 1), :] = row
        return 0

    lax.fori_loop(0, half, set_places, 0)

    def plc_copy(j):
        return pltpu.make_async_remote_copy(
            src_ref=plc_send.at[j], dst_ref=plc.at[j],
            send_sem=plc_ss.at[j - 1], recv_sem=plc_rs.at[j - 1],
            device_id=x_peer(j), device_id_type=MESH,
        )

    for j in range(1, nx):
        plc_copy(j).start()

    def x_copy(j, m):
        return pltpu.make_async_remote_copy(
            src_ref=xsend.at[j, m], dst_ref=xbuf.at[j, m],
            send_sem=x_ss.at[j - 1, m], recv_sem=x_rs.at[j - 1, m],
            device_id=x_peer(j), device_id_type=MESH,
        )

    tile_copy.wait()

    def pack(m, _):
        for j in list(range(1, nx)) + [0]:
            for fam in range(2):
                o = owner_of(j, fam, m)
                pair = jnp.concatenate([tiles_v[tab_s[0, o]], tiles_v[tab_s[1, o]]], axis=1)
                if j == 0:
                    xbuf[0, m, fam] = pair
                else:
                    xsend[j, m, fam] = pair
            if j:
                x_copy(j, m).start()
        return 0

    lax.fori_loop(0, half, pack, 0)

    for j in range(1, nx):
        plc_copy(j).wait_recv()

    right_half = (lane >= 64).astype(jnp.int32)

    def dense(fam, m):
        acc = [jnp.zeros((64, 128), jnp.float32) for _ in range(CH)]
        for j in range(nx):
            pair = xbuf[j, m, fam].astype(jnp.float32)
            swapped = pltpu.roll(pair, 64, 1)
            row = plc[j, pl.ds(m * 2 + fam, 1), :]
            row_swapped = pltpu.roll(row, 64, 1)
            for c in range(CH):
                target = (c // 2) * 4 + (c % 2) * 2 + right_half
                acc[c] += jnp.where(row == target, pair, 0.0)
                acc[c] += jnp.where(row_swapped == target, swapped, 0.0)
        for c in range(CH):
            rsend[fam, m, c] = acc[c]

    def prepare(m):
        for j in range(1, nx):
            x_copy(j, m).wait_recv()
        dense(0, m)
        dense(1, m)

    def ring_copy(way, s, c):
        return pltpu.make_async_remote_copy(
            src_ref=rsend.at[way, s, c], dst_ref=rrecv.at[way, s, c],
            send_sem=r_ss.at[way, s, c], recv_sem=r_rs.at[way, s, c],
            device_id=z_peer(1 if way == 0 else nz - 1), device_id_type=MESH,
        )

    def forward(way, s, c):
        ring_copy(way, s - 1, c).wait_recv()
        rsend[way, s, c] = rsend[way, s, c] + rrecv[way, s - 1, c]
        ring_copy(way, s, c).start()

    prepare(0)
    for c in range(CH):
        for way in range(2):
            ring_copy(way, 0, c).start()
    prepare(1)

    def ring(s, _):
        for c in range(CH):
            for way in range(2):
                forward(way, s, c)
        prepare(s + 1)
        return 0

    lax.fori_loop(1, half - 1, ring, 0)
    for c in range(CH):
        forward(0, half - 1, c)
    for c in range(CH):
        ring_copy(1, half - 2, c).wait_recv()
        ring_copy(0, half - 1, c).wait_recv()
        total = rsend[1, half - 1, c] + rrecv[1, half - 2, c] + rrecv[0, half - 1, c]
        high = total.astype(jnp.bfloat16)
        low = (total - high.astype(jnp.float32)).astype(jnp.bfloat16)
        r, cp = (c // 2) * 64, (c % 2) * 128
        wmat[r:r + 64, cp:cp + 128] = high
        wmat[128 + r:192 + r, cp:cp + 128] = low

    diag = diag_ref[...]
    inverse = 1.0 / diag
    from_lower = jnp.logical_and(left, dev > 0)
    from_upper = jnp.logical_and(jnp.logical_not(left), dev < ndev - 1)

    def apply_op(n, vec):
        for copy in ghost_copies(n):
            copy.wait_recv()
        ghosts = jnp.where(from_lower, grecv[n, 0].astype(jnp.float32), 0.0)
        ghosts = jnp.where(from_upper, grecv[n, 1].astype(jnp.float32), ghosts)
        extended = jnp.concatenate([vec, ghosts], axis=1).astype(jnp.bfloat16)
        both = lax.dot_general(
            extended, wmat[...], (((1,), (1,)), ((), ())), preferred_element_type=jnp.float32
        )
        return diag * vec + (both[:, :128] + both[:, 128:])

    lmax = 2.0
    lmin = 0.2
    theta = (lmax + lmin) / 2.0
    delta = (lmax - lmin) / 2.0
    sigma = theta / delta
    rho = 1.0 / sigma
    iterate = start
    residual = rhs_ref[0] - apply_op(0, start)
    direction = residual * (inverse * (1.0 / theta))
    for step in range(STEPS):
        send_ghosts(step + 1, direction)
        iterate = iterate + direction
        residual = residual - apply_op(step + 1, direction)
        if step + 1 < STEPS:
            rho_new = 1.0 / (2.0 * sigma - rho)
            direction = (rho_new * rho) * direction + (2.0 * rho_new / delta) * residual * inverse
            rho = rho_new
    out_ref[0] = iterate

    width = rhs_ref.shape[1]
    squares = jnp.sum((residual * residual).T, axis=0, keepdims=True)
    part = jnp.concatenate([squares, jnp.zeros((1, 128 - width), jnp.float32)], axis=1)
    sent = []
    for buf, ss, rs, here, count, peer in (
        (red_g, red_g_ss, red_g_rs, grp, ng, g_peer),
        (red_x, red_x_ss, red_x_rs, x, nx, x_peer),
        (red_z, red_z_ss, red_z_rs, z, nz, z_peer),
    ):
        buf[here] = part
        copies = [
            pltpu.make_async_remote_copy(
                src_ref=buf.at[here], dst_ref=buf.at[here],
                send_sem=ss.at[k - 1], recv_sem=rs.at[k - 1],
                device_id=peer(k), device_id_type=MESH,
            )
            for k in range(1, count)
        ]
        for copy in copies:
            copy.start()
        for k in range(1, count):
            other = lax.rem(here + count - k, count)
            pltpu.make_async_remote_copy(
                src_ref=buf.at[here], dst_ref=buf.at[other],
                send_sem=ss.at[k - 1], recv_sem=rs.at[k - 1],
                device_id=peer(k), device_id_type=MESH,
            ).wait_recv()
        part = buf[0]
        for k in range(1, count):
            part = part + buf[k]
        sent += copies
    rms_ref[...] = jnp.sqrt(part * (1.0 / (ng * ndev * 128)))[:, :width]

    for copy in sent:
        copy.wait_send()
    for n in range(STEPS + 1):
        for copy in ghost_copies(n):
            copy.wait_send()
    for j in range(1, nx):
        plc_copy(j).wait_send()

    def drain(s, _):
        for j in range(1, nx):
            x_copy(j, s).wait_send()
        for c in range(CH):
            ring_copy(0, s, c).wait_send()
        return 0

    lax.fori_loop(0, half, drain, 0)

    def drain_down(s, _):
        for c in range(CH):
            ring_copy(1, s, c).wait_send()
        return 0

    lax.fori_loop(0, half - 1, drain_down, 0)


def shards(ng, nx, nz, tiles, owner, tile_rows, tile_cols, ghost_rows, rhs, start, diag):
    tcount, block = tiles.shape[1], tiles.shape[2]
    width = rhs.shape[1]
    half = nz // 2
    f32, bf16, i32 = jnp.float32, jnp.bfloat16, jnp.int32
    dma = pltpu.SemaphoreType.DMA
    smem = pl.BlockSpec(memory_space=pltpu.SMEM)
    vmem = pl.BlockSpec(memory_space=pltpu.VMEM)
    smoothed, rms = pl.pallas_call(
        functools.partial(kernel, ng, nx, nz),
        out_shape=(
            jax.ShapeDtypeStruct((1, width, 128), f32),
            jax.ShapeDtypeStruct((1, width), f32),
        ),
        in_specs=[smem] * 4 + [pl.BlockSpec(memory_space=pl.ANY)] + [vmem] * 3,
        out_specs=(vmem, vmem),
        scratch_shapes=[
            pltpu.VMEM((tcount, block, block), bf16),
            pltpu.VMEM((8, 128), i32),
            pltpu.SMEM((8, 128), i32),
            pltpu.VMEM((nx, nz, 128), i32),
            pltpu.VMEM((nx, nz, 128), i32),
            pltpu.VMEM((nx, half, 2, 64, 128), bf16),
            pltpu.VMEM((nx, half, 2, 64, 128), bf16),
            pltpu.VMEM((2, half, CH, 64, 128), f32),
            pltpu.VMEM((2, half, CH, 64, 128), f32),
            pltpu.VMEM((256, 256), bf16),
            pltpu.VMEM((STEPS + 1, width, 128), bf16),
            pltpu.VMEM((STEPS + 1, 2, width, 128), bf16),
            pltpu.VMEM((ng, 1, 128), f32),
            pltpu.VMEM((nx, 1, 128), f32),
            pltpu.VMEM((nz, 1, 128), f32),
            dma,
            dma,
            dma((nx - 1,)),
            dma((nx - 1,)),
            dma((nx - 1, half)),
            dma((nx - 1, half)),
            dma((2, half, CH)),
            dma((2, half, CH)),
            dma((STEPS + 1, 2)),
            dma((STEPS + 1, 2)),
            dma((ng - 1,)),
            dma((ng - 1,)),
            dma((nx - 1,)),
            dma((nx - 1,)),
            dma((nz - 1,)),
            dma((nz - 1,)),
        ],
        compiler_params=pltpu.CompilerParams(
            collective_id=0, has_side_effects=True, vmem_limit_bytes=32 * 1024 * 1024
        ),
    )(owner.reshape(1, tcount), tile_rows, tile_cols, ghost_rows, tiles, rhs, start, diag)
    return smoothed, rms.reshape(width)


def solution(mesh):
    ng = mesh.shape["grp"]
    nx = mesh.shape["dev"] // NZ
    return jax.shard_map(
        functools.partial(shards, ng, nx, NZ),
        mesh=mesh,
        in_specs=(
            P("grp", "dev", None, None),
            P("grp", "dev", None),
            P("grp", "dev"),
            P("grp", "dev"),
            P("grp", "dev"),
            P("grp", None, "dev"),
            P("grp", None, "dev"),
            P("grp", "dev"),
        ),
        out_specs=(P("grp", None, "dev"), P()),
        check_vma=False,
    )
```

```python
import functools

import jax
import jax.numpy as jnp
from jax import lax
from jax.experimental import pallas as pl
from jax.experimental.pallas import tpu as pltpu
from jax.sharding import PartitionSpec as P

STEPS = 3
NZ = 16
CH = 4
MESH = pl.DeviceIdType.MESH


def kernel(
    ng, nx, nz,
    owner_h, rows_h, cols_h, ghost_h, tiles_h, rhs_h, start_h, diag_h,
    out_ref, rms_ref,
    owner_s, rows_s, cols_s, ghost_s, tiles_v, rhs_v, start_v, diag_v,
    tab_v, tab_s, po_send, po, pl_send, pl_recv, pq,
    osend, xown, lsend, lrecv, xleaf, dmat, qsend, qrecv, ssend, srecv, wmat,
    gsend, grecv, red_g, red_x, red_z,
    in_sem, tab_sem, po_ss, po_rs, pl_ss, pl_rs, pq_ss, pq_rs,
    o_ss, o_rs, l_ss, l_rs, y_ss, y_rs, q_ss, q_rs, s_ss, s_rs, g_ss, g_rs,
    red_g_ss, red_g_rs, red_x_ss, red_x_rs, red_z_ss, red_z_rs,
):
    half = nz // 2
    nk = half // 2
    ndev = nx * nz
    tcount = tiles_v.shape[0]
    width = rhs_v.shape[0]
    dev = lax.axis_index("dev")
    grp = lax.axis_index("grp")
    x = lax.div(dev, nz)
    z = lax.rem(dev, nz)

    def x_peer(j):
        return {"dev": lax.rem(x + j, nx) * nz + z}

    def z_peer(k):
        return {"dev": x * nz + lax.rem(z + k + nz, nz)}

    def g_peer(k):
        return {"grp": lax.rem(grp + k, ng)}

    upper = {"dev": lax.rem(dev + 1, ndev)}
    lower = {"dev": lax.rem(dev + ndev - 1, ndev)}

    fetches = [
        pltpu.make_async_copy(src, dst, in_sem.at[n])
        for n, (src, dst) in enumerate((
            (owner_h, owner_s), (rows_h, rows_s), (cols_h, cols_s), (ghost_h, ghost_s),
            (tiles_h.at[0], tiles_v), (start_h.at[0], start_v), (rhs_h.at[0], rhs_v),
            (diag_h, diag_v),
        ))
    ]
    for fetch in fetches:
        fetch.start()

    barrier = pltpu.get_barrier_semaphore()
    peers = [upper, lower, z_peer(1), z_peer(-1), z_peer(2), z_peer(-2)]
    peers += [x_peer(j) for j in range(1, nx)] + [g_peer(k) for k in range(1, ng)]
    for peer in peers:
        pl.semaphore_signal(barrier, inc=1, device_id=peer, device_id_type=MESH)

    lane = lax.broadcasted_iota(jnp.int32, (1, 128), 1)
    none = jnp.full((1, 128), -1, jnp.int32)
    for fetch in fetches[:4]:
        fetch.wait()

    def find(t, held):
        i0, i1, p0, p1 = held
        hit = lane == owner_s[0, t]
        place = rows_s[0, t] * 4 + cols_s[0, t]
        first = jnp.logical_and(hit, i0 < 0)
        second = jnp.logical_and(hit, i0 >= 0)
        return (
            jnp.where(first, t, i0), jnp.where(second, t, i1),
            jnp.where(first, place, p0), jnp.where(second, place, p1),
        )

    i0, i1, p0, p1 = lax.fori_loop(0, tcount, find, (none,) * 4, unroll=True)
    tab_v[0:1, :] = jnp.maximum(i0, 0)
    tab_v[1:2, :] = jnp.maximum(i1, 0)
    tab_v[2:3, :] = p0
    tab_v[3:4, :] = p1
    tab_copy = pltpu.make_async_copy(tab_v, tab_s, tab_sem)
    tab_copy.start()

    wide = lax.broadcasted_iota(jnp.int32, (width, 128), 1)
    left = wide < 64
    stay = jnp.where(left, ghost_s[0, 1], 1 - ghost_s[0, 0]) == 0

    def ghost_copies(n):
        return [
            pltpu.make_async_remote_copy(
                src_ref=gsend.at[n], dst_ref=grecv.at[n, way],
                send_sem=g_ss.at[n, way], recv_sem=g_rs.at[n, way],
                device_id=peer, device_id_type=MESH,
            )
            for way, peer in enumerate((upper, lower))
        ]

    def send_ghosts(n, vec):
        gsend[n] = jnp.where(stay, vec, pltpu.roll(vec, 64, 1)).astype(jnp.bfloat16)
        for copy in ghost_copies(n):
            copy.start()

    def remote(src, dst, ss, rs, peer):
        return pltpu.make_async_remote_copy(
            src_ref=src, dst_ref=dst, send_sem=ss, recv_sem=rs,
            device_id=peer, device_id_type=MESH,
        )

    def owner_of(j, step):
        return lax.rem(x + j, nx) * nz + lax.rem(z + step + nz, nz)

    def own_step(fam, k):
        if fam == 0:
            return half - 2 * k
        return 0 if k == 0 else 2 * k - half

    def leaf_step(way, k):
        return half - 1 - 2 * k if way == 0 else 2 * k + 1 - half

    def pair(o):
        return jnp.concatenate([tiles_v[tab_s[0, o]], tiles_v[tab_s[1, o]]], axis=1)

    def place(o):
        return jnp.where(lane < 64, tab_s[2, o], tab_s[3, o])

    def po_copy(j):
        return remote(po_send.at[j], po.at[j], po_ss.at[j - 1], po_rs.at[j - 1], x_peer(j))

    def pl_copy(way):
        return remote(
            pl_send.at[way], pl_recv.at[way], pl_ss.at[way], pl_rs.at[way],
            z_peer(1 if way == 0 else -1),
        )

    def pq_copy(j):
        return remote(pl_recv.at[:, j], pq.at[j], pq_ss.at[j - 1], pq_rs.at[j - 1], x_peer(j))

    def own_copy(j, k, fam):
        return remote(
            osend.at[j, k, fam], xown.at[j, k, fam],
            o_ss.at[j - 1, k, fam], o_rs.at[j - 1, k, fam], x_peer(j),
        )

    def leaf_copy(way, k):
        return remote(
            lsend.at[way, k], lrecv.at[k, way], l_ss.at[way, k], l_rs.at[way, k],
            z_peer(1 if way == 0 else -1),
        )

    def relay_copy(j, k):
        return remote(
            lrecv.at[k, :, j], xleaf.at[j, k], y_ss.at[j - 1, k], y_rs.at[j - 1, k], x_peer(j)
        )

    def pack_own(k, fam):
        for j in list(range(1, nx)) + [0]:
            both = pair(owner_of(j, own_step(fam, k)))
            if j:
                osend[j, k, fam] = both
                own_copy(j, k, fam).start()
            else:
                xown[0, k, fam] = both

    def pack_leaf(k):
        for way in range(2):
            for j in range(nx):
                lsend[way, k, j] = pair(owner_of(j, leaf_step(way, k)))
            leaf_copy(way, k).start()

    def relay(k):
        for way in range(2):
            leaf_copy(way, k).wait_recv()
        if k == 0:
            for way in range(2):
                pl_copy(way).wait_recv()
            for j in range(1, nx):
                pq_copy(j).start()
            pq[0] = pl_recv[:, 0]
        for j in range(1, nx):
            relay_copy(j, k).start()
        xleaf[0, k] = lrecv[k, :, 0]

    tab_copy.wait()
    fetches[4].wait()
    fetches[5].wait()
    start = start_v[...]
    for j in range(nx):
        for k in range(nk):
            for fam in range(2):
                row = place(owner_of(j, own_step(fam, k)))
                n = k * 2 + fam
                if j:
                    po_send[j, n:n + 1, :] = row
                else:
                    po[0, n:n + 1, :] = row
                pl_send[fam, j, k:k + 1, :] = place(owner_of(j, leaf_step(fam, k)))

    pl.semaphore_wait(barrier, len(peers))
    for j in range(1, nx):
        po_copy(j).start()
    pack_own(0, 0)
    for way in range(2):
        pl_copy(way).start()
    pack_leaf(0)
    for k in range(1, nk):
        pack_own(k, 0)
        pack_own(k, 1)
        pack_leaf(k)
    pack_own(0, 1)
    send_ghosts(0, start)

    right_half = (lane >= 64).astype(jnp.int32)

    def add_pair(acc, both, row):
        both = both.astype(jnp.float32)
        swapped = pltpu.roll(both, 64, 1)
        row_swapped = pltpu.roll(row, 64, 1)
        out = []
        for c in range(CH):
            target = (c // 2) * 4 + (c % 2) * 2 + right_half
            value = acc[c] + jnp.where(row == target, both, 0.0)
            out.append(value + jnp.where(row_swapped == target, swapped, 0.0))
        return tuple(out)

    def dense(n, own, leaves):
        k, fam = own
        for j in range(1, nx):
            own_copy(j, k, fam).wait_recv()

        def column(j, acc):
            acc = add_pair(acc, xown[j, k, fam], po[j, k * 2 + fam:k * 2 + fam + 1, :])
            for way, kk in leaves:
                acc = add_pair(acc, xleaf[j, kk, way], pq[j, way, kk:kk + 1, :])
            return acc

        acc = lax.fori_loop(
            0, nx, column, tuple(jnp.zeros((64, 128), jnp.float32) for _ in range(CH))
        )
        for c in range(CH):
            dmat[n, c] = acc[c]

    def chain_copies(way, s, h):
        peer = z_peer(2 if way == 0 else -2)
        return (
            remote(
                ssend.at[way, s, h], srecv.at[way, s, h], s_ss.at[way, s, h],
                s_rs.at[way, s, h], peer,
            ),
            remote(
                qsend.at[way, s, h], qrecv.at[way, s, h], q_ss.at[way, s, h],
                q_rs.at[way, s, h], peer,
            ),
        )

    def send_half(way, s, h, values):
        for cp in range(2):
            most = jnp.maximum(jnp.max(jnp.abs(values[cp]), axis=0, keepdims=True), 1e-30)
            scaled = jnp.round(values[cp] * (32767.0 / most))
            qsend[way, s, h, cp] = scaled.astype(jnp.int32).astype(jnp.int16)
            ssend[way, s, h, cp:cp + 1, :] = most * (1.0 / 32767.0)
        for copy in chain_copies(way, s, h):
            copy.start()

    def arrived(way, s, h, cp):
        whole = qrecv[way, s, h, cp].astype(jnp.int32).astype(jnp.float32)
        return whole * srecv[way, s, h, cp:cp + 1, :]

    def halves(way, s):
        return (way,) if s == 0 else (0, 1)

    for j in range(1, nx):
        po_copy(j).wait_recv()
    dense(0, (0, 0), ())
    for way in range(2):
        send_half(way, 0, way, [dmat[0, way * 2 + cp] for cp in range(2)])
    for k in range(nk):
        relay(k)
        if k == 0:
            for j in range(1, nx):
                pq_copy(j).wait_recv()
        for j in range(1, nx):
            relay_copy(j, k).wait_recv()
        s = k + 1
        if s < nk:
            for way in range(2):
                dense(way, (s, way), ((way, k),))
            for h in range(2):
                for way in range(2):
                    values = [dmat[way, h * 2 + cp] for cp in range(2)]
                    if h in halves(way, k):
                        for copy in chain_copies(way, k, h):
                            copy.wait_recv()
                        values = [values[cp] + arrived(way, k, h, cp) for cp in range(2)]
                    send_half(way, s, h, values)
    dense(0, (0, 1), ((0, nk - 1), (1, nk - 1)))
    for h in range(2):
        values = [dmat[0, h * 2 + cp] for cp in range(2)]
        for way in range(2):
            if h in halves(way, nk - 1):
                for copy in chain_copies(way, nk - 1, h):
                    copy.wait_recv()
                values = [values[cp] + arrived(way, nk - 1, h, cp) for cp in range(2)]
        for cp in range(2):
            high = values[cp].astype(jnp.bfloat16)
            low = (values[cp] - high.astype(jnp.float32)).astype(jnp.bfloat16)
            wmat[h * 64:h * 64 + 64, cp * 128:cp * 128 + 128] = high
            wmat[128 + h * 64:192 + h * 64, cp * 128:cp * 128 + 128] = low

    fetches[6].wait()
    fetches[7].wait()
    diag = diag_v[...]
    inverse = 1.0 / diag
    from_lower = jnp.logical_and(left, dev > 0)
    from_upper = jnp.logical_and(jnp.logical_not(left), dev < ndev - 1)

    def product(vec, columns):
        both = lax.dot_general(
            vec.astype(jnp.bfloat16), wmat[:, columns:columns + 128],
            (((1,), (1,)), ((), ())), preferred_element_type=jnp.float32,
        )
        return both[:, :128] + both[:, 128:]

    def own_part(vec):
        return diag * vec + product(vec, 0)

    def ghost_part(n):
        for copy in ghost_copies(n):
            copy.wait_recv()
        ghosts = jnp.where(from_lower, grecv[n, 0].astype(jnp.float32), 0.0)
        ghosts = jnp.where(from_upper, grecv[n, 1].astype(jnp.float32), ghosts)
        return product(ghosts, 128)

    lmax = 2.0
    lmin = 0.2
    theta = (lmax + lmin) / 2.0
    delta = (lmax - lmin) / 2.0
    sigma = theta / delta
    rho = 1.0 / sigma
    iterate = start
    residual = (rhs_v[...] - own_part(start)) - ghost_part(0)
    direction = residual * (inverse * (1.0 / theta))
    for step in range(STEPS):
        send_ghosts(step + 1, direction)
        iterate = iterate + direction
        rest = residual - own_part(direction)
        if step + 1 < STEPS:
            rho_new = 1.0 / (2.0 * sigma - rho)
            gain = (2.0 * rho_new / delta) * inverse
            kept = (rho_new * rho) * direction + gain * rest
            ghosts = ghost_part(step + 1)
            direction = kept - gain * ghosts
            residual = rest - ghosts
            rho = rho_new
        else:
            out_ref[0] = iterate
            residual = rest - ghost_part(step + 1)

    squares = jnp.sum((residual * residual).T, axis=0, keepdims=True)
    part = jnp.concatenate([squares, jnp.zeros((1, 128 - width), jnp.float32)], axis=1)
    sent = []
    for buf, ss, rs, here, count, peer in (
        (red_g, red_g_ss, red_g_rs, grp, ng, g_peer),
        (red_x, red_x_ss, red_x_rs, x, nx, x_peer),
        (red_z, red_z_ss, red_z_rs, z, nz, z_peer),
    ):
        buf[here] = part
        copies = [
            pltpu.make_async_remote_copy(
                src_ref=buf.at[here], dst_ref=buf.at[here],
                send_sem=ss.at[k - 1], recv_sem=rs.at[k - 1],
                device_id=peer(k), device_id_type=MESH,
            )
            for k in range(1, count)
        ]
        for copy in copies:
            copy.start()
        for k in range(1, count):
            other = lax.rem(here + count - k, count)
            pltpu.make_async_remote_copy(
                src_ref=buf.at[here], dst_ref=buf.at[other],
                send_sem=ss.at[k - 1], recv_sem=rs.at[k - 1],
                device_id=peer(k), device_id_type=MESH,
            ).wait_recv()
        part = buf[0]
        for k in range(1, count):
            part = part + buf[k]
        sent += copies
    rms_ref[...] = jnp.sqrt(part * (1.0 / (ng * ndev * 128)))[:, :width]

    for copy in sent:
        copy.wait_send()
    for n in range(STEPS + 1):
        for copy in ghost_copies(n):
            copy.wait_send()
    for way in range(2):
        pl_copy(way).wait_send()
        for k in range(nk):
            leaf_copy(way, k).wait_send()
            for h in halves(way, k):
                for copy in chain_copies(way, k, h):
                    copy.wait_send()
    for j in range(1, nx):
        po_copy(j).wait_send()
        pq_copy(j).wait_send()
        for k in range(nk):
            relay_copy(j, k).wait_send()
            for fam in range(2):
                own_copy(j, k, fam).wait_send()


def shards(ng, nx, nz, tiles, owner, tile_rows, tile_cols, ghost_rows, rhs, start, diag):
    tcount, block = tiles.shape[1], tiles.shape[2]
    width = rhs.shape[1]
    nk = nz // 4
    f32, bf16, i32, i16 = jnp.float32, jnp.bfloat16, jnp.int32, jnp.int16
    vmem, smem, dma = pltpu.VMEM, pltpu.SMEM, pltpu.SemaphoreType.DMA
    whole = pl.BlockSpec(memory_space=pltpu.VMEM)
    smoothed, rms = pl.pallas_call(
        functools.partial(kernel, ng, nx, nz),
        out_shape=(
            jax.ShapeDtypeStruct((1, width, 128), f32),
            jax.ShapeDtypeStruct((1, width), f32),
        ),
        in_specs=[pl.BlockSpec(memory_space=pltpu.HBM)] * 8,
        out_specs=(whole, whole),
        scratch_shapes=[
            smem((1, tcount), i32),
            smem((1, tcount), i32),
            smem((1, tcount), i32),
            smem((1, 2), i32),
            vmem((tcount, block, block), bf16),
            vmem((width, 128), f32),
            vmem((width, 128), f32),
            vmem((1, 128), f32),
            vmem((8, 128), i32),
            smem((8, 128), i32),
            vmem((nx, 2 * nk, 128), i32),
            vmem((nx, 2 * nk, 128), i32),
            vmem((2, nx, nk, 128), i32),
            vmem((2, nx, nk, 128), i32),
            vmem((nx, 2, nk, 128), i32),
            vmem((nx, nk, 2, 64, 128), bf16),
            vmem((nx, nk, 2, 64, 128), bf16),
            vmem((2, nk, nx, 64, 128), bf16),
            vmem((nk, 2, nx, 64, 128), bf16),
            vmem((nx, nk, 2, 64, 128), bf16),
            vmem((2, CH, 64, 128), f32),
            vmem((2, nk, 2, 2, 64, 128), i16),
            vmem((2, nk, 2, 2, 64, 128), i16),
            vmem((2, nk, 2, 2, 128), f32),
            vmem((2, nk, 2, 2, 128), f32),
            vmem((256, 256), bf16),
            vmem((STEPS + 1, width, 128), bf16),
            vmem((STEPS + 1, 2, width, 128), bf16),
            vmem((ng, 1, 128), f32),
            vmem((nx, 1, 128), f32),
            vmem((nz, 1, 128), f32),
            dma((8,)),
            dma,
            dma((nx - 1,)),
            dma((nx - 1,)),
            dma((2,)),
            dma((2,)),
            dma((nx - 1,)),
            dma((nx - 1,)),
            dma((nx - 1, nk, 2)),
            dma((nx - 1, nk, 2)),
            dma((2, nk)),
            dma((2, nk)),
            dma((nx - 1, nk)),
            dma((nx - 1, nk)),
            dma((2, nk, 2)),
            dma((2, nk, 2)),
            dma((2, nk, 2)),
            dma((2, nk, 2)),
            dma((STEPS + 1, 2)),
            dma((STEPS + 1, 2)),
            dma((ng - 1,)),
            dma((ng - 1,)),
            dma((nx - 1,)),
            dma((nx - 1,)),
            dma((nz - 1,)),
            dma((nz - 1,)),
        ],
        compiler_params=pltpu.CompilerParams(
            collective_id=0, has_side_effects=True, vmem_limit_bytes=32 * 1024 * 1024
        ),
    )(owner.reshape(1, tcount), tile_rows, tile_cols, ghost_rows, tiles, rhs, start, diag)
    return smoothed, rms.reshape(width)


def solution(mesh):
    ng = mesh.shape["grp"]
    nx = mesh.shape["dev"] // NZ
    return jax.shard_map(
        functools.partial(shards, ng, nx, NZ),
        mesh=mesh,
        in_specs=(
            P("grp", "dev", None, None),
            P("grp", "dev", None),
            P("grp", "dev"),
            P("grp", "dev"),
            P("grp", "dev"),
            P("grp", None, "dev"),
            P("grp", None, "dev"),
            P("grp", "dev"),
        ),
        out_specs=(P("grp", None, "dev"), P()),
        check_vma=False,
    )
```

```python
import functools

import jax
import jax.numpy as jnp
from jax import lax
from jax.experimental import pallas as pl
from jax.experimental.pallas import tpu as pltpu
from jax.sharding import PartitionSpec as P

STEPS = 3
NZ = 16
CH = 4
MESH = pl.DeviceIdType.MESH


def kernel(
    ng, nx, nz,
    owner_h, rows_h, cols_h, ghost_h, tiles_h, rhs_h, start_h, diag_h,
    out_ref, rms_ref,
    owner_s, rows_s, cols_s, ghost_s, tiles_v, rhs_v, start_v, diag_v,
    tab_v, tab_s, po_send, po, pl_send, pl_recv, pf_send, pf_recv,
    osend, xown, lsend, lrecv, fsend, frecv, dmat, qsend, qrecv, ssend, srecv, wmat,
    gsend, grecv, red_p, red_z,
    in_sem, tab_sem, po_ss, po_rs, pl_ss, pl_rs, pf_ss, pf_rs,
    o_ss, o_rs, l_ss, l_rs, f_ss, f_rs, q_ss, q_rs, s_ss, s_rs, g_ss, g_rs,
    red_p_ss, red_p_rs, red_z_ss, red_z_rs,
):
    half = nz // 2
    nk = half // 2
    ndev = nx * nz
    tcount = tiles_v.shape[0]
    width = rhs_v.shape[0]
    dev = lax.axis_index("dev")
    grp = lax.axis_index("grp")
    x = lax.div(dev, nz)
    z = lax.rem(dev, nz)

    def at(j, k):
        return {"dev": lax.rem(x + j, nx) * nz + lax.rem(z + k + nz, nz)}

    plane = grp * nx + x

    def plane_peer(n):
        there = lax.rem(plane + n, ng * nx)
        return {"grp": lax.div(there, nx), "dev": lax.rem(there, nx) * nz + z}

    def z_peer(n):
        return at(0, n)

    upper = {"dev": lax.rem(dev + 1, ndev)}
    lower = {"dev": lax.rem(dev + ndev - 1, ndev)}

    fetches = [
        pltpu.make_async_copy(src, dst, in_sem.at[n])
        for n, (src, dst) in enumerate((
            (owner_h, owner_s), (rows_h, rows_s), (cols_h, cols_s), (ghost_h, ghost_s),
            (tiles_h.at[0], tiles_v), (start_h.at[0], start_v), (rhs_h.at[0], rhs_v),
            (diag_h, diag_v),
        ))
    ]
    for fetch in fetches:
        fetch.start()

    barrier = pltpu.get_barrier_semaphore()
    peers = [upper, lower]
    peers += [at(j, k) for j in range(nx) for k in (-1, 1)]
    peers += [at(j, k) for j in range(nx) for k in (-2, 2)]
    peers += [plane_peer(n) for n in range(1, ng * nx)]
    for peer in peers:
        pl.semaphore_signal(barrier, inc=1, device_id=peer, device_id_type=MESH)

    lane = lax.broadcasted_iota(jnp.int32, (1, 128), 1)
    none = jnp.full((1, 128), -1, jnp.int32)
    for fetch in fetches[:4]:
        fetch.wait()

    def find(t, held):
        i0, i1, p0, p1 = held
        hit = lane == owner_s[0, t]
        place = rows_s[0, t] * 4 + cols_s[0, t]
        first = jnp.logical_and(hit, i0 < 0)
        second = jnp.logical_and(hit, i0 >= 0)
        return (
            jnp.where(first, t, i0), jnp.where(second, t, i1),
            jnp.where(first, place, p0), jnp.where(second, place, p1),
        )

    i0, i1, p0, p1 = lax.fori_loop(0, tcount, find, (none,) * 4, unroll=True)
    tab_v[0:1, :] = jnp.maximum(i0, 0)
    tab_v[1:2, :] = jnp.maximum(i1, 0)
    tab_v[2:3, :] = p0
    tab_v[3:4, :] = p1
    tab_copy = pltpu.make_async_copy(tab_v, tab_s, tab_sem)
    tab_copy.start()

    wide = lax.broadcasted_iota(jnp.int32, (width, 128), 1)
    left = wide < 64
    stay = jnp.where(left, ghost_s[0, 1], 1 - ghost_s[0, 0]) == 0

    def ghost_copies(n):
        return [
            pltpu.make_async_remote_copy(
                src_ref=gsend.at[n], dst_ref=grecv.at[n, way],
                send_sem=g_ss.at[n, way], recv_sem=g_rs.at[n, way],
                device_id=peer, device_id_type=MESH,
            )
            for way, peer in enumerate((upper, lower))
        ]

    def send_ghosts(n, vec):
        gsend[n] = jnp.where(stay, vec, pltpu.roll(vec, 64, 1)).astype(jnp.bfloat16)
        for copy in ghost_copies(n):
            copy.start()

    def remote(src, dst, ss, rs, peer):
        return pltpu.make_async_remote_copy(
            src_ref=src, dst_ref=dst, send_sem=ss, recv_sem=rs,
            device_id=peer, device_id_type=MESH,
        )

    def owner_of(j, step):
        return lax.rem(x + j, nx) * nz + lax.rem(z + step + nz, nz)

    def own_step(fam, k):
        if k == 0:
            return 0
        return half - 2 * k if fam == 0 else 2 * k - half

    def leaf_step(way, k):
        return half - 1 - 2 * k if way == 0 else 2 * k + 1 - half

    def pair(o):
        return jnp.concatenate([tiles_v[tab_s[0, o]], tiles_v[tab_s[1, o]]], axis=1)

    def place(o):
        return jnp.where(lane < 64, tab_s[2, o], tab_s[3, o])

    def po_copy(j):
        return remote(po_send.at[j], po.at[j], po_ss.at[j - 1], po_rs.at[j - 1], at(j, 0))

    def pl_copy(way, j):
        return remote(
            pl_send.at[way, j], pl_recv.at[way, j], pl_ss.at[way, j], pl_rs.at[way, j],
            at(j, 1 - 2 * way),
        )

    def pf_copy(j):
        return remote(pf_send.at[j], pf_recv.at[j], pf_ss.at[j], pf_rs.at[j], at(j, 2 - 4 * (j % 2)))

    def own_copy(j, k):
        count = 1 if k == 0 else 2
        return remote(
            osend.at[j, k, pl.ds(0, count)], xown.at[j, k, pl.ds(0, count)],
            o_ss.at[j - 1, k], o_rs.at[j - 1, k], at(j, 0),
        )

    def leaf_copy(way, k, j):
        return remote(
            lsend.at[way, k, j], lrecv.at[way, k, j], l_ss.at[way, k, j], l_rs.at[way, k, j],
            at(j, 1 - 2 * way),
        )

    def far_copy(j):
        return remote(fsend.at[j], frecv.at[j], f_ss.at[j], f_rs.at[j], at(j, 2 - 4 * (j % 2)))

    order = list(range(1, nx)) + [0]

    def pack_own(k):
        for j in order:
            for fam in range(1 if k == 0 else 2):
                both = pair(owner_of(j, own_step(fam, k)))
                if j:
                    osend[j, k, fam] = both
                else:
                    xown[0, k, fam] = both
            if j:
                own_copy(j, k).start()

    def pack_leaf(k):
        for j in order:
            for way in range(2):
                lsend[way, k, j] = pair(owner_of(j, leaf_step(way, k)))
                leaf_copy(way, k, j).start()

    def pack_far():
        for j in order:
            fsend[j] = pair(owner_of(j, half))
            far_copy(j).start()

    tab_copy.wait()
    fetches[4].wait()
    fetches[5].wait()
    start = start_v[...]
    for j in range(nx):
        pf_send[j] = place(owner_of(j, half))
        for k in range(nk):
            for fam in range(2):
                n = k * 2 + fam
                if n != 1:
                    row = place(owner_of(j, own_step(fam, k)))
                    if j:
                        po_send[j, n:n + 1, :] = row
                    else:
                        po[0, n:n + 1, :] = row
                pl_send[fam, j, k:k + 1, :] = place(owner_of(j, leaf_step(fam, k)))
        if j:
            po_send[j, 1:2, :] = none
        else:
            po[0, 1:2, :] = none

    pl.semaphore_wait(barrier, len(peers))
    for j in order:
        pf_copy(j).start()
        for way in range(2):
            pl_copy(way, j).start()
        if j:
            po_copy(j).start()
    pack_far()
    for k in range(1, nk):
        pack_leaf(k - 1)
        pack_own(k)
    pack_leaf(nk - 1)
    pack_own(0)
    send_ghosts(0, start)

    right_half = (lane >= 64).astype(jnp.int32)

    def add_pair(acc, both, row):
        both = both.astype(jnp.float32)
        swapped = pltpu.roll(both, 64, 1)
        row_swapped = pltpu.roll(row, 64, 1)
        out = []
        for c in range(CH):
            target = (c // 2) * 4 + (c % 2) * 2 + right_half
            value = acc[c] + jnp.where(row == target, both, 0.0)
            out.append(value + jnp.where(row_swapped == target, swapped, 0.0))
        return tuple(out)

    def dense(n, k, fam, leaves, far):
        acc = tuple(jnp.zeros((64, 128), jnp.float32) for _ in range(CH))
        for j in far:
            far_copy(j).wait_recv()
            acc = add_pair(acc, frecv[j], pf_recv[j])

        for way, kk in leaves:
            def leaf(j, acc, way=way, kk=kk):
                leaf_copy(way, kk, j).wait_recv()
                return add_pair(acc, lrecv[way, kk, j], pl_recv[way, j, kk:kk + 1, :])

            acc = lax.fori_loop(0, nx, leaf, acc)
        if fam == 0:
            for j in range(1, nx):
                own_copy(j, k).wait_recv()

        def own(j, acc):
            return add_pair(acc, xown[j, k, fam], po[j, k * 2 + fam:k * 2 + fam + 1, :])

        acc = lax.fori_loop(0, nx, own, acc)
        for c in range(CH):
            dmat[n, c] = acc[c]

    def chain_copies(way, s, h):
        peer = z_peer(2 if way == 0 else -2)
        return (
            remote(
                ssend.at[way, s, h], srecv.at[way, s, h], s_ss.at[way, s, h],
                s_rs.at[way, s, h], peer,
            ),
            remote(
                qsend.at[way, s, h], qrecv.at[way, s, h], q_ss.at[way, s, h],
                q_rs.at[way, s, h], peer,
            ),
        )

    def send_half(way, s, h, values):
        for cp in range(2):
            most = jnp.maximum(jnp.max(jnp.abs(values[cp]), axis=0, keepdims=True), 1e-30)
            scaled = jnp.round(values[cp] * (32767.0 / most))
            qsend[way, s, h, cp] = scaled.astype(jnp.int32).astype(jnp.int16)
            ssend[way, s, h, cp:cp + 1, :] = most * (1.0 / 32767.0)
        for copy in chain_copies(way, s, h):
            copy.start()

    def arrived(way, s, h, cp):
        whole = qrecv[way, s, h, cp].astype(jnp.int32).astype(jnp.float32)
        return whole * srecv[way, s, h, cp:cp + 1, :]

    for j in range(1, nx):
        po_copy(j).wait_recv()
    for j in range(nx):
        pf_copy(j).wait_recv()
        for way in range(2):
            pl_copy(way, j).wait_recv()
    for s in range(1, nk):
        for way in range(2):
            far = [j for j in range(nx) if j % 2 == way] if s == 1 else []
            dense(way, s, way, [(way, s - 1)], far)
        for h in range(2):
            for way in range(2):
                values = [dmat[way, h * 2 + cp] for cp in range(2)]
                if s > 1:
                    for copy in chain_copies(way, s - 1, h):
                        copy.wait_recv()
                    values = [values[cp] + arrived(way, s - 1, h, cp) for cp in range(2)]
                send_half(way, s, h, values)
    dense(0, 0, 0, [(0, nk - 1), (1, nk - 1)], [])
    for h in range(2):
        values = [dmat[0, h * 2 + cp] for cp in range(2)]
        for way in range(2):
            for copy in chain_copies(way, nk - 1, h):
                copy.wait_recv()
            values = [values[cp] + arrived(way, nk - 1, h, cp) for cp in range(2)]
        for cp in range(2):
            high = values[cp].astype(jnp.bfloat16)
            low = (values[cp] - high.astype(jnp.float32)).astype(jnp.bfloat16)
            wmat[h * 64:h * 64 + 64, cp * 128:cp * 128 + 128] = high
            wmat[128 + h * 64:192 + h * 64, cp * 128:cp * 128 + 128] = low

    fetches[6].wait()
    fetches[7].wait()
    diag = diag_v[...]
    inverse = 1.0 / diag
    from_lower = jnp.logical_and(left, dev > 0)
    from_upper = jnp.logical_and(jnp.logical_not(left), dev < ndev - 1)

    def product(vec, columns):
        both = lax.dot_general(
            vec.astype(jnp.bfloat16), wmat[:, columns:columns + 128],
            (((1,), (1,)), ((), ())), preferred_element_type=jnp.float32,
        )
        return both[:, :128] + both[:, 128:]

    def own_part(vec):
        return diag * vec + product(vec, 0)

    def ghost_part(n):
        for copy in ghost_copies(n):
            copy.wait_recv()
        ghosts = jnp.where(from_lower, grecv[n, 0].astype(jnp.float32), 0.0)
        ghosts = jnp.where(from_upper, grecv[n, 1].astype(jnp.float32), ghosts)
        return product(ghosts, 128)

    lmax = 2.0
    lmin = 0.2
    theta = (lmax + lmin) / 2.0
    delta = (lmax - lmin) / 2.0
    sigma = theta / delta
    rho = 1.0 / sigma
    iterate = start
    residual = (rhs_v[...] - own_part(start)) - ghost_part(0)
    direction = residual * (inverse * (1.0 / theta))
    for step in range(STEPS):
        send_ghosts(step + 1, direction)
        iterate = iterate + direction
        rest = residual - own_part(direction)
        if step + 1 < STEPS:
            rho_new = 1.0 / (2.0 * sigma - rho)
            gain = (2.0 * rho_new / delta) * inverse
            kept = (rho_new * rho) * direction + gain * rest
            ghosts = ghost_part(step + 1)
            direction = kept - gain * ghosts
            residual = rest - ghosts
            rho = rho_new
        else:
            out_ref[0] = iterate
            residual = rest - ghost_part(step + 1)

    squares = jnp.sum((residual * residual).T, axis=0, keepdims=True)
    part = jnp.concatenate([squares, jnp.zeros((1, 128 - width), jnp.float32)], axis=1)
    sent = []
    for buf, ss, rs, here, count, peer in (
        (red_p, red_p_ss, red_p_rs, plane, ng * nx, plane_peer),
        (red_z, red_z_ss, red_z_rs, z, nz, z_peer),
    ):
        buf[here] = part
        copies = [
            pltpu.make_async_remote_copy(
                src_ref=buf.at[here], dst_ref=buf.at[here],
                send_sem=ss.at[k - 1], recv_sem=rs.at[k - 1],
                device_id=peer(k), device_id_type=MESH,
            )
            for k in range(1, count)
        ]
        for copy in copies:
            copy.start()
        for k in range(1, count):
            other = lax.rem(here + count - k, count)
            pltpu.make_async_remote_copy(
                src_ref=buf.at[here], dst_ref=buf.at[other],
                send_sem=ss.at[k - 1], recv_sem=rs.at[k - 1],
                device_id=peer(k), device_id_type=MESH,
            ).wait_recv()
        part = buf[0]
        for k in range(1, count):
            part = part + buf[k]
        sent += copies
    rms_ref[...] = jnp.sqrt(part * (1.0 / (ng * ndev * 128)))[:, :width]

    for copy in sent:
        copy.wait_send()
    for n in range(STEPS + 1):
        for copy in ghost_copies(n):
            copy.wait_send()
    for j in range(nx):
        far_copy(j).wait_send()
        pf_copy(j).wait_send()
        if j:
            po_copy(j).wait_send()
        for way in range(2):
            pl_copy(way, j).wait_send()
        for k in range(nk):
            if j:
                own_copy(j, k).wait_send()
            for way in range(2):
                leaf_copy(way, k, j).wait_send()
    for s in range(1, nk):
        for way in range(2):
            for h in range(2):
                for copy in chain_copies(way, s, h):
                    copy.wait_send()


def shards(ng, nx, nz, tiles, owner, tile_rows, tile_cols, ghost_rows, rhs, start, diag):
    tcount, block = tiles.shape[1], tiles.shape[2]
    width = rhs.shape[1]
    nk = nz // 4
    f32, bf16, i32, i16 = jnp.float32, jnp.bfloat16, jnp.int32, jnp.int16
    vmem, smem, dma = pltpu.VMEM, pltpu.SMEM, pltpu.SemaphoreType.DMA
    whole = pl.BlockSpec(memory_space=pltpu.VMEM)
    smoothed, rms = pl.pallas_call(
        functools.partial(kernel, ng, nx, nz),
        out_shape=(
            jax.ShapeDtypeStruct((1, width, 128), f32),
            jax.ShapeDtypeStruct((1, width), f32),
        ),
        in_specs=[pl.BlockSpec(memory_space=pltpu.HBM)] * 8,
        out_specs=(whole, whole),
        scratch_shapes=[
            smem((1, tcount), i32),
            smem((1, tcount), i32),
            smem((1, tcount), i32),
            smem((1, 2), i32),
            vmem((tcount, block, block), bf16),
            vmem((width, 128), f32),
            vmem((width, 128), f32),
            vmem((1, 128), f32),
            vmem((8, 128), i32),
            smem((8, 128), i32),
            vmem((nx, 2 * nk, 128), i32),
            vmem((nx, 2 * nk, 128), i32),
            vmem((2, nx, nk, 128), i32),
            vmem((2, nx, nk, 128), i32),
            vmem((nx, 1, 128), i32),
            vmem((nx, 1, 128), i32),
            vmem((nx, nk, 2, 64, 128), bf16),
            vmem((nx, nk, 2, 64, 128), bf16),
            vmem((2, nk, nx, 64, 128), bf16),
            vmem((2, nk, nx, 64, 128), bf16),
            vmem((nx, 64, 128), bf16),
            vmem((nx, 64, 128), bf16),
            vmem((2, CH, 64, 128), f32),
            vmem((2, nk, 2, 2, 64, 128), i16),
            vmem((2, nk, 2, 2, 64, 128), i16),
            vmem((2, nk, 2, 2, 128), f32),
            vmem((2, nk, 2, 2, 128), f32),
            vmem((256, 256), bf16),
            vmem((STEPS + 1, width, 128), bf16),
            vmem((STEPS + 1, 2, width, 128), bf16),
            vmem((ng * nx, 1, 128), f32),
            vmem((nz, 1, 128), f32),
            dma((8,)),
            dma,
            dma((nx - 1,)),
            dma((nx - 1,)),
            dma((2, nx)),
            dma((2, nx)),
            dma((nx,)),
            dma((nx,)),
            dma((nx - 1, nk)),
            dma((nx - 1, nk)),
            dma((2, nk, nx)),
            dma((2, nk, nx)),
            dma((nx,)),
            dma((nx,)),
            dma((2, nk, 2)),
            dma((2, nk, 2)),
            dma((2, nk, 2)),
            dma((2, nk, 2)),
            dma((STEPS + 1, 2)),
            dma((STEPS + 1, 2)),
            dma((ng * nx - 1,)),
            dma((ng * nx - 1,)),
            dma((nz - 1,)),
            dma((nz - 1,)),
        ],
        compiler_params=pltpu.CompilerParams(
            collective_id=0, has_side_effects=True, vmem_limit_bytes=60 * 1024 * 1024
        ),
    )(owner.reshape(1, tcount), tile_rows, tile_cols, ghost_rows, tiles, rhs, start, diag)
    return smoothed, rms.reshape(width)


def solution(mesh):
    ng = mesh.shape["grp"]
    nx = mesh.shape["dev"] // NZ
    return jax.shard_map(
        functools.partial(shards, ng, nx, NZ),
        mesh=mesh,
        in_specs=(
            P("grp", "dev", None, None),
            P("grp", "dev", None),
            P("grp", "dev"),
            P("grp", "dev"),
            P("grp", "dev"),
            P("grp", None, "dev"),
            P("grp", None, "dev"),
            P("grp", "dev"),
        ),
        out_specs=(P("grp", None, "dev"), P()),
        check_vma=False,
    )
```

```python
import functools

import jax
import jax.numpy as jnp
from jax import lax
from jax.experimental import pallas as pl
from jax.experimental.pallas import tpu as pltpu
from jax.sharding import PartitionSpec as P

STEPS = 3
NZ = 16
CH = 4
MESH = pl.DeviceIdType.MESH


def kernel(
    ng, nx, nz,
    owner_h, rows_h, cols_h, ghost_h, tiles_h, rhs_h, start_h, diag_h,
    out_ref, rms_ref,
    owner_s, rows_s, cols_s, ghost_s, tiles_v, rhs_v, start_v, diag_v,
    tab_v, tab_s, psend, precv, bsend, xown, lrecv, frecv, dmat,
    qsend, qrecv, ssend, srecv, wmat, gsend, grecv, nsend, nrecv, wsend, wrecv, red_p, red_z,
    out_v, in_sem, tab_sem, out_sem, p_ss, p_rs, b_ss, o_rs, l_rs, f_rs,
    q_ss, q_rs, s_ss, s_rs, g_ss, g_rs, n_ss, n_rs, w_ss, w_rs,
    red_p_ss, red_p_rs, red_z_ss, red_z_rs,
):
    half = nz // 2
    nk = half // 2
    ndev = nx * nz
    tcount = tiles_v.shape[0]
    width = rhs_v.shape[0]
    dev = lax.axis_index("dev")
    grp = lax.axis_index("grp")
    x = lax.div(dev, nz)
    z = lax.rem(dev, nz)

    def at(j, k):
        return {"dev": lax.rem(x + j, nx) * nz + lax.rem(z + k + nz, nz)}

    plane = grp * nx + x

    def plane_peer(n):
        there = lax.rem(plane + n, ng * nx)
        return {"grp": lax.div(there, nx), "dev": lax.rem(there, nx) * nz + z}

    def z_peer(n):
        return at(0, n)

    upper = {"dev": lax.rem(dev + 1, ndev)}
    lower = {"dev": lax.rem(dev + ndev - 1, ndev)}
    upper2 = {"dev": lax.rem(dev + 2, ndev)}
    lower2 = {"dev": lax.rem(dev + ndev - 2, ndev)}

    fetches = [
        pltpu.make_async_copy(src, dst, in_sem.at[n])
        for n, (src, dst) in enumerate((
            (owner_h, owner_s), (rows_h, rows_s), (cols_h, cols_s), (ghost_h, ghost_s),
            (tiles_h.at[0], tiles_v), (start_h.at[0], start_v), (rhs_h.at[0], rhs_v),
            (diag_h, diag_v),
        ))
    ]
    for fetch in fetches:
        fetch.start()

    barrier = pltpu.get_barrier_semaphore()
    peers = [upper, lower, upper2, lower2]
    peers += [at(j, k) for j in range(nx) for k in (-1, 1)]
    peers += [at(j, k) for j in range(nx) for k in (-2, 2)]
    peers += [plane_peer(n) for n in range(1, ng * nx)]
    for peer in peers:
        pl.semaphore_signal(barrier, inc=1, device_id=peer, device_id_type=MESH)

    lane = lax.broadcasted_iota(jnp.int32, (1, 128), 1)
    none = jnp.full((1, 128), -1, jnp.int32)
    for fetch in fetches[:4]:
        fetch.wait()

    def find(t, held):
        i0, i1, p0, p1 = held
        hit = lane == owner_s[0, t]
        place = rows_s[0, t] * 4 + cols_s[0, t]
        first = jnp.logical_and(hit, i0 < 0)
        second = jnp.logical_and(hit, i0 >= 0)
        return (
            jnp.where(first, t, i0), jnp.where(second, t, i1),
            jnp.where(first, place, p0), jnp.where(second, place, p1),
        )

    i0, i1, p0, p1 = lax.fori_loop(0, tcount, find, (none,) * 4, unroll=True)
    tab_v[0:1, :] = jnp.maximum(i0, 0)
    tab_v[1:2, :] = jnp.maximum(i1, 0)
    tab_v[2:3, :] = p0
    tab_v[3:4, :] = p1
    tab_copy = pltpu.make_async_copy(tab_v, tab_s, tab_sem)
    tab_copy.start()

    wide = lax.broadcasted_iota(jnp.int32, (width, 128), 1)
    left = wide < 64
    stay = jnp.where(left, ghost_s[0, 1], 1 - ghost_s[0, 0]) == 0

    def pack_ghosts(vec):
        return jnp.where(stay[:vec.shape[0]], vec, pltpu.roll(vec, 64, 1))

    def remote(src, dst, ss, rs, peer):
        return pltpu.make_async_remote_copy(
            src_ref=src, dst_ref=dst, send_sem=ss, recv_sem=rs,
            device_id=peer, device_id_type=MESH,
        )

    def wait_bytes(ref, sem):
        pltpu.make_async_copy(ref, ref, sem).wait()

    def send_ghosts(n, vec):
        gsend[n] = pack_ghosts(vec).astype(jnp.bfloat16)
        for way, peer in enumerate((upper, lower)):
            remote(gsend.at[n], grecv.at[2 * n + way], g_ss, g_rs.at[n], peer).start()

    def owner_of(j, step):
        return lax.rem(x + j, nx) * nz + lax.rem(z + step + nz, nz)

    def own_step(fam, k):
        if k == 0:
            return 0
        return half - 2 * k if fam == 0 else 2 * k - half

    def leaf_step(way, k):
        return half - 1 - 2 * k if way == 0 else 2 * k + 1 - half

    def pair(o):
        return jnp.concatenate([tiles_v[tab_s[0, o]], tiles_v[tab_s[1, o]]], axis=1)

    def place(o):
        return jnp.where(lane < 64, tab_s[2, o], tab_s[3, o])

    oc = 2 * nk - 1
    leaf_row, far_row = nx * oc, nx * oc + 2 * nx * nk
    leaf_slot, own_slot = nx, nx + 2 * nk * nx

    def own_index(k, fam):
        return oc - 1 if k == 0 else 2 * (k - 1) + fam

    order = list(range(1, nx)) + [0]

    def send_places():
        for j in order:
            spans = [
                (leaf_row + (way * nx + j) * nk, nk, at(j, 1 - 2 * way)) for way in range(2)
            ]
            spans.append((far_row + j, 1, at(j, 2 - 4 * (j % 2))))
            if j:
                spans.append((j * oc, oc, at(j, 0)))
            for first, count, peer in spans:
                rows = pl.ds(first, count)
                remote(psend.at[rows], precv.at[rows], p_ss, p_rs, peer).start()

    def send_far():
        for j in order:
            remote(
                bsend.at[j], frecv.at[j], b_ss, f_rs.at[j % 2], at(j, 2 - 4 * (j % 2))
            ).start()

    def send_leaf(k):
        for j in order:
            for way in range(2):
                slot = leaf_slot + (way * nk + k) * nx + j
                remote(
                    bsend.at[slot], lrecv.at[way, k, j], b_ss, l_rs.at[way, k],
                    at(j, 1 - 2 * way),
                ).start()

    def send_own(k):
        count = 1 if k == 0 else 2
        for j in range(1, nx):
            slot = own_slot + (j - 1) * oc + own_index(k, 0)
            remote(
                bsend.at[pl.ds(slot, count)], xown.at[j, pl.ds(own_index(k, 0), count)],
                b_ss, o_rs.at[k], at(j, 0),
            ).start()

    tab_copy.wait()
    fetches[4].wait()
    fetches[5].wait()
    start = start_v[...]
    for j in range(nx):
        o = owner_of(j, half)
        psend[far_row + j] = place(o)
        bsend[j] = pair(o)
        for k in range(nk):
            for way in range(2):
                o = owner_of(j, leaf_step(way, k))
                psend[leaf_row + (way * nx + j) * nk + k] = place(o)
                bsend[leaf_slot + (way * nk + k) * nx + j] = pair(o)
            for fam in range(1 if k == 0 else 2):
                o = owner_of(j, own_step(fam, k))
                n = own_index(k, fam)
                if j:
                    psend[j * oc + n] = place(o)
                    bsend[own_slot + (j - 1) * oc + n] = pair(o)
                else:
                    precv[n] = place(o)
                    xown[0, n] = pair(o)

    pl.semaphore_wait(barrier, len(peers))
    send_far()
    send_leaf(0)
    send_own(1)
    send_places()
    for k in range(1, nk):
        send_leaf(k)
        send_own((k + 1) % nk)
    send_ghosts(0, start)

    right_half = (lane >= 64).astype(jnp.int32)

    def add_pair(acc, both, row):
        both = both.astype(jnp.float32)
        swapped = pltpu.roll(both, 64, 1)
        row_swapped = pltpu.roll(row, 64, 1)
        out = []
        for c in range(CH):
            target = (c // 2) * 4 + (c % 2) * 2 + right_half
            value = acc[c] + jnp.where(row == target, both, 0.0)
            out.append(value + jnp.where(row_swapped == target, swapped, 0.0))
        return tuple(out)

    def dense(n, k, fam, leaves, far):
        acc = tuple(jnp.zeros((64, 128), jnp.float32) for _ in range(CH))
        if far:
            wait_bytes(frecv.at[pl.ds(0, len(far))], f_rs.at[fam])
        for j in far:
            acc = add_pair(acc, frecv[j], precv[far_row + j])
        for way, kk in leaves:
            wait_bytes(lrecv.at[way, kk], l_rs.at[way, kk])
            for j in range(nx):
                row = leaf_row + (way * nx + j) * nk + kk
                acc = add_pair(acc, lrecv[way, kk, j], precv[row])
        if fam == 0:
            count = 1 if k == 0 else 2
            wait_bytes(
                xown.at[pl.ds(1, nx - 1), pl.ds(own_index(k, 0), count)], o_rs.at[k]
            )
        for j in range(nx):
            i = own_index(k, fam)
            acc = add_pair(acc, xown[j, i], precv[j * oc + i])
        for c in range(CH):
            dmat[n, c] = acc[c]

    def chain_copies(way, s, h):
        peer = z_peer(2 if way == 0 else -2)
        n = s - 1
        return (
            remote(ssend.at[way, n, h], srecv.at[way, n, h], s_ss, s_rs.at[way, n, h], peer),
            remote(qsend.at[way, n, h], qrecv.at[way, n, h], q_ss, q_rs.at[way, n, h], peer),
        )

    def send_half(way, s, h, values):
        for cp in range(2):
            most = jnp.maximum(jnp.max(jnp.abs(values[cp]), axis=0, keepdims=True), 1e-30)
            scaled = jnp.round(values[cp] * (32767.0 / most))
            qsend[way, s - 1, h, cp] = scaled.astype(jnp.int32).astype(jnp.int16)
            ssend[way, s - 1, h, cp:cp + 1, :] = most * (1.0 / 32767.0)
        for copy in chain_copies(way, s, h):
            copy.start()

    def arrived(way, s, h, cp):
        whole = qrecv[way, s - 1, h, cp].astype(jnp.int32).astype(jnp.float32)
        return whole * srecv[way, s - 1, h, cp:cp + 1, :]

    wait_bytes(precv.at[pl.ds(oc, far_row + nx - oc)], p_rs)
    for s in range(1, nk):
        for way in range(2):
            far = [j for j in range(nx) if j % 2 == way] if s == 1 else []
            dense(way, s, way, [(way, s - 1)], far)
        for h in range(2):
            for way in range(2):
                values = [dmat[way, h * 2 + cp] for cp in range(2)]
                if s > 1:
                    for copy in chain_copies(way, s - 1, h):
                        copy.wait_recv()
                    values = [values[cp] + arrived(way, s - 1, h, cp) for cp in range(2)]
                send_half(way, s, h, values)
    dense(0, 0, 0, [(0, nk - 1), (1, nk - 1)], [])
    ghost_rows = []
    for h in range(2):
        values = [dmat[0, h * 2 + cp] for cp in range(2)]
        for way in range(2):
            for copy in chain_copies(way, nk - 1, h):
                copy.wait_recv()
            values = [values[cp] + arrived(way, nk - 1, h, cp) for cp in range(2)]
        for cp in range(2):
            high = values[cp].astype(jnp.bfloat16)
            low = (values[cp] - high.astype(jnp.float32)).astype(jnp.bfloat16)
            wmat[h * 64:h * 64 + 64, cp * 128:cp * 128 + 128] = high
            wmat[128 + h * 64:192 + h * 64, cp * 128:cp * 128 + 128] = low
        ghost_rows.append(values[1])

    for way, peer in enumerate((upper, lower)):
        chosen = jnp.where(ghost_s[0, 1 - way] == 0, ghost_rows[0], ghost_rows[1])
        high = chosen.astype(jnp.bfloat16)
        nsend[way, 0:64, :] = high
        nsend[way, 64:128, :] = (chosen - high.astype(jnp.float32)).astype(jnp.bfloat16)
        remote(nsend.at[way], nrecv.at[way], n_ss, n_rs, peer).start()

    fetches[6].wait()
    fetches[7].wait()
    diag = diag_v[...]
    inverse = 1.0 / diag
    from_lower = jnp.logical_and(left, dev > 0)
    from_upper = jnp.logical_and(jnp.logical_not(left), dev < ndev - 1)

    def product(vec, columns):
        both = lax.dot_general(
            vec.astype(jnp.bfloat16), wmat[:, columns:columns + 128],
            (((1,), (1,)), ((), ())), preferred_element_type=jnp.float32,
        )
        return both[:, :128] + both[:, 128:]

    def own_part(vec):
        return diag * vec + product(vec, 0)

    def ghost_part(n):
        wait_bytes(grecv.at[pl.ds(2 * n, 2)], g_rs.at[n])
        ghosts = jnp.where(from_lower, grecv[2 * n].astype(jnp.float32), 0.0)
        ghosts = jnp.where(from_upper, grecv[2 * n + 1].astype(jnp.float32), ghosts)
        return product(ghosts, 128)

    def neighbour_part(vec, way):
        both = lax.dot_general(
            vec.astype(jnp.bfloat16), nrecv[way], (((1,), (1,)), ((), ())),
            preferred_element_type=jnp.float32,
        )
        return both + pltpu.roll(both, 64, 1)

    def next_ghosts(mine):
        far = jnp.where(
            jnp.logical_and(left, dev > 1), grecv[6].astype(jnp.float32), 0.0
        )
        below = jnp.where(left, far, mine)
        far = jnp.where(
            jnp.logical_and(jnp.logical_not(left), dev < ndev - 2),
            grecv[7].astype(jnp.float32), 0.0,
        )
        above = jnp.where(left, mine, far)
        summed = jnp.where(left, neighbour_part(below, 0), neighbour_part(above, 1))
        kept = jnp.where(left, wrecv[0, 0:width, :], wrecv[1, 0:width, :])
        scale = jnp.where(
            left[:8], wrecv[0, width:width + 8, :], wrecv[1, width:width + 8, :]
        )[0:1]
        ghosts = kept - scale * summed
        return jnp.where(jnp.logical_or(from_lower, from_upper), ghosts, 0.0)

    lmax = 2.0
    lmin = 0.2
    theta = (lmax + lmin) / 2.0
    delta = (lmax - lmin) / 2.0
    sigma = theta / delta
    rho = 1.0 / sigma
    iterate = start
    residual = (rhs_v[...] - own_part(start)) - ghost_part(0)
    direction = residual * (inverse * (1.0 / theta))
    for step in range(1, STEPS):
        send_ghosts(step, direction)
        if step == STEPS - 1:
            remote(gsend.at[step], grecv.at[6], g_ss, g_rs.at[STEPS], upper2).start()
            remote(gsend.at[step], grecv.at[7], g_ss, g_rs.at[STEPS], lower2).start()
        iterate = iterate + direction
        rest = residual - own_part(direction)
        rho_new = 1.0 / (2.0 * sigma - rho)
        gain = (2.0 * rho_new / delta) * inverse
        kept = (rho_new * rho) * direction + gain * rest
        if step == STEPS - 1:
            wsend[0:width, :] = pack_ghosts(kept)
            wsend[width:width + 8, :] = pack_ghosts(jnp.broadcast_to(gain, (8, 128)))
            for way, peer in enumerate((upper, lower)):
                remote(wsend, wrecv.at[way], w_ss, w_rs, peer).start()
        ghosts = ghost_part(step)
        direction = kept - gain * ghosts
        residual = rest - ghosts
        rho = rho_new
    out_v[...] = iterate + direction
    out_copy = pltpu.make_async_copy(out_v, out_ref.at[0], out_sem)
    out_copy.start()
    rest = residual - own_part(direction)
    wait_bytes(nrecv, n_rs)
    wait_bytes(grecv.at[pl.ds(6, 2)], g_rs.at[STEPS])
    wait_bytes(wrecv, w_rs)
    residual = rest - product(next_ghosts(gsend[STEPS - 1].astype(jnp.float32)), 128)

    squares = jnp.sum((residual * residual).T, axis=0, keepdims=True)
    part = jnp.concatenate([squares, jnp.zeros((1, 128 - width), jnp.float32)], axis=1)
    for buf, ss, rs, here, count, peer in (
        (red_p, red_p_ss, red_p_rs, plane, ng * nx, plane_peer),
        (red_z, red_z_ss, red_z_rs, z, nz, z_peer),
    ):
        buf[here] = part
        for n in range(1, count):
            remote(buf.at[here], buf.at[here], ss, rs, peer(n)).start()
        wait_bytes(buf.at[pl.ds(0, count - 1)], rs)
        part = buf[0]
        for n in range(1, count):
            part = part + buf[n]
    rms_ref[...] = jnp.sqrt(part * (1.0 / (ng * ndev * 128)))[:, :width]

    out_copy.wait()
    wait_bytes(psend.at[pl.ds(oc, far_row + nx - oc)], p_ss)
    wait_bytes(bsend, b_ss)
    wait_bytes(qsend, q_ss)
    wait_bytes(ssend, s_ss)
    wait_bytes(grecv, g_ss)
    wait_bytes(nsend, n_ss)
    wait_bytes(wrecv, w_ss)
    wait_bytes(red_p.at[pl.ds(0, ng * nx - 1)], red_p_ss)
    wait_bytes(red_z.at[pl.ds(0, nz - 1)], red_z_ss)


def shards(ng, nx, nz, tiles, owner, tile_rows, tile_cols, ghost_rows, rhs, start, diag):
    tcount, block = tiles.shape[1], tiles.shape[2]
    width = rhs.shape[1]
    nk = nz // 4
    f32, bf16, i32, i16 = jnp.float32, jnp.bfloat16, jnp.int32, jnp.int16
    vmem, smem, dma = pltpu.VMEM, pltpu.SMEM, pltpu.SemaphoreType.DMA
    whole = pl.BlockSpec(memory_space=pltpu.VMEM)
    smoothed, rms = pl.pallas_call(
        functools.partial(kernel, ng, nx, nz),
        out_shape=(
            jax.ShapeDtypeStruct((1, width, 128), f32),
            jax.ShapeDtypeStruct((1, width), f32),
        ),
        in_specs=[pl.BlockSpec(memory_space=pltpu.HBM)] * 8,
        out_specs=(pl.BlockSpec(memory_space=pltpu.HBM), whole),
        scratch_shapes=[
            smem((1, tcount), i32),
            smem((1, tcount), i32),
            smem((1, tcount), i32),
            smem((1, 2), i32),
            vmem((tcount, block, block), bf16),
            vmem((width, 128), f32),
            vmem((width, 128), f32),
            vmem((1, 128), f32),
            vmem((8, 128), i32),
            smem((8, 128), i32),
            vmem((nx * (4 * nk), 1, 128), i32),
            vmem((nx * (4 * nk), 1, 128), i32),
            vmem((nx + 2 * nk * nx + (nx - 1) * (2 * nk - 1), 64, 128), bf16),
            vmem((nx, 2 * nk - 1, 64, 128), bf16),
            vmem((2, nk, nx, 64, 128), bf16),
            vmem((nx, 64, 128), bf16),
            vmem((2, CH, 64, 128), f32),
            vmem((2, nk - 1, 2, 2, 64, 128), i16),
            vmem((2, nk - 1, 2, 2, 64, 128), i16),
            vmem((2, nk - 1, 2, 2, 128), f32),
            vmem((2, nk - 1, 2, 2, 128), f32),
            vmem((256, 256), bf16),
            vmem((STEPS, width, 128), bf16),
            vmem((2 * STEPS + 2, width, 128), bf16),
            vmem((2, 128, 128), bf16),
            vmem((2, 128, 128), bf16),
            vmem((width + 8, 128), f32),
            vmem((2, width + 8, 128), f32),
            vmem((ng * nx, 1, 128), f32),
            vmem((nz, 1, 128), f32),
            vmem((width, 128), f32),
            dma((8,)),
            dma,
            dma,
            dma,
            dma,
            dma,
            dma((nk,)),
            dma((2, nk)),
            dma((2,)),
            dma,
            dma((2, nk - 1, 2)),
            dma,
            dma((2, nk - 1, 2)),
            dma,
            dma((STEPS + 1,)),
            dma,
            dma,
            dma,
            dma,
            dma,
            dma,
            dma,
            dma,
        ],
        compiler_params=pltpu.CompilerParams(
            collective_id=0, has_side_effects=True, vmem_limit_bytes=60 * 1024 * 1024
        ),
    )(owner.reshape(1, tcount), tile_rows, tile_cols, ghost_rows, tiles, rhs, start, diag)
    return smoothed, rms.reshape(width)


def solution(mesh):
    ng = mesh.shape["grp"]
    nx = mesh.shape["dev"] // NZ
    return jax.shard_map(
        functools.partial(shards, ng, nx, NZ),
        mesh=mesh,
        in_specs=(
            P("grp", "dev", None, None),
            P("grp", "dev", None),
            P("grp", "dev"),
            P("grp", "dev"),
            P("grp", "dev"),
            P("grp", None, "dev"),
            P("grp", None, "dev"),
            P("grp", "dev"),
        ),
        out_specs=(P("grp", None, "dev"), P()),
        check_vma=False,
    )
```

```python
import functools

import jax
import jax.numpy as jnp
from jax import lax
from jax.experimental import pallas as pl
from jax.experimental.pallas import tpu as pltpu
from jax.sharding import PartitionSpec as P

STEPS = 3
NZ = 16
CH = 4
MESH = pl.DeviceIdType.MESH


def kernel(
    ng, nx, nz,
    owner_h, rows_h, cols_h, ghost_h, tiles_h, rhs_h, start_h, diag_h,
    out_ref, rms_ref,
    owner_s, rows_s, cols_s, ghost_s, tiles_v, rhs_v, start_v, diag_v,
    tab_v, tab_s, psend, precv, bsend, xown, lrecv, frecv, dmat,
    qsend, qrecv, ssend, srecv, wmat, gsend, grecv, nsend, nrecv, wsend, wrecv, red_p, red_z,
    out_v, in_sem, tab_sem, out_sem, p_ss, p_rs, b_ss, o_rs, l_rs, f_rs,
    q_ss, q_rs, s_ss, s_rs, g_ss, g_rs, n_ss, n_rs, w_ss, w_rs,
    red_p_ss, red_p_rs, red_z_ss, red_z_rs,
):
    half = nz // 2
    nk = half // 2
    ndev = nx * nz
    tcount = tiles_v.shape[0]
    width = rhs_v.shape[0]
    dev = lax.axis_index("dev")
    grp = lax.axis_index("grp")
    x = lax.div(dev, nz)
    z = lax.rem(dev, nz)

    def at(j, k):
        return {"dev": lax.rem(x + j, nx) * nz + lax.rem(z + k + nz, nz)}

    plane = grp * nx + x

    def plane_peer(n):
        there = lax.rem(plane + n, ng * nx)
        return {"grp": lax.div(there, nx), "dev": lax.rem(there, nx) * nz + z}

    def z_peer(n):
        return at(0, n)

    upper = {"dev": lax.rem(dev + 1, ndev)}
    lower = {"dev": lax.rem(dev + ndev - 1, ndev)}
    upper2 = {"dev": lax.rem(dev + 2, ndev)}
    lower2 = {"dev": lax.rem(dev + ndev - 2, ndev)}

    fetches = [
        pltpu.make_async_copy(src, dst, in_sem.at[n])
        for n, (src, dst) in enumerate((
            (owner_h, owner_s), (rows_h, rows_s), (cols_h, cols_s), (ghost_h, ghost_s),
            (tiles_h.at[0], tiles_v), (start_h.at[0], start_v), (rhs_h.at[0], rhs_v),
            (diag_h, diag_v),
        ))
    ]
    for fetch in fetches:
        fetch.start()

    barrier = pltpu.get_barrier_semaphore()
    peers = [upper, lower, upper2, lower2]
    peers += [at(j, k) for j in range(nx) for k in (-1, 1)]
    peers += [at(j, k) for j in range(nx) for k in (-2, 2)]
    peers += [plane_peer(n) for n in range(1, ng * nx)]
    for peer in peers:
        pl.semaphore_signal(barrier, inc=1, device_id=peer, device_id_type=MESH)

    lane = lax.broadcasted_iota(jnp.int32, (1, 128), 1)
    none = jnp.full((1, 128), -1, jnp.int32)
    for fetch in fetches[:4]:
        fetch.wait()

    def find(t, held):
        i0, i1, p0, p1 = held
        hit = lane == owner_s[0, t]
        place = rows_s[0, t] * 4 + cols_s[0, t]
        first = jnp.logical_and(hit, i0 < 0)
        second = jnp.logical_and(hit, i0 >= 0)
        return (
            jnp.where(first, t, i0), jnp.where(second, t, i1),
            jnp.where(first, place, p0), jnp.where(second, place, p1),
        )

    i0, i1, p0, p1 = lax.fori_loop(0, tcount, find, (none,) * 4, unroll=True)
    tab_v[0:1, :] = jnp.maximum(i0, 0)
    tab_v[1:2, :] = jnp.maximum(i1, 0)
    tab_v[2:3, :] = p0
    tab_v[3:4, :] = p1
    tab_copy = pltpu.make_async_copy(tab_v, tab_s, tab_sem)
    tab_copy.start()

    wide = lax.broadcasted_iota(jnp.int32, (width, 128), 1)
    left = wide < 64
    stay = jnp.where(left, ghost_s[0, 1], 1 - ghost_s[0, 0]) == 0

    def pack_ghosts(vec):
        return jnp.where(stay[:vec.shape[0]], vec, pltpu.roll(vec, 64, 1))

    def remote(src, dst, ss, rs, peer):
        return pltpu.make_async_remote_copy(
            src_ref=src, dst_ref=dst, send_sem=ss, recv_sem=rs,
            device_id=peer, device_id_type=MESH,
        )

    def wait_bytes(ref, sem):
        pltpu.make_async_copy(ref, ref, sem).wait()

    def send_ghosts(n, vec):
        gsend[n] = pack_ghosts(vec).astype(jnp.bfloat16)
        for way, peer in enumerate((upper, lower)):
            remote(gsend.at[n], grecv.at[2 * n + way], g_ss, g_rs.at[n], peer).start()

    def owner_of(j, step):
        return lax.rem(x + j, nx) * nz + lax.rem(z + step + nz, nz)

    def own_step(fam, k):
        if k == 0:
            return 0
        return half - 2 * k if fam == 0 else 2 * k - half

    def leaf_step(way, k):
        return half - 1 - 2 * k if way == 0 else 2 * k + 1 - half

    def pair(o):
        return jnp.concatenate([tiles_v[tab_s[0, o]], tiles_v[tab_s[1, o]]], axis=1)

    def place(o):
        return jnp.where(lane < 64, tab_s[2, o], tab_s[3, o])

    oc = 2 * nk - 1
    leaf_row, far_row = nx * oc, nx * oc + 2 * nx * nk
    leaf_slot, own_slot = nx, nx + 2 * nk * nx

    def own_index(k, fam):
        return oc - 1 if k == 0 else 2 * (k - 1) + fam

    order = list(range(1, nx)) + [0]

    def send_places():
        for j in order:
            spans = [
                (leaf_row + (way * nx + j) * nk, nk, at(j, 1 - 2 * way)) for way in range(2)
            ]
            spans.append((far_row + j, 1, at(j, 2 - 4 * (j % 2))))
            if j:
                spans.append((j * oc, oc, at(j, 0)))
            for first, count, peer in spans:
                rows = pl.ds(first, count)
                remote(psend.at[rows], precv.at[rows], p_ss, p_rs, peer).start()

    def send_far():
        for j in order:
            remote(
                bsend.at[j], frecv.at[j], b_ss, f_rs.at[j % 2], at(j, 2 - 4 * (j % 2))
            ).start()

    def send_leaf(k):
        for j in order:
            for way in range(2):
                slot = leaf_slot + (way * nk + k) * nx + j
                remote(
                    bsend.at[slot], lrecv.at[way, k, j], b_ss, l_rs.at[way, k],
                    at(j, 1 - 2 * way),
                ).start()

    def send_own(k):
        count = 1 if k == 0 else 2
        for j in range(1, nx):
            slot = own_slot + (j - 1) * oc + own_index(k, 0)
            remote(
                bsend.at[pl.ds(slot, count)], xown.at[j, pl.ds(own_index(k, 0), count)],
                b_ss, o_rs.at[k], at(j, 0),
            ).start()

    tab_copy.wait()
    fetches[4].wait()
    fetches[5].wait()
    start = start_v[...]
    for j in range(nx):
        o = owner_of(j, half)
        psend[far_row + j] = place(o)
        bsend[j] = pair(o)
        for k in range(nk):
            for way in range(2):
                o = owner_of(j, leaf_step(way, k))
                psend[leaf_row + (way * nx + j) * nk + k] = place(o)
                bsend[leaf_slot + (way * nk + k) * nx + j] = pair(o)
            for fam in range(1 if k == 0 else 2):
                o = owner_of(j, own_step(fam, k))
                n = own_index(k, fam)
                if j:
                    psend[j * oc + n] = place(o)
                    bsend[own_slot + (j - 1) * oc + n] = pair(o)
                else:
                    precv[n] = place(o)
                    xown[0, n] = pair(o)

    pl.semaphore_wait(barrier, len(peers))
    send_far()
    send_leaf(0)
    send_own(1)
    send_places()
    send_leaf(1)
    send_own(2 % nk)
    send_ghosts(0, start)

    right_half = (lane >= 64).astype(jnp.int32)

    def add_pair(acc, both, row):
        both = both.astype(jnp.float32)
        swapped = pltpu.roll(both, 64, 1)
        row_swapped = pltpu.roll(row, 64, 1)
        out = []
        for c in range(CH):
            target = (c // 2) * 4 + (c % 2) * 2 + right_half
            value = acc[c] + jnp.where(row == target, both, 0.0)
            out.append(value + jnp.where(row_swapped == target, swapped, 0.0))
        return tuple(out)

    def dense(n, k, fam, leaves, far):
        acc = tuple(jnp.zeros((64, 128), jnp.float32) for _ in range(CH))
        if far:
            wait_bytes(frecv.at[pl.ds(0, len(far))], f_rs.at[fam])
        for j in far:
            acc = add_pair(acc, frecv[j], precv[far_row + j])
        for way, kk in leaves:
            wait_bytes(lrecv.at[way, kk], l_rs.at[way, kk])
            for j in range(nx):
                row = leaf_row + (way * nx + j) * nk + kk
                acc = add_pair(acc, lrecv[way, kk, j], precv[row])
        if fam == 0:
            count = 1 if k == 0 else 2
            wait_bytes(
                xown.at[pl.ds(1, nx - 1), pl.ds(own_index(k, 0), count)], o_rs.at[k]
            )
        for j in range(nx):
            i = own_index(k, fam)
            acc = add_pair(acc, xown[j, i], precv[j * oc + i])
        for c in range(CH):
            dmat[n, c] = acc[c]

    def chain_copies(way, s, h):
        peer = z_peer(2 if way == 0 else -2)
        n = s - 1
        return (
            remote(ssend.at[way, n, h], srecv.at[way, n, h], s_ss, s_rs.at[way, n, h], peer),
            remote(qsend.at[way, n, h], qrecv.at[way, n, h], q_ss, q_rs.at[way, n, h], peer),
        )

    def send_half(way, s, h, values):
        for cp in range(2):
            most = jnp.maximum(jnp.max(jnp.abs(values[cp]), axis=0, keepdims=True), 1e-30)
            scaled = jnp.round(values[cp] * (32767.0 / most))
            qsend[way, s - 1, h, cp] = scaled.astype(jnp.int32).astype(jnp.int16)
            ssend[way, s - 1, h, cp:cp + 1, :] = most * (1.0 / 32767.0)
        for copy in chain_copies(way, s, h):
            copy.start()

    def arrived(way, s, h, cp):
        whole = qrecv[way, s - 1, h, cp].astype(jnp.int32).astype(jnp.float32)
        return whole * srecv[way, s - 1, h, cp:cp + 1, :]

    wait_bytes(precv.at[pl.ds(oc, far_row + nx - oc)], p_rs)
    for s in range(1, nk):
        for way in range(2):
            far = [j for j in range(nx) if j % 2 == way] if s == 1 else []
            dense(way, s, way, [(way, s - 1)], far)
        for h in range(2):
            for way in range(2):
                values = [dmat[way, h * 2 + cp] for cp in range(2)]
                if s > 1:
                    for copy in chain_copies(way, s - 1, h):
                        copy.wait_recv()
                    values = [values[cp] + arrived(way, s - 1, h, cp) for cp in range(2)]
                send_half(way, s, h, values)
        if s + 1 < nk:
            send_leaf(s + 1)
            send_own((s + 2) % nk)
    dense(0, 0, 0, [(0, nk - 1), (1, nk - 1)], [])
    ghost_rows = []
    for h in range(2):
        values = [dmat[0, h * 2 + cp] for cp in range(2)]
        for way in range(2):
            for copy in chain_copies(way, nk - 1, h):
                copy.wait_recv()
            values = [values[cp] + arrived(way, nk - 1, h, cp) for cp in range(2)]
        for cp in range(2):
            high = values[cp].astype(jnp.bfloat16)
            low = (values[cp] - high.astype(jnp.float32)).astype(jnp.bfloat16)
            wmat[h * 64:h * 64 + 64, cp * 128:cp * 128 + 128] = high
            wmat[128 + h * 64:192 + h * 64, cp * 128:cp * 128 + 128] = low
        ghost_rows.append(values[1])

    for way, peer in enumerate((upper, lower)):
        chosen = jnp.where(ghost_s[0, 1 - way] == 0, ghost_rows[0], ghost_rows[1])
        high = chosen.astype(jnp.bfloat16)
        nsend[way, 0:64, :] = high
        nsend[way, 64:128, :] = (chosen - high.astype(jnp.float32)).astype(jnp.bfloat16)
        remote(nsend.at[way], nrecv.at[way], n_ss, n_rs, peer).start()

    fetches[6].wait()
    fetches[7].wait()
    diag = diag_v[...]
    inverse = 1.0 / diag
    from_lower = jnp.logical_and(left, dev > 0)
    from_upper = jnp.logical_and(jnp.logical_not(left), dev < ndev - 1)

    def product(vec, columns):
        both = lax.dot_general(
            vec.astype(jnp.bfloat16), wmat[:, columns:columns + 128],
            (((1,), (1,)), ((), ())), preferred_element_type=jnp.float32,
        )
        return both[:, :128] + both[:, 128:]

    def own_part(vec):
        return diag * vec + product(vec, 0)

    def ghost_part(n):
        wait_bytes(grecv.at[pl.ds(2 * n, 2)], g_rs.at[n])
        ghosts = jnp.where(from_lower, grecv[2 * n].astype(jnp.float32), 0.0)
        ghosts = jnp.where(from_upper, grecv[2 * n + 1].astype(jnp.float32), ghosts)
        return product(ghosts, 128)

    def neighbour_part(vec, way):
        both = lax.dot_general(
            vec.astype(jnp.bfloat16), nrecv[way], (((1,), (1,)), ((), ())),
            preferred_element_type=jnp.float32,
        )
        return both + pltpu.roll(both, 64, 1)

    def next_ghosts(mine):
        far = jnp.where(
            jnp.logical_and(left, dev > 1), grecv[6].astype(jnp.float32), 0.0
        )
        below = jnp.where(left, far, mine)
        far = jnp.where(
            jnp.logical_and(jnp.logical_not(left), dev < ndev - 2),
            grecv[7].astype(jnp.float32), 0.0,
        )
        above = jnp.where(left, mine, far)
        summed = jnp.where(left, neighbour_part(below, 0), neighbour_part(above, 1))
        kept = jnp.where(left, wrecv[0, 0:width, :], wrecv[1, 0:width, :])
        scale = jnp.where(
            left[:8], wrecv[0, width:width + 8, :], wrecv[1, width:width + 8, :]
        )[0:1]
        ghosts = kept - scale * summed
        return jnp.where(jnp.logical_or(from_lower, from_upper), ghosts, 0.0)

    lmax = 2.0
    lmin = 0.2
    theta = (lmax + lmin) / 2.0
    delta = (lmax - lmin) / 2.0
    sigma = theta / delta
    rho = 1.0 / sigma
    iterate = start
    residual = (rhs_v[...] - own_part(start)) - ghost_part(0)
    direction = residual * (inverse * (1.0 / theta))
    for step in range(1, STEPS):
        send_ghosts(step, direction)
        if step == STEPS - 1:
            remote(gsend.at[step], grecv.at[6], g_ss, g_rs.at[STEPS], upper2).start()
            remote(gsend.at[step], grecv.at[7], g_ss, g_rs.at[STEPS], lower2).start()
        iterate = iterate + direction
        rest = residual - own_part(direction)
        rho_new = 1.0 / (2.0 * sigma - rho)
        gain = (2.0 * rho_new / delta) * inverse
        kept = (rho_new * rho) * direction + gain * rest
        if step == STEPS - 1:
            wsend[0:width, :] = pack_ghosts(kept)
            wsend[width:width + 8, :] = pack_ghosts(jnp.broadcast_to(gain, (8, 128)))
            for way, peer in enumerate((upper, lower)):
                remote(wsend, wrecv.at[way], w_ss, w_rs, peer).start()
        ghosts = ghost_part(step)
        direction = kept - gain * ghosts
        residual = rest - ghosts
        rho = rho_new
    out_v[...] = iterate + direction
    out_copy = pltpu.make_async_copy(out_v, out_ref.at[0], out_sem)
    out_copy.start()
    rest = residual - own_part(direction)
    wait_bytes(nrecv, n_rs)
    wait_bytes(grecv.at[pl.ds(6, 2)], g_rs.at[STEPS])
    wait_bytes(wrecv, w_rs)
    residual = rest - product(next_ghosts(gsend[STEPS - 1].astype(jnp.float32)), 128)

    squares = jnp.sum((residual * residual).T, axis=0, keepdims=True)
    part = jnp.concatenate([squares, jnp.zeros((1, 128 - width), jnp.float32)], axis=1)
    for buf, ss, rs, here, count, peer in (
        (red_p, red_p_ss, red_p_rs, plane, ng * nx, plane_peer),
        (red_z, red_z_ss, red_z_rs, z, nz, z_peer),
    ):
        buf[here] = part
        for n in range(1, count):
            remote(buf.at[here], buf.at[here], ss, rs, peer(n)).start()
        wait_bytes(buf.at[pl.ds(0, count - 1)], rs)
        part = buf[0]
        for n in range(1, count):
            part = part + buf[n]
    rms_ref[...] = jnp.sqrt(part * (1.0 / (ng * ndev * 128)))[:, :width]

    out_copy.wait()
    wait_bytes(psend.at[pl.ds(oc, far_row + nx - oc)], p_ss)
    wait_bytes(bsend, b_ss)
    wait_bytes(qsend, q_ss)
    wait_bytes(ssend, s_ss)
    wait_bytes(grecv, g_ss)
    wait_bytes(nsend, n_ss)
    wait_bytes(wrecv, w_ss)
    wait_bytes(red_p.at[pl.ds(0, ng * nx - 1)], red_p_ss)
    wait_bytes(red_z.at[pl.ds(0, nz - 1)], red_z_ss)


def shards(ng, nx, nz, tiles, owner, tile_rows, tile_cols, ghost_rows, rhs, start, diag):
    tcount, block = tiles.shape[1], tiles.shape[2]
    width = rhs.shape[1]
    nk = nz // 4
    f32, bf16, i32, i16 = jnp.float32, jnp.bfloat16, jnp.int32, jnp.int16
    vmem, smem, dma = pltpu.VMEM, pltpu.SMEM, pltpu.SemaphoreType.DMA
    whole = pl.BlockSpec(memory_space=pltpu.VMEM)
    smoothed, rms = pl.pallas_call(
        functools.partial(kernel, ng, nx, nz),
        out_shape=(
            jax.ShapeDtypeStruct((1, width, 128), f32),
            jax.ShapeDtypeStruct((1, width), f32),
        ),
        in_specs=[pl.BlockSpec(memory_space=pltpu.HBM)] * 8,
        out_specs=(pl.BlockSpec(memory_space=pltpu.HBM), whole),
        scratch_shapes=[
            smem((1, tcount), i32),
            smem((1, tcount), i32),
            smem((1, tcount), i32),
            smem((1, 2), i32),
            vmem((tcount, block, block), bf16),
            vmem((width, 128), f32),
            vmem((width, 128), f32),
            vmem((1, 128), f32),
            vmem((8, 128), i32),
            smem((8, 128), i32),
            vmem((nx * (4 * nk), 1, 128), i32),
            vmem((nx * (4 * nk), 1, 128), i32),
            vmem((nx + 2 * nk * nx + (nx - 1) * (2 * nk - 1), 64, 128), bf16),
            vmem((nx, 2 * nk - 1, 64, 128), bf16),
            vmem((2, nk, nx, 64, 128), bf16),
            vmem((nx, 64, 128), bf16),
            vmem((2, CH, 64, 128), f32),
            vmem((2, nk - 1, 2, 2, 64, 128), i16),
            vmem((2, nk - 1, 2, 2, 64, 128), i16),
            vmem((2, nk - 1, 2, 2, 128), f32),
            vmem((2, nk - 1, 2, 2, 128), f32),
            vmem((256, 256), bf16),
            vmem((STEPS, width, 128), bf16),
            vmem((2 * STEPS + 2, width, 128), bf16),
            vmem((2, 128, 128), bf16),
            vmem((2, 128, 128), bf16),
            vmem((width + 8, 128), f32),
            vmem((2, width + 8, 128), f32),
            vmem((ng * nx, 1, 128), f32),
            vmem((nz, 1, 128), f32),
            vmem((width, 128), f32),
            dma((8,)),
            dma,
            dma,
            dma,
            dma,
            dma,
            dma((nk,)),
            dma((2, nk)),
            dma((2,)),
            dma,
            dma((2, nk - 1, 2)),
            dma,
            dma((2, nk - 1, 2)),
            dma,
            dma((STEPS + 1,)),
            dma,
            dma,
            dma,
            dma,
            dma,
            dma,
            dma,
            dma,
        ],
        compiler_params=pltpu.CompilerParams(
            collective_id=0, has_side_effects=True, vmem_limit_bytes=60 * 1024 * 1024
        ),
    )(owner.reshape(1, tcount), tile_rows, tile_cols, ghost_rows, tiles, rhs, start, diag)
    return smoothed, rms.reshape(width)


def solution(mesh):
    ng = mesh.shape["grp"]
    nx = mesh.shape["dev"] // NZ
    return jax.shard_map(
        functools.partial(shards, ng, nx, NZ),
        mesh=mesh,
        in_specs=(
            P("grp", "dev", None, None),
            P("grp", "dev", None),
            P("grp", "dev"),
            P("grp", "dev"),
            P("grp", "dev"),
            P("grp", None, "dev"),
            P("grp", None, "dev"),
            P("grp", "dev"),
        ),
        out_specs=(P("grp", None, "dev"), P()),
        check_vma=False,
    )
```

```python
import functools

import jax
import jax.numpy as jnp
from jax import lax
from jax.experimental import pallas as pl
from jax.experimental.pallas import tpu as pltpu
from jax.sharding import PartitionSpec as P

STEPS = 3
THETA = (2.0 + 0.2) / 2.0
DELTA = (2.0 - 0.2) / 2.0
SIGMA = THETA / DELTA
NZ = 16
CH = 4
MESH = pl.DeviceIdType.MESH


def kernel(
    ng, nx, nz,
    owner_h, rows_h, cols_h, ghost_h, tiles_h, rhs_h, start_h, diag_h,
    out_ref, rms_ref,
    owner_s, rows_s, cols_s, ghost_s, tiles_v, rhs_v, start_v, diag_v,
    tab_v, tab_s, psend, precv, bsend, xown, lrecv, frecv, dmat,
    qsend, qrecv, ssend, srecv, wmat, gsend, grecv, nsend, nrecv, wsend, wrecv,
    esend, erecv, pmat, ysend, yrecv, vsend, vrecv, red_c, red_p, red_z, out_v, in_sem, tab_sem, out_sem, p_ss, p_rs, b_ss, o_rs, l_rs, f_rs,
    q_ss, q_rs, s_ss, s_rs, g_ss, g_rs, n_ss, n_rs, w_ss, w_rs,
    e_ss, e_rs, y_ss, y_rs, v_ss, v_rs, red_c_ss, red_c_rs, red_p_ss, red_p_rs, red_z_ss, red_z_rs,
):
    half = nz // 2
    nk = half // 2
    ndev = nx * nz
    tcount = tiles_v.shape[0]
    width = rhs_v.shape[0]
    dev = lax.axis_index("dev")
    grp = lax.axis_index("grp")
    x = lax.div(dev, nz)
    z = lax.rem(dev, nz)

    def at(j, k):
        return {"dev": lax.rem(x + j, nx) * nz + lax.rem(z + k + nz, nz)}

    cores = 2 if ng % 2 == 0 else 1
    core = lax.rem(grp, cores)
    chips = ng // cores * nx
    plane = lax.div(grp, cores) * nx + x

    def core_peer(n):
        return {"grp": grp + 1 - 2 * core}

    def plane_peer(n):
        there = lax.rem(plane + n, chips)
        return {"grp": lax.div(there, nx) * cores + core, "dev": lax.rem(there, nx) * nz + z}

    def z_peer(n):
        return at(0, n)

    upper = {"dev": lax.rem(dev + 1, ndev)}
    lower = {"dev": lax.rem(dev + ndev - 1, ndev)}
    upper2 = {"dev": lax.rem(dev + 2, ndev)}
    lower2 = {"dev": lax.rem(dev + ndev - 2, ndev)}

    fetches = [
        pltpu.make_async_copy(src, dst, in_sem.at[n])
        for n, (src, dst) in enumerate((
            (owner_h, owner_s), (rows_h, rows_s), (cols_h, cols_s), (ghost_h, ghost_s),
            (tiles_h.at[0], tiles_v), (start_h.at[0], start_v), (rhs_h.at[0], rhs_v),
            (diag_h, diag_v),
        ))
    ]
    for fetch in fetches:
        fetch.start()

    barrier = pltpu.get_barrier_semaphore()
    peers = [at(j, k) for j in range(nx) for k in (-1, 1)]
    peers += [at(j, 0) for j in range(1, nx)] + [at(0, -2), at(0, 2)]
    peers += [at(nx - j, 4 * (j % 2) - 2) for j in range(1, nx)]
    peers += [upper, lower, upper2, lower2] + [core_peer(n) for n in range(1, cores)]
    peers += [plane_peer(n) for n in range(1, chips)]
    for peer in peers:
        pl.semaphore_signal(barrier, inc=1, device_id=peer, device_id_type=MESH)

    lane = lax.broadcasted_iota(jnp.int32, (1, 128), 1)
    none = jnp.full((1, 128), -1, jnp.int32)
    for fetch in fetches[:4]:
        fetch.wait()

    def find(t, held):
        i0, i1, p0, p1 = held
        hit = lane == owner_s[0, t]
        place = rows_s[0, t] * 4 + cols_s[0, t]
        first = jnp.logical_and(hit, i0 < 0)
        second = jnp.logical_and(hit, i0 >= 0)
        return (
            jnp.where(first, t, i0), jnp.where(second, t, i1),
            jnp.where(first, place, p0), jnp.where(second, place, p1),
        )

    i0, i1, p0, p1 = lax.fori_loop(0, tcount, find, (none,) * 4, unroll=True)
    tab_v[0:1, :] = jnp.maximum(i0, 0)
    tab_v[1:2, :] = jnp.maximum(i1, 0)
    tab_v[2:3, :] = p0
    tab_v[3:4, :] = p1
    tab_copy = pltpu.make_async_copy(tab_v, tab_s, tab_sem)
    tab_copy.start()

    wide = lax.broadcasted_iota(jnp.int32, (width, 128), 1)
    left = wide < 64
    stay = jnp.where(left, ghost_s[0, 1], 1 - ghost_s[0, 0]) == 0

    def pack_ghosts(vec):
        return jnp.where(stay[:vec.shape[0]], vec, pltpu.roll(vec, 64, 1))

    def remote(src, dst, ss, rs, peer):
        return pltpu.make_async_remote_copy(
            src_ref=src, dst_ref=dst, send_sem=ss, recv_sem=rs,
            device_id=peer, device_id_type=MESH,
        )

    def wait_bytes(ref, sem):
        pltpu.make_async_copy(ref, ref, sem).wait()

    def send_ghosts(n, vec):
        gsend[n] = pack_ghosts(vec).astype(jnp.bfloat16)
        for way, peer in enumerate((upper, lower)):
            remote(gsend.at[n], grecv.at[2 * n + way], g_ss, g_rs.at[n], peer).start()

    def owner_of(j, step):
        return lax.rem(x + j, nx) * nz + lax.rem(z + step + nz, nz)

    def own_step(fam, k):
        if k == 0:
            return 0
        return half - 2 * k if fam == 0 else 2 * k - half

    def leaf_step(way, k):
        return half - 1 - 2 * k if way == 0 else 2 * k + 1 - half

    def pair(o):
        return jnp.concatenate([tiles_v[tab_s[0, o]], tiles_v[tab_s[1, o]]], axis=1)

    def place(o):
        return jnp.where(lane < 64, tab_s[2, o], tab_s[3, o])

    oc = 2 * nk - 1
    leaf_row, far_row = nx * oc, nx * oc + 2 * nx * nk
    leaf_slot, own_slot = nx, nx + 2 * nk * nx

    def own_index(k, fam):
        return oc - 1 if k == 0 else 2 * (k - 1) + fam

    order = list(range(1, nx)) + [0]

    def send_places():
        for j in order:
            spans = [
                (leaf_row + (way * nx + j) * nk, nk, at(j, 1 - 2 * way)) for way in range(2)
            ]
            spans.append((far_row + j, 1, at(j, 2 - 4 * (j % 2))))
            if j:
                spans.append((j * oc, oc, at(j, 0)))
            for first, count, peer in spans:
                rows = pl.ds(first, count)
                remote(psend.at[rows], precv.at[rows], p_ss, p_rs, peer).start()

    def send_far():
        for j in order:
            remote(
                bsend.at[j], frecv.at[j], b_ss, f_rs.at[j % 2], at(j, 2 - 4 * (j % 2))
            ).start()

    def send_leaf(k):
        for j in order:
            for way in range(2):
                slot = leaf_slot + (way * nk + k) * nx + j
                remote(
                    bsend.at[slot], lrecv.at[way, k, j], b_ss, l_rs.at[way, k],
                    at(j, 1 - 2 * way),
                ).start()

    def send_own(k):
        count = 1 if k == 0 else 2
        for j in range(1, nx):
            slot = own_slot + (j - 1) * oc + own_index(k, 0)
            remote(
                bsend.at[pl.ds(slot, count)], xown.at[j, pl.ds(own_index(k, 0), count)],
                b_ss, o_rs.at[k], at(j, 0),
            ).start()

    tab_copy.wait()
    fetches[4].wait()
    fetches[5].wait()
    start = start_v[...]
    for j in range(nx):
        o = owner_of(j, half)
        psend[far_row + j] = place(o)
        bsend[j] = pair(o)
        for k in range(nk):
            for way in range(2):
                o = owner_of(j, leaf_step(way, k))
                psend[leaf_row + (way * nx + j) * nk + k] = place(o)
                bsend[leaf_slot + (way * nk + k) * nx + j] = pair(o)
            for fam in range(1 if k == 0 else 2):
                o = owner_of(j, own_step(fam, k))
                n = own_index(k, fam)
                if j:
                    psend[j * oc + n] = place(o)
                    bsend[own_slot + (j - 1) * oc + n] = pair(o)
                else:
                    precv[n] = place(o)
                    xown[0, n] = pair(o)

    pl.semaphore_wait(barrier, len(peers))
    send_far()
    send_leaf(0)
    send_own(1)
    send_places()
    send_leaf(1)
    send_own(2 % nk)
    send_ghosts(0, start)

    right_half = (lane >= 64).astype(jnp.int32)

    def add_pair(acc, both, row):
        both = both.astype(jnp.float32)
        swapped = pltpu.roll(both, 64, 1)
        row_swapped = pltpu.roll(row, 64, 1)
        out = []
        for c in range(CH):
            target = (c // 2) * 4 + (c % 2) * 2 + right_half
            value = acc[c] + jnp.where(row == target, both, 0.0)
            out.append(value + jnp.where(row_swapped == target, swapped, 0.0))
        return tuple(out)

    def dense(n, k, fam, leaves, far):
        acc = tuple(jnp.zeros((64, 128), jnp.float32) for _ in range(CH))
        if far:
            wait_bytes(frecv.at[pl.ds(0, len(far))], f_rs.at[fam])
        for j in far:
            acc = add_pair(acc, frecv[j], precv[far_row + j])
        for way, kk in leaves:
            wait_bytes(lrecv.at[way, kk], l_rs.at[way, kk])
            for j in range(nx):
                row = leaf_row + (way * nx + j) * nk + kk
                acc = add_pair(acc, lrecv[way, kk, j], precv[row])
        if fam == 0:
            count = 1 if k == 0 else 2
            wait_bytes(
                xown.at[pl.ds(1, nx - 1), pl.ds(own_index(k, 0), count)], o_rs.at[k]
            )
        for j in range(nx):
            i = own_index(k, fam)
            acc = add_pair(acc, xown[j, i], precv[j * oc + i])
        for c in range(CH):
            dmat[n, c] = acc[c]

    def chain_copies(way, s, h):
        peer = z_peer(2 if way == 0 else -2)
        n = s - 1
        return (
            remote(ssend.at[way, n, h], srecv.at[way, n, h], s_ss, s_rs.at[way, n, h], peer),
            remote(qsend.at[way, n, h], qrecv.at[way, n, h], q_ss, q_rs.at[way, n, h], peer),
        )

    def send_half(way, s, h, values):
        for cp in range(2):
            most = jnp.maximum(jnp.max(jnp.abs(values[cp]), axis=0, keepdims=True), 1e-30)
            scaled = jnp.round(values[cp] * (32767.0 / most))
            qsend[way, s - 1, h, cp] = scaled.astype(jnp.int32).astype(jnp.int16)
            ssend[way, s - 1, h, cp:cp + 1, :] = most * (1.0 / 32767.0)
        for copy in chain_copies(way, s, h):
            copy.start()

    def arrived(way, s, h, cp):
        whole = qrecv[way, s - 1, h, cp].astype(jnp.int32).astype(jnp.float32)
        return whole * srecv[way, s - 1, h, cp:cp + 1, :]

    wait_bytes(precv.at[pl.ds(oc, far_row + nx - oc)], p_rs)
    def split(matrix, h, cp, value):
        high = value.astype(jnp.bfloat16)
        low = (value - high.astype(jnp.float32)).astype(jnp.bfloat16)
        matrix[h * 64:h * 64 + 64, cp * 128:cp * 128 + 128] = high
        matrix[128 + h * 64:192 + h * 64, cp * 128:cp * 128 + 128] = low

    def times(vec, matrix):
        both = lax.dot_general(
            vec, matrix, (((1,), (1,)), ((), ())), preferred_element_type=jnp.float32
        )
        return both[:, :128] + both[:, 128:]

    from_lower = jnp.logical_and(left, dev > 0)
    from_upper = jnp.logical_and(jnp.logical_not(left), dev < ndev - 1)

    def ghosts_of(n):
        wait_bytes(grecv.at[pl.ds(2 * n, 2)], g_rs.at[n])
        ghosts = jnp.where(from_lower, grecv[2 * n].astype(jnp.float32), 0.0)
        return jnp.where(from_upper, grecv[2 * n + 1].astype(jnp.float32), ghosts)

    for s in range(1, nk):
        for way in range(2):
            far = [j for j in range(nx) if j % 2 == way] if s == 1 else []
            dense(way, s, way, [(way, s - 1)], far)
        for h in range(2):
            for way in range(2):
                values = [dmat[way, h * 2 + cp] for cp in range(2)]
                if s > 1:
                    for copy in chain_copies(way, s - 1, h):
                        copy.wait_recv()
                    values = [values[cp] + arrived(way, s - 1, h, cp) for cp in range(2)]
                send_half(way, s, h, values)
                if s == nk - 1:
                    for cp in range(2):
                        split(pmat.at[way], h, cp, values[cp])
        if s == 1:
            ghosts = ghosts_of(0)
            esend[0:width, 0:128] = start.astype(jnp.bfloat16)
            esend[0:width, 128:256] = ghosts.astype(jnp.bfloat16)
            turned = jnp.broadcast_to(stay[0:1].astype(jnp.float32), (16, 128))
            esend[width:width + 16, 0:128] = turned.astype(jnp.bfloat16)
            esend[width:width + 16, 128:256] = turned.astype(jnp.bfloat16)
            for way in range(2):
                remote(esend, erecv.at[way], e_ss, e_rs, z_peer(2 * (2 * way - 1))).start()
        if s + 1 < nk:
            send_leaf(s + 1)
            send_own((s + 2) % nk)
    wait_bytes(erecv, e_rs)
    for way in range(2):
        part = times(erecv[way, 0:width, :], pmat[way])
        turned = erecv[way, width:width + 16, 0:128].astype(jnp.float32)[0:1]
        ysend[way] = jnp.where(turned > 0.5, part, pltpu.roll(part, 64, 1))
        first = lax.rem(z + 2 - 4 * way + nz, nz) + x * nz
        for side in range(2):
            remote(
                ysend.at[way], yrecv.at[side, way], y_ss, y_rs,
                {"dev": lax.rem(first + 1 - 2 * side + ndev, ndev)},
            ).start()

    dense(0, 0, 0, [(0, nk - 1), (1, nk - 1)], [])
    fetches[6].wait()
    fetches[7].wait()
    diag = diag_v[...]
    inverse = 1.0 / diag
    for c in range(CH):
        split(wmat, c // 2, c % 2, dmat[0, c])
    base = rhs_v[...] - diag * start
    vsend[0:width, :] = pack_ghosts(base - times(esend[0:width, :], wmat[...]))
    vsend[width:width + 8, :] = pack_ghosts(jnp.broadcast_to(inverse * (1.0 / THETA), (8, 128)))
    for way, peer in enumerate((upper, lower)):
        remote(vsend, vrecv.at[way], v_ss, v_rs, peer).start()

    ghost_rows = []
    for h in range(2):
        values = [dmat[0, h * 2 + cp] for cp in range(2)]
        for way in range(2):
            for copy in chain_copies(way, nk - 1, h):
                copy.wait_recv()
            values = [values[cp] + arrived(way, nk - 1, h, cp) for cp in range(2)]
        for cp in range(2):
            split(wmat, h, cp, values[cp])
        ghost_rows.append(values[1])

    for way, peer in enumerate((upper, lower)):
        chosen = jnp.where(ghost_s[0, 1 - way] == 0, ghost_rows[0], ghost_rows[1])
        high = chosen.astype(jnp.bfloat16)
        nsend[way, 0:64, :] = high
        nsend[way, 64:128, :] = (chosen - high.astype(jnp.float32)).astype(jnp.bfloat16)
        remote(nsend.at[way], nrecv.at[way], n_ss, n_rs, peer).start()

    def product(vec, columns):
        return times(vec.astype(jnp.bfloat16), wmat[:, columns:columns + 128])

    def own_part(vec):
        return diag * vec + product(vec, 0)

    def mixed(ref):
        return jnp.where(left, ref[0, 0:width, :], ref[1, 0:width, :])

    def mixed_scale(ref):
        return jnp.where(left[:8], ref[0, width:width + 8, :], ref[1, width:width + 8, :])[0:1]

    def inside(ghosts):
        return jnp.where(jnp.logical_or(from_lower, from_upper), ghosts, 0.0)

    def first_ghosts():
        wait_bytes(vrecv, v_rs)
        wait_bytes(yrecv, y_rs)
        parts = jnp.where(left, yrecv[0, 0] + yrecv[0, 1], yrecv[1, 0] + yrecv[1, 1])
        return inside(mixed_scale(vrecv) * (mixed(vrecv) - parts))

    def neighbour_part(vec, way):
        both = lax.dot_general(
            vec.astype(jnp.bfloat16), nrecv[way], (((1,), (1,)), ((), ())),
            preferred_element_type=jnp.float32,
        )
        return both + pltpu.roll(both, 64, 1)

    def next_ghosts(mine):
        far = jnp.where(jnp.logical_and(left, dev > 1), grecv[4].astype(jnp.float32), 0.0)
        below = jnp.where(left, far, mine)
        far = jnp.where(
            jnp.logical_and(jnp.logical_not(left), dev < ndev - 2),
            grecv[5].astype(jnp.float32), 0.0,
        )
        above = jnp.where(left, mine, far)
        summed = jnp.where(left, neighbour_part(below, 0), neighbour_part(above, 1))
        return inside(mixed(wrecv) - mixed_scale(wrecv) * summed)

    rho = 1.0 / SIGMA
    iterate = start
    residual = base - times(esend[0:width, :], wmat[...])
    direction = residual * (inverse * (1.0 / THETA))
    for step in range(1, STEPS):
        last = step == STEPS - 1
        if last:
            send_ghosts(1, direction)
            remote(gsend.at[1], grecv.at[4], g_ss, g_rs.at[2], upper2).start()
            remote(gsend.at[1], grecv.at[5], g_ss, g_rs.at[2], lower2).start()
        iterate = iterate + direction
        rest = residual - own_part(direction)
        rho_new = 1.0 / (2.0 * SIGMA - rho)
        gain = (2.0 * rho_new / DELTA) * inverse
        kept = (rho_new * rho) * direction + gain * rest
        if last:
            wsend[0:width, :] = pack_ghosts(kept)
            wsend[width:width + 8, :] = pack_ghosts(jnp.broadcast_to(gain, (8, 128)))
            for way, peer in enumerate((upper, lower)):
                remote(wsend, wrecv.at[way], w_ss, w_rs, peer).start()
        ghosts = product(ghosts_of(1) if last else first_ghosts(), 128)
        direction = kept - gain * ghosts
        residual = rest - ghosts
        rho = rho_new
    out_v[...] = iterate + direction
    out_copy = pltpu.make_async_copy(out_v, out_ref.at[0], out_sem)
    out_copy.start()
    rest = residual - own_part(direction)
    wait_bytes(nrecv, n_rs)
    wait_bytes(grecv.at[pl.ds(4, 2)], g_rs.at[2])
    wait_bytes(wrecv, w_rs)
    residual = rest - product(next_ghosts(gsend[1].astype(jnp.float32)), 128)

    squares = jnp.sum((residual * residual).T, axis=0, keepdims=True)
    part = jnp.concatenate([squares, jnp.zeros((1, 128 - width), jnp.float32)], axis=1)
    for buf, ss, rs, here, count, peer in (
        (red_c, red_c_ss, red_c_rs, core, cores, core_peer),
        (red_p, red_p_ss, red_p_rs, plane, chips, plane_peer),
        (red_z, red_z_ss, red_z_rs, z, nz, z_peer),
    ):
        if count == 1:
            continue
        buf[here] = part
        for n in range(1, count):
            remote(buf.at[here], buf.at[here], ss, rs, peer(n)).start()
        wait_bytes(buf.at[pl.ds(0, count - 1)], rs)
        part = buf[0]
        for n in range(1, count):
            part = part + buf[n]
    rms_ref[...] = jnp.sqrt(part * (1.0 / (ng * ndev * 128)))[:, :width]

    out_copy.wait()
    wait_bytes(psend.at[pl.ds(oc, far_row + nx - oc)], p_ss)
    wait_bytes(bsend, b_ss)
    wait_bytes(qsend, q_ss)
    wait_bytes(ssend, s_ss)
    wait_bytes(grecv, g_ss)
    wait_bytes(nsend, n_ss)
    wait_bytes(wrecv, w_ss)
    wait_bytes(erecv, e_ss)
    wait_bytes(yrecv, y_ss)
    wait_bytes(vrecv, v_ss)
    if cores > 1:
        wait_bytes(red_c.at[pl.ds(0, 1)], red_c_ss)
    wait_bytes(red_p.at[pl.ds(0, chips - 1)], red_p_ss)
    wait_bytes(red_z.at[pl.ds(0, nz - 1)], red_z_ss)


def shards(ng, nx, nz, tiles, owner, tile_rows, tile_cols, ghost_rows, rhs, start, diag):
    tcount, block = tiles.shape[1], tiles.shape[2]
    width = rhs.shape[1]
    nk = nz // 4
    f32, bf16, i32, i16 = jnp.float32, jnp.bfloat16, jnp.int32, jnp.int16
    vmem, smem, dma = pltpu.VMEM, pltpu.SMEM, pltpu.SemaphoreType.DMA
    whole = pl.BlockSpec(memory_space=pltpu.VMEM)
    smoothed, rms = pl.pallas_call(
        functools.partial(kernel, ng, nx, nz),
        out_shape=(
            jax.ShapeDtypeStruct((1, width, 128), f32),
            jax.ShapeDtypeStruct((1, width), f32),
        ),
        in_specs=[pl.BlockSpec(memory_space=pltpu.HBM)] * 8,
        out_specs=(pl.BlockSpec(memory_space=pltpu.HBM), whole),
        scratch_shapes=[
            smem((1, tcount), i32),
            smem((1, tcount), i32),
            smem((1, tcount), i32),
            smem((1, 2), i32),
            vmem((tcount, block, block), bf16),
            vmem((width, 128), f32),
            vmem((width, 128), f32),
            vmem((1, 128), f32),
            vmem((8, 128), i32),
            smem((8, 128), i32),
            vmem((nx * (4 * nk), 1, 128), i32),
            vmem((nx * (4 * nk), 1, 128), i32),
            vmem((nx + 2 * nk * nx + (nx - 1) * (2 * nk - 1), 64, 128), bf16),
            vmem((nx, 2 * nk - 1, 64, 128), bf16),
            vmem((2, nk, nx, 64, 128), bf16),
            vmem((nx, 64, 128), bf16),
            vmem((2, CH, 64, 128), f32),
            vmem((2, nk - 1, 2, 2, 64, 128), i16),
            vmem((2, nk - 1, 2, 2, 64, 128), i16),
            vmem((2, nk - 1, 2, 2, 128), f32),
            vmem((2, nk - 1, 2, 2, 128), f32),
            vmem((256, 256), bf16),
            vmem((2, width, 128), bf16),
            vmem((6, width, 128), bf16),
            vmem((2, 128, 128), bf16),
            vmem((2, 128, 128), bf16),
            vmem((width + 8, 128), f32),
            vmem((2, width + 8, 128), f32),
            vmem((width + 16, 256), bf16),
            vmem((2, width + 16, 256), bf16),
            vmem((2, 256, 256), bf16),
            vmem((2, width, 128), f32),
            vmem((2, 2, width, 128), f32),
            vmem((width + 8, 128), f32),
            vmem((2, width + 8, 128), f32),
            vmem((2, 1, 128), f32),
            vmem((ng * nx, 1, 128), f32),
            vmem((nz, 1, 128), f32),
            vmem((width, 128), f32),
            dma((8,)),
            dma,
            dma,
            dma,
            dma,
            dma,
            dma((nk,)),
            dma((2, nk)),
            dma((2,)),
            dma,
            dma((2, nk - 1, 2)),
            dma,
            dma((2, nk - 1, 2)),
            dma,
            dma((3,)),
            dma,
            dma,
            dma,
            dma,
            dma,
            dma,
            dma,
            dma,
            dma,
            dma,
            dma,
            dma,
            dma,
            dma,
            dma,
            dma,
        ],
        compiler_params=pltpu.CompilerParams(
            collective_id=0, has_side_effects=True, vmem_limit_bytes=60 * 1024 * 1024
        ),
    )(owner.reshape(1, tcount), tile_rows, tile_cols, ghost_rows, tiles, rhs, start, diag)
    return smoothed, rms.reshape(width)


def solution(mesh):
    ng = mesh.shape["grp"]
    nx = mesh.shape["dev"] // NZ
    return jax.shard_map(
        functools.partial(shards, ng, nx, NZ),
        mesh=mesh,
        in_specs=(
            P("grp", "dev", None, None),
            P("grp", "dev", None),
            P("grp", "dev"),
            P("grp", "dev"),
            P("grp", "dev"),
            P("grp", None, "dev"),
            P("grp", None, "dev"),
            P("grp", "dev"),
        ),
        out_specs=(P("grp", None, "dev"), P()),
        check_vma=False,
    )
```

```python
import functools

import jax
import jax.numpy as jnp
from jax import lax
from jax.experimental import pallas as pl
from jax.experimental.pallas import tpu as pltpu
from jax.sharding import PartitionSpec as P

STEPS = 3
THETA = (2.0 + 0.2) / 2.0
DELTA = (2.0 - 0.2) / 2.0
SIGMA = THETA / DELTA
NZ = 16
CH = 4
MESH = pl.DeviceIdType.MESH


def kernel(
    ng, nx, nz,
    owner_h, rows_h, cols_h, ghost_h, tiles_h, rhs_h, start_h, diag_h,
    out_ref, rms_ref,
    owner_s, rows_s, cols_s, ghost_s, tiles_v, rhs_v, start_v, diag_v,
    tab_v, tab_s, psend, precv, bsend, xown, lrecv, frecv, dmat,
    qsend, qrecv, ssend, srecv, wmat, gsend, grecv, nsend, nrecv, wsend, wrecv,
    esend, erecv, pmat, ysend, yrecv, vsend, vrecv, red_c, red_p, red_z, out_v, in_sem, tab_sem, out_sem, p_ss, p_rs, b_ss, o_rs, l_rs, f_rs,
    q_ss, q_rs, s_ss, s_rs, g_ss, g_rs, n_ss, n_rs, w_ss, w_rs,
    e_ss, e_rs, y_ss, y_rs, v_ss, v_rs, red_c_ss, red_c_rs, red_p_ss, red_p_rs, red_z_ss, red_z_rs,
):
    half = nz // 2
    nk = half // 2
    ndev = nx * nz
    tcount = tiles_v.shape[0]
    width = rhs_v.shape[0]
    dev = lax.axis_index("dev")
    grp = lax.axis_index("grp")
    x = lax.div(dev, nz)
    z = lax.rem(dev, nz)

    def at(j, k):
        return {"dev": lax.rem(x + j, nx) * nz + lax.rem(z + k + nz, nz)}

    cores = 2 if ng % 2 == 0 else 1
    core = lax.rem(grp, cores)
    chips = ng // cores * nx
    plane = lax.div(grp, cores) * nx + x

    def core_peer(n):
        return {"grp": grp + 1 - 2 * core}

    def plane_peer(n):
        there = lax.rem(plane + n, chips)
        return {"grp": lax.div(there, nx) * cores + core, "dev": lax.rem(there, nx) * nz + z}

    def z_peer(n):
        return at(0, n)

    upper = {"dev": lax.rem(dev + 1, ndev)}
    lower = {"dev": lax.rem(dev + ndev - 1, ndev)}
    upper2 = {"dev": lax.rem(dev + 2, ndev)}
    lower2 = {"dev": lax.rem(dev + ndev - 2, ndev)}

    barrier = pltpu.get_barrier_semaphore()
    def ring_hops(n, count):
        return min(n % count, count - n % count)

    peers = [(ring_hops(j, nx) + 1, at(j, k)) for j in range(nx) for k in (-1, 1)]
    peers += [(ring_hops(j, nx), at(j, 0)) for j in range(1, nx)]
    peers += [(2, at(0, -2)), (2, at(0, 2))]
    peers += [(ring_hops(j, nx) + 2, at(nx - j, 4 * (j % 2) - 2)) for j in range(1, nx)]
    peers += [(2, upper), (2, lower), (3, upper2), (3, lower2)]
    peers += [(0, core_peer(n)) for n in range(1, cores)]
    peers += [
        (ring_hops(n, nx) + ring_hops(n // nx, chips // nx), plane_peer(n))
        for n in range(1, chips)
    ]
    peers = [peer for _, peer in sorted(peers, key=lambda entry: -entry[0])]

    def greet(some):
        for peer in some:
            pl.semaphore_signal(barrier, inc=1, device_id=peer, device_id_type=MESH)

    greet(peers[:10])
    fetches = [
        pltpu.make_async_copy(src, dst, in_sem.at[n])
        for n, (src, dst) in enumerate((
            (owner_h, owner_s), (rows_h, rows_s), (cols_h, cols_s), (ghost_h, ghost_s),
            (tiles_h.at[0], tiles_v), (start_h.at[0], start_v), (rhs_h.at[0], rhs_v),
            (diag_h, diag_v),
        ))
    ]
    for fetch in fetches:
        fetch.start()

    greet(peers[10:])

    lane = lax.broadcasted_iota(jnp.int32, (1, 128), 1)
    none = jnp.full((1, 128), -1, jnp.int32)
    for fetch in fetches[:4]:
        fetch.wait()

    def find(t, held):
        i0, i1, p0, p1 = held
        hit = lane == owner_s[0, t]
        place = rows_s[0, t] * 4 + cols_s[0, t]
        first = jnp.logical_and(hit, i0 < 0)
        second = jnp.logical_and(hit, i0 >= 0)
        return (
            jnp.where(first, t, i0), jnp.where(second, t, i1),
            jnp.where(first, place, p0), jnp.where(second, place, p1),
        )

    i0, i1, p0, p1 = lax.fori_loop(0, tcount, find, (none,) * 4, unroll=True)
    tab_v[0:1, :] = jnp.maximum(i0, 0)
    tab_v[1:2, :] = jnp.maximum(i1, 0)
    tab_v[2:3, :] = p0
    tab_v[3:4, :] = p1
    tab_copy = pltpu.make_async_copy(tab_v, tab_s, tab_sem)
    tab_copy.start()

    wide = lax.broadcasted_iota(jnp.int32, (width, 128), 1)
    left = wide < 64
    stay = jnp.where(left, ghost_s[0, 1], 1 - ghost_s[0, 0]) == 0

    def pack_ghosts(vec):
        return jnp.where(stay[:vec.shape[0]], vec, pltpu.roll(vec, 64, 1))

    def remote(src, dst, ss, rs, peer):
        return pltpu.make_async_remote_copy(
            src_ref=src, dst_ref=dst, send_sem=ss, recv_sem=rs,
            device_id=peer, device_id_type=MESH,
        )

    def wait_bytes(ref, sem):
        pltpu.make_async_copy(ref, ref, sem).wait()

    def send_ghosts(n, vec):
        gsend[n] = pack_ghosts(vec).astype(jnp.bfloat16)
        for way, peer in enumerate((upper, lower)):
            remote(gsend.at[n], grecv.at[2 * n + way], g_ss, g_rs.at[n], peer).start()

    def owner_of(j, step):
        return lax.rem(x + j, nx) * nz + lax.rem(z + step + nz, nz)

    def own_step(fam, k):
        if k == 0:
            return 0
        return half - 2 * k if fam == 0 else 2 * k - half

    def leaf_step(way, k):
        return half - 1 - 2 * k if way == 0 else 2 * k + 1 - half

    def pair(o):
        return jnp.concatenate([tiles_v[tab_s[0, o]], tiles_v[tab_s[1, o]]], axis=1)

    def place(o):
        return jnp.where(lane < 64, tab_s[2, o], tab_s[3, o])

    oc = 2 * nk - 1
    leaf_row, far_row = nx * oc, nx * oc + 2 * nx * nk
    leaf_slot, own_slot = nx, nx + 2 * nk * nx

    def own_index(k, fam):
        return oc - 1 if k == 0 else 2 * (k - 1) + fam

    def over_x(body, count=nx):
        def turn(i, _):
            body(lax.rem(i + 1, nx))
            return 0

        lax.fori_loop(0, count, turn, 0)

    def far_hops(j):
        return 2 - 4 * lax.rem(j, 2)

    def own_slots(j):
        return own_slot + lax.rem(j + nx - 1, nx) * oc

    def send_rows(first, count, peer):
        rows = pl.ds(first, count)
        remote(psend.at[rows], precv.at[rows], p_ss, p_rs, peer).start()

    def send_places():
        def body(j):
            for way in range(2):
                send_rows(leaf_row + (way * nx + j) * nk, nk, at(j, 1 - 2 * way))
            send_rows(far_row + j, 1, at(j, far_hops(j)))

        over_x(body)
        over_x(lambda j: send_rows(j * oc, oc, at(j, 0)), nx - 1)

    def send_far():
        def body(j):
            remote(
                bsend.at[j], frecv.at[j], b_ss, f_rs.at[lax.rem(j, 2)], at(j, far_hops(j))
            ).start()

        over_x(body)

    def send_leaf(k):
        def body(j):
            for way in range(2):
                slot = leaf_slot + (way * nk + k) * nx + j
                remote(
                    bsend.at[slot], lrecv.at[way, k, j], b_ss, l_rs.at[way, k],
                    at(j, 1 - 2 * way),
                ).start()

        over_x(body)

    def send_own(k):
        def body(j):
            count = 1 if k == 0 else 2
            remote(
                bsend.at[pl.ds(own_slots(j) + own_index(k, 0), count)],
                xown.at[j, pl.ds(own_index(k, 0), count)], b_ss, o_rs.at[k], at(j, 0),
            ).start()

        over_x(body, nx - 1)

    tab_copy.wait()
    fetches[4].wait()
    fetches[5].wait()
    start = start_v[...]
    def pack(j):
        o = owner_of(j, half)
        psend[far_row + j] = place(o)
        bsend[j] = pair(o)
        for k in range(nk):
            for way in range(2):
                o = owner_of(j, leaf_step(way, k))
                psend[leaf_row + (way * nx + j) * nk + k] = place(o)
                bsend[leaf_slot + (way * nk + k) * nx + j] = pair(o)
            for fam in range(1 if k == 0 else 2):
                o = owner_of(j, own_step(fam, k))
                psend[j * oc + own_index(k, fam)] = place(o)
                bsend[own_slots(j) + own_index(k, fam)] = pair(o)

    over_x(pack)
    precv[0:oc] = psend[0:oc]
    xown[0] = bsend[own_slot + (nx - 1) * oc:own_slot + nx * oc]

    pl.semaphore_wait(barrier, len(peers))
    send_far()
    send_leaf(0)
    send_own(1)
    send_places()
    send_leaf(1)
    send_own(2 % nk)
    send_ghosts(0, start)

    right_half = (lane >= 64).astype(jnp.int32)

    def add_pair(acc, both, row):
        both = both.astype(jnp.float32)
        swapped = pltpu.roll(both, 64, 1)
        row_swapped = pltpu.roll(row, 64, 1)
        out = []
        for c in range(CH):
            target = (c // 2) * 4 + (c % 2) * 2 + right_half
            value = acc[c] + jnp.where(row == target, both, 0.0)
            out.append(value + jnp.where(row_swapped == target, swapped, 0.0))
        return tuple(out)

    def own_arrived(k):
        count = 1 if k == 0 else 2
        wait_bytes(xown.at[pl.ds(1, nx - 1), pl.ds(own_index(k, 0), count)], o_rs.at[k])

    def dense(n, k, fam, leaves, far):
        acc = tuple(jnp.zeros((64, 128), jnp.float32) for _ in range(CH))
        if far:
            wait_bytes(frecv.at[pl.ds(0, nx // 2)], f_rs.at[fam])
            for i in range(nx // 2):
                acc = add_pair(acc, frecv[2 * i + fam], precv[far_row + 2 * i + fam])
        for way, kk in leaves:
            wait_bytes(lrecv.at[way, kk], l_rs.at[way, kk])
            for j in range(nx):
                row = leaf_row + (way * nx + j) * nk + kk
                acc = add_pair(acc, lrecv[way, kk, j], precv[row])
        for j in range(nx):
            i = own_index(k, fam)
            acc = add_pair(acc, xown[j, i], precv[j * oc + i])
        for c in range(CH):
            dmat[n, c] = acc[c]

    def both_ways(body):
        def turn(way, _):
            body(way)
            return 0

        lax.fori_loop(0, 2, turn, 0)

    def chain_copies(way, s, h):
        peer = z_peer(2 - 4 * way)
        n = s - 1
        return (
            remote(ssend.at[way, n, h], srecv.at[way, n, h], s_ss, s_rs.at[way, n, h], peer),
            remote(qsend.at[way, n, h], qrecv.at[way, n, h], q_ss, q_rs.at[way, n, h], peer),
        )

    def send_half(way, s, h, values):
        for cp in range(2):
            most = jnp.maximum(jnp.max(jnp.abs(values[cp]), axis=0, keepdims=True), 1e-30)
            scaled = jnp.round(values[cp] * (32767.0 / most))
            qsend[way, s - 1, h, cp] = scaled.astype(jnp.int32).astype(jnp.int16)
            ssend[way, s - 1, h, cp:cp + 1, :] = most * (1.0 / 32767.0)
        for copy in chain_copies(way, s, h):
            copy.start()

    def arrived(way, s, h, cp):
        whole = qrecv[way, s - 1, h, cp].astype(jnp.int32).astype(jnp.float32)
        return whole * srecv[way, s - 1, h, cp:cp + 1, :]

    wait_bytes(precv.at[pl.ds(oc, far_row + nx - oc)], p_rs)
    def split(matrix, h, cp, value):
        high = value.astype(jnp.bfloat16)
        low = (value - high.astype(jnp.float32)).astype(jnp.bfloat16)
        matrix[h * 64:h * 64 + 64, cp * 128:cp * 128 + 128] = high
        matrix[128 + h * 64:192 + h * 64, cp * 128:cp * 128 + 128] = low

    def times(vec, matrix):
        both = lax.dot_general(
            vec, matrix, (((1,), (1,)), ((), ())), preferred_element_type=jnp.float32
        )
        return both[:, :128] + both[:, 128:]

    from_lower = jnp.logical_and(left, dev > 0)
    from_upper = jnp.logical_and(jnp.logical_not(left), dev < ndev - 1)

    def ghosts_of(n):
        wait_bytes(grecv.at[pl.ds(2 * n, 2)], g_rs.at[n])
        ghosts = jnp.where(from_lower, grecv[2 * n].astype(jnp.float32), 0.0)
        return jnp.where(from_upper, grecv[2 * n + 1].astype(jnp.float32), ghosts)

    for s in range(1, nk):
        def form(way):
            dense(way, s, way, [(way, s - 1)], s == 1)

        def pass_on(way, h):
            values = [dmat[way, h * 2 + cp] for cp in range(2)]
            if s > 1:
                for copy in chain_copies(way, s - 1, h):
                    copy.wait_recv()
                values = [values[cp] + arrived(way, s - 1, h, cp) for cp in range(2)]
            send_half(way, s, h, values)
            if s == nk - 1:
                for cp in range(2):
                    split(pmat.at[way], h, cp, values[cp])

        def first(way):
            form(way)
            for h in range(2):
                pass_on(way, h)

        own_arrived(s)
        if s == 1:
            both_ways(first)
        else:
            both_ways(form)
            for h in range(2):
                both_ways(functools.partial(pass_on, h=h))
        if s == 1:
            ghosts = ghosts_of(0)
            esend[0:width, 0:128] = start.astype(jnp.bfloat16)
            esend[0:width, 128:256] = ghosts.astype(jnp.bfloat16)
            turned = jnp.broadcast_to(stay[0:1].astype(jnp.float32), (16, 128))
            esend[width:width + 16, 0:128] = turned.astype(jnp.bfloat16)
            esend[width:width + 16, 128:256] = turned.astype(jnp.bfloat16)
            for way in range(2):
                remote(esend, erecv.at[way], e_ss, e_rs, z_peer(2 * (2 * way - 1))).start()
        if s + 1 < nk:
            send_leaf(s + 1)
            send_own((s + 2) % nk)
    wait_bytes(erecv, e_rs)
    def pass_products(way):
        part = times(erecv[way, 0:width, :], pmat[way])
        turned = erecv[way, width:width + 16, 0:128].astype(jnp.float32)[0:1]
        ysend[way] = jnp.where(turned > 0.5, part, pltpu.roll(part, 64, 1))
        first = lax.rem(z + 2 - 4 * way + nz, nz) + x * nz
        for side in range(2):
            remote(
                ysend.at[way], yrecv.at[side, way], y_ss, y_rs,
                {"dev": lax.rem(first + 1 - 2 * side + ndev, ndev)},
            ).start()

    both_ways(pass_products)
    own_arrived(0)
    dense(0, 0, 0, [(0, nk - 1), (1, nk - 1)], [])
    fetches[6].wait()
    fetches[7].wait()
    diag = diag_v[...]
    inverse = 1.0 / diag
    for c in range(CH):
        split(wmat, c // 2, c % 2, dmat[0, c])
    base = rhs_v[...] - diag * start
    vsend[0:width, :] = pack_ghosts(base - times(esend[0:width, :], wmat[...]))
    vsend[width:width + 8, :] = pack_ghosts(jnp.broadcast_to(inverse * (1.0 / THETA), (8, 128)))
    for way, peer in enumerate((upper, lower)):
        remote(vsend, vrecv.at[way], v_ss, v_rs, peer).start()

    ghost_rows = []
    for h in range(2):
        values = [dmat[0, h * 2 + cp] for cp in range(2)]
        for way in range(2):
            for copy in chain_copies(way, nk - 1, h):
                copy.wait_recv()
            values = [values[cp] + arrived(way, nk - 1, h, cp) for cp in range(2)]
        for cp in range(2):
            split(wmat, h, cp, values[cp])
        ghost_rows.append(values[1])

    for way, peer in enumerate((upper, lower)):
        chosen = jnp.where(ghost_s[0, 1 - way] == 0, ghost_rows[0], ghost_rows[1])
        high = chosen.astype(jnp.bfloat16)
        nsend[way, 0:64, :] = high
        nsend[way, 64:128, :] = (chosen - high.astype(jnp.float32)).astype(jnp.bfloat16)
        remote(nsend.at[way], nrecv.at[way], n_ss, n_rs, peer).start()

    def product(vec, columns):
        return times(vec.astype(jnp.bfloat16), wmat[:, columns:columns + 128])

    def own_part(vec):
        return diag * vec + product(vec, 0)

    def mixed(ref):
        return jnp.where(left, ref[0, 0:width, :], ref[1, 0:width, :])

    def mixed_scale(ref):
        return jnp.where(left[:8], ref[0, width:width + 8, :], ref[1, width:width + 8, :])[0:1]

    def inside(ghosts):
        return jnp.where(jnp.logical_or(from_lower, from_upper), ghosts, 0.0)

    def first_ghosts():
        wait_bytes(vrecv, v_rs)
        wait_bytes(yrecv, y_rs)
        parts = jnp.where(left, yrecv[0, 0] + yrecv[0, 1], yrecv[1, 0] + yrecv[1, 1])
        return inside(mixed_scale(vrecv) * (mixed(vrecv) - parts))

    def neighbour_part(vec, way):
        both = lax.dot_general(
            vec.astype(jnp.bfloat16), nrecv[way], (((1,), (1,)), ((), ())),
            preferred_element_type=jnp.float32,
        )
        return both + pltpu.roll(both, 64, 1)

    def next_ghosts(mine):
        far = jnp.where(jnp.logical_and(left, dev > 1), grecv[4].astype(jnp.float32), 0.0)
        below = jnp.where(left, far, mine)
        far = jnp.where(
            jnp.logical_and(jnp.logical_not(left), dev < ndev - 2),
            grecv[5].astype(jnp.float32), 0.0,
        )
        above = jnp.where(left, mine, far)
        summed = jnp.where(left, neighbour_part(below, 0), neighbour_part(above, 1))
        return inside(mixed(wrecv) - mixed_scale(wrecv) * summed)

    rho = 1.0 / SIGMA
    iterate = start
    residual = base - times(esend[0:width, :], wmat[...])
    direction = residual * (inverse * (1.0 / THETA))
    for step in range(1, STEPS):
        last = step == STEPS - 1
        if last:
            send_ghosts(1, direction)
            remote(gsend.at[1], grecv.at[4], g_ss, g_rs.at[2], upper2).start()
            remote(gsend.at[1], grecv.at[5], g_ss, g_rs.at[2], lower2).start()
        iterate = iterate + direction
        rest = residual - own_part(direction)
        rho_new = 1.0 / (2.0 * SIGMA - rho)
        gain = (2.0 * rho_new / DELTA) * inverse
        kept = (rho_new * rho) * direction + gain * rest
        if last:
            wsend[0:width, :] = pack_ghosts(kept)
            wsend[width:width + 8, :] = pack_ghosts(jnp.broadcast_to(gain, (8, 128)))
            for way, peer in enumerate((upper, lower)):
                remote(wsend, wrecv.at[way], w_ss, w_rs, peer).start()
        ghosts = product(ghosts_of(1) if last else first_ghosts(), 128)
        direction = kept - gain * ghosts
        residual = rest - ghosts
        rho = rho_new
    out_v[...] = iterate + direction
    out_copy = pltpu.make_async_copy(out_v, out_ref.at[0], out_sem)
    out_copy.start()
    rest = residual - own_part(direction)
    wait_bytes(nrecv, n_rs)
    wait_bytes(grecv.at[pl.ds(4, 2)], g_rs.at[2])
    wait_bytes(wrecv, w_rs)
    residual = rest - product(next_ghosts(gsend[1].astype(jnp.float32)), 128)

    squares = jnp.sum((residual * residual).T, axis=0, keepdims=True)
    part = jnp.concatenate([squares, jnp.zeros((1, 128 - width), jnp.float32)], axis=1)
    for buf, ss, rs, here, count, peer in (
        (red_c, red_c_ss, red_c_rs, core, cores, core_peer),
        (red_p, red_p_ss, red_p_rs, plane, chips, plane_peer),
        (red_z, red_z_ss, red_z_rs, z, nz, z_peer),
    ):
        if count == 1:
            continue
        buf[here] = part
        for n in range(1, count):
            remote(buf.at[here], buf.at[here], ss, rs, peer(n)).start()
        wait_bytes(buf.at[pl.ds(0, count - 1)], rs)
        part = buf[0]
        for n in range(1, count):
            part = part + buf[n]
    rms_ref[...] = jnp.sqrt(part * (1.0 / (ng * ndev * 128)))[:, :width]

    out_copy.wait()
    wait_bytes(psend.at[pl.ds(oc, far_row + nx - oc)], p_ss)
    wait_bytes(bsend.at[pl.ds(0, own_slot + (nx - 1) * oc)], b_ss)
    wait_bytes(qsend, q_ss)
    wait_bytes(ssend, s_ss)
    wait_bytes(grecv, g_ss)
    wait_bytes(nsend, n_ss)
    wait_bytes(wrecv, w_ss)
    wait_bytes(erecv, e_ss)
    wait_bytes(yrecv, y_ss)
    wait_bytes(vrecv, v_ss)
    if cores > 1:
        wait_bytes(red_c.at[pl.ds(0, 1)], red_c_ss)
    wait_bytes(red_p.at[pl.ds(0, chips - 1)], red_p_ss)
    wait_bytes(red_z.at[pl.ds(0, nz - 1)], red_z_ss)


def shards(ng, nx, nz, tiles, owner, tile_rows, tile_cols, ghost_rows, rhs, start, diag):
    tcount, block = tiles.shape[1], tiles.shape[2]
    width = rhs.shape[1]
    nk = nz // 4
    f32, bf16, i32, i16 = jnp.float32, jnp.bfloat16, jnp.int32, jnp.int16
    vmem, smem, dma = pltpu.VMEM, pltpu.SMEM, pltpu.SemaphoreType.DMA
    whole = pl.BlockSpec(memory_space=pltpu.VMEM)
    smoothed, rms = pl.pallas_call(
        functools.partial(kernel, ng, nx, nz),
        out_shape=(
            jax.ShapeDtypeStruct((1, width, 128), f32),
            jax.ShapeDtypeStruct((1, width), f32),
        ),
        in_specs=[pl.BlockSpec(memory_space=pltpu.HBM)] * 8,
        out_specs=(pl.BlockSpec(memory_space=pltpu.HBM), whole),
        scratch_shapes=[
            smem((1, tcount), i32),
            smem((1, tcount), i32),
            smem((1, tcount), i32),
            smem((1, 2), i32),
            vmem((tcount, block, block), bf16),
            vmem((width, 128), f32),
            vmem((width, 128), f32),
            vmem((1, 128), f32),
            vmem((8, 128), i32),
            smem((8, 128), i32),
            vmem((nx * (4 * nk), 1, 128), i32),
            vmem((nx * (4 * nk), 1, 128), i32),
            vmem((nx * 4 * nk, 64, 128), bf16),
            vmem((nx, 2 * nk - 1, 64, 128), bf16),
            vmem((2, nk, nx, 64, 128), bf16),
            vmem((nx, 64, 128), bf16),
            vmem((2, CH, 64, 128), f32),
            vmem((2, nk - 1, 2, 2, 64, 128), i16),
            vmem((2, nk - 1, 2, 2, 64, 128), i16),
            vmem((2, nk - 1, 2, 2, 128), f32),
            vmem((2, nk - 1, 2, 2, 128), f32),
            vmem((256, 256), bf16),
            vmem((2, width, 128), bf16),
            vmem((6, width, 128), bf16),
            vmem((2, 128, 128), bf16),
            vmem((2, 128, 128), bf16),
            vmem((width + 8, 128), f32),
            vmem((2, width + 8, 128), f32),
            vmem((width + 16, 256), bf16),
            vmem((2, width + 16, 256), bf16),
            vmem((2, 256, 256), bf16),
            vmem((2, width, 128), f32),
            vmem((2, 2, width, 128), f32),
            vmem((width + 8, 128), f32),
            vmem((2, width + 8, 128), f32),
            vmem((2, 1, 128), f32),
            vmem((ng * nx, 1, 128), f32),
            vmem((nz, 1, 128), f32),
            vmem((width, 128), f32),
            dma((8,)),
            dma,
            dma,
            dma,
            dma,
            dma,
            dma((nk,)),
            dma((2, nk)),
            dma((2,)),
            dma,
            dma((2, nk - 1, 2)),
            dma,
            dma((2, nk - 1, 2)),
            dma,
            dma((3,)),
            dma,
            dma,
            dma,
            dma,
            dma,
            dma,
            dma,
            dma,
            dma,
            dma,
            dma,
            dma,
            dma,
            dma,
            dma,
            dma,
        ],
        compiler_params=pltpu.CompilerParams(
            collective_id=0, has_side_effects=True, vmem_limit_bytes=60 * 1024 * 1024
        ),
    )(owner.reshape(1, tcount), tile_rows, tile_cols, ghost_rows, tiles, rhs, start, diag)
    return smoothed, rms.reshape(width)


def solution(mesh):
    ng = mesh.shape["grp"]
    nx = mesh.shape["dev"] // NZ
    return jax.shard_map(
        functools.partial(shards, ng, nx, NZ),
        mesh=mesh,
        in_specs=(
            P("grp", "dev", None, None),
            P("grp", "dev", None),
            P("grp", "dev"),
            P("grp", "dev"),
            P("grp", "dev"),
            P("grp", None, "dev"),
            P("grp", None, "dev"),
            P("grp", "dev"),
        ),
        out_specs=(P("grp", None, "dev"), P()),
        check_vma=False,
    )
```

```python
import functools

import jax
import jax.numpy as jnp
from jax import lax
from jax.experimental import pallas as pl
from jax.experimental.pallas import tpu as pltpu
from jax.sharding import PartitionSpec as P

STEPS = 3
THETA = (2.0 + 0.2) / 2.0
DELTA = (2.0 - 0.2) / 2.0
SIGMA = THETA / DELTA
NZ = 16
CH = 4
MESH = pl.DeviceIdType.MESH


def kernel(
    ng, nx, nz,
    owner_h, rows_h, cols_h, ghost_h, tiles_h, rhs_h, start_h, diag_h,
    out_ref, rms_ref,
    owner_s, rows_s, cols_s, ghost_s, tiles_v, rhs_v, start_v, diag_v,
    tab_v, tab_s, psend, precv, bsend, xown, lrecv, frecv, dmat,
    qsend, qrecv, ssend, srecv, wmat, gsend, grecv, nsend, nrecv, wsend, wrecv,
    esend, erecv, pmat, ysend, yrecv, vsend, vrecv, red_c, red_p, red_z, out_v, in_sem, tab_sem, out_sem, p_ss, p_rs, b_ss, o_rs, l_rs, f_rs,
    q_ss, q_rs, s_ss, s_rs, g_ss, g_rs, n_ss, n_rs, w_ss, w_rs,
    e_ss, e_rs, y_ss, y_rs, v_ss, v_rs, red_c_ss, red_c_rs, red_p_ss, red_p_rs, red_z_ss, red_z_rs,
):
    half = nz // 2
    nk = half // 2
    ndev = nx * nz
    tcount = tiles_v.shape[0]
    width = rhs_v.shape[0]
    dev = lax.axis_index("dev")
    grp = lax.axis_index("grp")
    x = lax.div(dev, nz)
    z = lax.rem(dev, nz)

    def at(j, k):
        return {"dev": lax.rem(x + j, nx) * nz + lax.rem(z + k + nz, nz)}

    cores = 2 if ng % 2 == 0 else 1
    core = lax.rem(grp, cores)
    chips = ng // cores * nx
    plane = lax.div(grp, cores) * nx + x

    def core_peer(n):
        return {"grp": grp + 1 - 2 * core}

    def plane_peer(n):
        there = lax.rem(plane + n, chips)
        return {"grp": lax.div(there, nx) * cores + core, "dev": lax.rem(there, nx) * nz + z}

    def z_peer(n):
        return at(0, n)

    upper = {"dev": lax.rem(dev + 1, ndev)}
    lower = {"dev": lax.rem(dev + ndev - 1, ndev)}
    upper2 = {"dev": lax.rem(dev + 2, ndev)}
    lower2 = {"dev": lax.rem(dev + ndev - 2, ndev)}

    barrier = pltpu.get_barrier_semaphore()
    def ring_hops(n, count):
        return min(n % count, count - n % count)

    peers = [(ring_hops(j, nx) + 1, at(j, k)) for j in range(nx) for k in (-1, 1)]
    peers += [(ring_hops(j, nx), at(j, 0)) for j in range(1, nx)]
    peers += [(2, at(0, -2)), (2, at(0, 2))]
    peers += [(ring_hops(j, nx) + 2, at(nx - j, 4 * (j % 2) - 2)) for j in range(1, nx)]
    peers += [(2, upper), (2, lower), (3, upper2), (3, lower2)]
    peers += [(0, core_peer(n)) for n in range(1, cores)]
    peers += [
        (ring_hops(n, nx) + ring_hops(n // nx, chips // nx), plane_peer(n))
        for n in range(1, chips)
    ]
    peers = [peer for _, peer in sorted(peers, key=lambda entry: -entry[0])]

    def greet(some):
        for peer in some:
            pl.semaphore_signal(barrier, inc=1, device_id=peer, device_id_type=MESH)

    greet(peers[:10])
    fetches = [
        pltpu.make_async_copy(src, dst, in_sem.at[n])
        for n, (src, dst) in enumerate((
            (owner_h, owner_s), (rows_h, rows_s), (cols_h, cols_s), (ghost_h, ghost_s),
            (tiles_h.at[0], tiles_v), (start_h.at[0], start_v), (rhs_h.at[0], rhs_v),
            (diag_h, diag_v),
        ))
    ]
    for fetch in fetches:
        fetch.start()

    greet(peers[10:])

    lane = lax.broadcasted_iota(jnp.int32, (1, 128), 1)
    none = jnp.full((1, 128), -1, jnp.int32)
    for fetch in fetches[:4]:
        fetch.wait()

    def find(t, held):
        i0, i1, p0, p1 = held
        hit = lane == owner_s[0, t]
        place = rows_s[0, t] * 4 + cols_s[0, t]
        first = jnp.logical_and(hit, i0 < 0)
        second = jnp.logical_and(hit, i0 >= 0)
        return (
            jnp.where(first, t, i0), jnp.where(second, t, i1),
            jnp.where(first, place, p0), jnp.where(second, place, p1),
        )

    i0, i1, p0, p1 = lax.fori_loop(0, tcount, find, (none,) * 4, unroll=True)
    tab_v[0:1, :] = jnp.maximum(i0, 0)
    tab_v[1:2, :] = jnp.maximum(i1, 0)
    tab_v[2:3, :] = p0
    tab_v[3:4, :] = p1
    tab_copy = pltpu.make_async_copy(tab_v, tab_s, tab_sem)
    tab_copy.start()

    wide = lax.broadcasted_iota(jnp.int32, (width, 128), 1)
    left = wide < 64
    stay = jnp.where(left, ghost_s[0, 1], 1 - ghost_s[0, 0]) == 0

    def pack_ghosts(vec):
        return jnp.where(stay[:vec.shape[0]], vec, pltpu.roll(vec, 64, 1))

    def remote(src, dst, ss, rs, peer):
        return pltpu.make_async_remote_copy(
            src_ref=src, dst_ref=dst, send_sem=ss, recv_sem=rs,
            device_id=peer, device_id_type=MESH,
        )

    def wait_bytes(ref, sem):
        pltpu.make_async_copy(ref, ref, sem).wait()

    def send_ghosts(n, vec):
        gsend[n] = pack_ghosts(vec).astype(jnp.bfloat16)
        for way, peer in enumerate((upper, lower)):
            remote(gsend.at[n], grecv.at[2 * n + way], g_ss, g_rs.at[n], peer).start()

    def owner_of(j, step):
        return lax.rem(x + j, nx) * nz + lax.rem(z + step + nz, nz)

    def own_step(fam, k):
        if k == 0:
            return 0
        return half - 2 * k if fam == 0 else 2 * k - half

    def leaf_step(way, k):
        return half - 1 - 2 * k if way == 0 else 2 * k + 1 - half

    def pair(o):
        return jnp.concatenate([tiles_v[tab_s[0, o]], tiles_v[tab_s[1, o]]], axis=1)

    def place(o):
        return jnp.where(lane < 64, tab_s[2, o], tab_s[3, o])

    oc = 2 * nk - 1
    leaf_row, far_row = nx * oc, nx * oc + 2 * nx * nk
    leaf_slot, own_slot = nx, nx + 2 * nk * nx

    def own_index(k, fam):
        return oc - 1 if k == 0 else 2 * (k - 1) + fam

    def over_x(body, count=nx):
        def turn(i, _):
            body(lax.rem(i + 1, nx))
            return 0

        lax.fori_loop(0, count, turn, 0)

    def far_hops(j):
        return 2 - 4 * lax.rem(j, 2)

    def own_slots(j):
        return own_slot + lax.rem(j + nx - 1, nx) * oc

    def send_rows(first, count, peer):
        rows = pl.ds(first, count)
        remote(psend.at[rows], precv.at[rows], p_ss, p_rs, peer).start()

    def send_places():
        def body(j):
            for way in range(2):
                send_rows(leaf_row + (way * nx + j) * nk, nk, at(j, 1 - 2 * way))
            send_rows(far_row + j, 1, at(j, far_hops(j)))

        over_x(body)
        over_x(lambda j: send_rows(j * oc, oc, at(j, 0)), nx - 1)

    def send_far():
        def body(j):
            remote(
                bsend.at[j], frecv.at[j], b_ss, f_rs.at[lax.rem(j, 2)], at(j, far_hops(j))
            ).start()

        over_x(body)

    def send_leaf(k):
        def body(j):
            for way in range(2):
                slot = leaf_slot + (way * nk + k) * nx + j
                remote(
                    bsend.at[slot], lrecv.at[way, k, j], b_ss, l_rs.at[way, k],
                    at(j, 1 - 2 * way),
                ).start()

        over_x(body)

    def send_own(k):
        def body(j):
            count = 1 if k == 0 else 2
            remote(
                bsend.at[pl.ds(own_slots(j) + own_index(k, 0), count)],
                xown.at[j, pl.ds(own_index(k, 0), count)], b_ss, o_rs.at[k], at(j, 0),
            ).start()

        over_x(body, nx - 1)

    tab_copy.wait()
    fetches[4].wait()
    fetches[5].wait()
    start = start_v[...]
    def pack(j):
        o = owner_of(j, half)
        psend[far_row + j] = place(o)
        bsend[j] = pair(o)
        for k in range(nk):
            for way in range(2):
                o = owner_of(j, leaf_step(way, k))
                psend[leaf_row + (way * nx + j) * nk + k] = place(o)
                bsend[leaf_slot + (way * nk + k) * nx + j] = pair(o)
            for fam in range(1 if k == 0 else 2):
                o = owner_of(j, own_step(fam, k))
                psend[j * oc + own_index(k, fam)] = place(o)
                bsend[own_slots(j) + own_index(k, fam)] = pair(o)

    over_x(pack)
    precv[0:oc] = psend[0:oc]
    xown[0] = bsend[own_slot + (nx - 1) * oc:own_slot + nx * oc]

    pl.semaphore_wait(barrier, len(peers))
    send_ghosts(0, start)
    send_far()
    send_leaf(0)
    send_own(1)
    send_places()
    send_leaf(1)
    send_own(2 % nk)

    right_half = (lane >= 64).astype(jnp.int32)

    def add_pair(acc, both, row):
        both = both.astype(jnp.float32)
        swapped = pltpu.roll(both, 64, 1)
        row_swapped = pltpu.roll(row, 64, 1)
        out = []
        for c in range(CH):
            target = (c // 2) * 4 + (c % 2) * 2 + right_half
            value = acc[c] + jnp.where(row == target, both, 0.0)
            out.append(value + jnp.where(row_swapped == target, swapped, 0.0))
        return tuple(out)

    def own_arrived(k):
        count = 1 if k == 0 else 2
        wait_bytes(xown.at[pl.ds(1, nx - 1), pl.ds(own_index(k, 0), count)], o_rs.at[k])

    def dense(n, k, fam, leaves, far):
        acc = tuple(jnp.zeros((64, 128), jnp.float32) for _ in range(CH))
        if far:
            wait_bytes(frecv.at[pl.ds(0, nx // 2)], f_rs.at[fam])
            for i in range(nx // 2):
                acc = add_pair(acc, frecv[2 * i + fam], precv[far_row + 2 * i + fam])
        for way, kk in leaves:
            wait_bytes(lrecv.at[way, kk], l_rs.at[way, kk])
            for j in range(nx):
                row = leaf_row + (way * nx + j) * nk + kk
                acc = add_pair(acc, lrecv[way, kk, j], precv[row])
        for j in range(nx):
            i = own_index(k, fam)
            acc = add_pair(acc, xown[j, i], precv[j * oc + i])
        for c in range(CH):
            dmat[n, c] = acc[c]

    def both_ways(body):
        def turn(way, _):
            body(way)
            return 0

        lax.fori_loop(0, 2, turn, 0)

    def chain_copies(way, s, h):
        peer = z_peer(2 - 4 * way)
        n = s - 1
        return (
            remote(ssend.at[way, n, h], srecv.at[way, n, h], s_ss, s_rs.at[way, n, h], peer),
            remote(qsend.at[way, n, h], qrecv.at[way, n, h], q_ss, q_rs.at[way, n, h], peer),
        )

    def send_half(way, s, h, values):
        for cp in range(2):
            most = jnp.maximum(jnp.max(jnp.abs(values[cp]), axis=0, keepdims=True), 1e-30)
            scaled = jnp.round(values[cp] * (32767.0 / most))
            qsend[way, s - 1, h, cp] = scaled.astype(jnp.int32).astype(jnp.int16)
            ssend[way, s - 1, h, cp:cp + 1, :] = most * (1.0 / 32767.0)
        for copy in chain_copies(way, s, h):
            copy.start()

    def arrived(way, s, h, cp):
        whole = qrecv[way, s - 1, h, cp].astype(jnp.int32).astype(jnp.float32)
        return whole * srecv[way, s - 1, h, cp:cp + 1, :]

    wait_bytes(precv.at[pl.ds(oc, far_row + nx - oc)], p_rs)
    def split(matrix, h, cp, value):
        high = value.astype(jnp.bfloat16)
        low = (value - high.astype(jnp.float32)).astype(jnp.bfloat16)
        matrix[h * 64:h * 64 + 64, cp * 128:cp * 128 + 128] = high
        matrix[128 + h * 64:192 + h * 64, cp * 128:cp * 128 + 128] = low

    def times(vec, matrix):
        both = lax.dot_general(
            vec, matrix, (((1,), (1,)), ((), ())), preferred_element_type=jnp.float32
        )
        return both[:, :128] + both[:, 128:]

    from_lower = jnp.logical_and(left, dev > 0)
    from_upper = jnp.logical_and(jnp.logical_not(left), dev < ndev - 1)

    def ghosts_of(n):
        wait_bytes(grecv.at[pl.ds(2 * n, 2)], g_rs.at[n])
        ghosts = jnp.where(from_lower, grecv[2 * n].astype(jnp.float32), 0.0)
        return jnp.where(from_upper, grecv[2 * n + 1].astype(jnp.float32), ghosts)

    for s in range(1, nk):
        def form(way):
            dense(way, s, way, [(way, s - 1)], s == 1)

        def pass_on(way, h):
            values = [dmat[way, h * 2 + cp] for cp in range(2)]
            if s > 1:
                for copy in chain_copies(way, s - 1, h):
                    copy.wait_recv()
                values = [values[cp] + arrived(way, s - 1, h, cp) for cp in range(2)]
            send_half(way, s, h, values)
            if s == nk - 1:
                for cp in range(2):
                    split(pmat.at[way], h, cp, values[cp])

        def first(way):
            form(way)
            for h in range(2):
                pass_on(way, h)

        own_arrived(s)
        if s == 1:
            both_ways(first)
        else:
            both_ways(form)
            for h in range(2):
                both_ways(functools.partial(pass_on, h=h))
        if s == 1:
            ghosts = ghosts_of(0)
            esend[0:width, 0:128] = start.astype(jnp.bfloat16)
            esend[0:width, 128:256] = ghosts.astype(jnp.bfloat16)
            turned = jnp.broadcast_to(stay[0:1].astype(jnp.float32), (16, 128))
            esend[width:width + 16, 0:128] = turned.astype(jnp.bfloat16)
            esend[width:width + 16, 128:256] = turned.astype(jnp.bfloat16)
            for way in range(2):
                remote(esend, erecv.at[way], e_ss, e_rs, z_peer(2 * (2 * way - 1))).start()
        if s + 1 < nk:
            send_leaf(s + 1)
            send_own((s + 2) % nk)
    wait_bytes(erecv, e_rs)
    def pass_products(way):
        part = times(erecv[way, 0:width, :], pmat[way])
        turned = erecv[way, width:width + 16, 0:128].astype(jnp.float32)[0:1]
        ysend[way] = jnp.where(turned > 0.5, part, pltpu.roll(part, 64, 1))
        first = lax.rem(z + 2 - 4 * way + nz, nz) + x * nz
        for side in range(2):
            remote(
                ysend.at[way], yrecv.at[side, way], y_ss, y_rs,
                {"dev": lax.rem(first + 1 - 2 * side + ndev, ndev)},
            ).start()

    both_ways(pass_products)
    own_arrived(0)
    dense(0, 0, 0, [(0, nk - 1), (1, nk - 1)], [])
    fetches[6].wait()
    fetches[7].wait()
    diag = diag_v[...]
    inverse = 1.0 / diag
    for c in range(CH):
        split(wmat, c // 2, c % 2, dmat[0, c])
    base = rhs_v[...] - diag * start
    vsend[0:width, :] = pack_ghosts(base - times(esend[0:width, :], wmat[...]))
    vsend[width:width + 8, :] = pack_ghosts(jnp.broadcast_to(inverse * (1.0 / THETA), (8, 128)))
    for way, peer in enumerate((upper, lower)):
        remote(vsend, vrecv.at[way], v_ss, v_rs, peer).start()

    ghost_rows = []
    for h in range(2):
        values = [dmat[0, h * 2 + cp] for cp in range(2)]
        for way in range(2):
            for copy in chain_copies(way, nk - 1, h):
                copy.wait_recv()
            values = [values[cp] + arrived(way, nk - 1, h, cp) for cp in range(2)]
        for cp in range(2):
            split(wmat, h, cp, values[cp])
        ghost_rows.append(values[1])

    for way, peer in enumerate((upper, lower)):
        chosen = jnp.where(ghost_s[0, 1 - way] == 0, ghost_rows[0], ghost_rows[1])
        high = chosen.astype(jnp.bfloat16)
        nsend[way, 0:64, :] = high
        nsend[way, 64:128, :] = (chosen - high.astype(jnp.float32)).astype(jnp.bfloat16)
        remote(nsend.at[way], nrecv.at[way], n_ss, n_rs, peer).start()

    def product(vec, columns):
        return times(vec.astype(jnp.bfloat16), wmat[:, columns:columns + 128])

    def own_part(vec):
        return diag * vec + product(vec, 0)

    def mixed(ref):
        return jnp.where(left, ref[0, 0:width, :], ref[1, 0:width, :])

    def mixed_scale(ref):
        return jnp.where(left[:8], ref[0, width:width + 8, :], ref[1, width:width + 8, :])[0:1]

    def inside(ghosts):
        return jnp.where(jnp.logical_or(from_lower, from_upper), ghosts, 0.0)

    def first_ghosts():
        wait_bytes(vrecv, v_rs)
        wait_bytes(yrecv, y_rs)
        parts = jnp.where(left, yrecv[0, 0] + yrecv[0, 1], yrecv[1, 0] + yrecv[1, 1])
        return inside(mixed_scale(vrecv) * (mixed(vrecv) - parts))

    def neighbour_part(vec, way):
        both = lax.dot_general(
            vec.astype(jnp.bfloat16), nrecv[way], (((1,), (1,)), ((), ())),
            preferred_element_type=jnp.float32,
        )
        return both + pltpu.roll(both, 64, 1)

    def next_ghosts(mine):
        far = jnp.where(jnp.logical_and(left, dev > 1), grecv[4].astype(jnp.float32), 0.0)
        below = jnp.where(left, far, mine)
        far = jnp.where(
            jnp.logical_and(jnp.logical_not(left), dev < ndev - 2),
            grecv[5].astype(jnp.float32), 0.0,
        )
        above = jnp.where(left, mine, far)
        summed = jnp.where(left, neighbour_part(below, 0), neighbour_part(above, 1))
        return inside(mixed(wrecv) - mixed_scale(wrecv) * summed)

    rho = 1.0 / SIGMA
    iterate = start
    residual = base - times(esend[0:width, :], wmat[...])
    direction = residual * (inverse * (1.0 / THETA))
    for step in range(1, STEPS):
        last = step == STEPS - 1
        if last:
            send_ghosts(1, direction)
            remote(gsend.at[1], grecv.at[4], g_ss, g_rs.at[2], upper2).start()
            remote(gsend.at[1], grecv.at[5], g_ss, g_rs.at[2], lower2).start()
        iterate = iterate + direction
        rest = residual - own_part(direction)
        rho_new = 1.0 / (2.0 * SIGMA - rho)
        gain = (2.0 * rho_new / DELTA) * inverse
        kept = (rho_new * rho) * direction + gain * rest
        if last:
            wsend[0:width, :] = pack_ghosts(kept)
            wsend[width:width + 8, :] = pack_ghosts(jnp.broadcast_to(gain, (8, 128)))
            for way, peer in enumerate((upper, lower)):
                remote(wsend, wrecv.at[way], w_ss, w_rs, peer).start()
        ghosts = product(ghosts_of(1) if last else first_ghosts(), 128)
        direction = kept - gain * ghosts
        residual = rest - ghosts
        rho = rho_new
    out_v[...] = iterate + direction
    out_copy = pltpu.make_async_copy(out_v, out_ref.at[0], out_sem)
    out_copy.start()
    rest = residual - own_part(direction)
    wait_bytes(nrecv, n_rs)
    wait_bytes(grecv.at[pl.ds(4, 2)], g_rs.at[2])
    wait_bytes(wrecv, w_rs)
    residual = rest - product(next_ghosts(gsend[1].astype(jnp.float32)), 128)

    squares = jnp.sum((residual * residual).T, axis=0, keepdims=True)
    part = jnp.concatenate([squares, jnp.zeros((1, 128 - width), jnp.float32)], axis=1)
    for buf, ss, rs, here, count, peer in (
        (red_c, red_c_ss, red_c_rs, core, cores, core_peer),
        (red_p, red_p_ss, red_p_rs, plane, chips, plane_peer),
        (red_z, red_z_ss, red_z_rs, z, nz, z_peer),
    ):
        if count == 1:
            continue
        buf[here] = part
        for n in range(1, count):
            remote(buf.at[here], buf.at[here], ss, rs, peer(n)).start()
        wait_bytes(buf.at[pl.ds(0, count - 1)], rs)
        part = buf[0]
        for n in range(1, count):
            part = part + buf[n]
    rms_ref[...] = jnp.sqrt(part * (1.0 / (ng * ndev * 128)))[:, :width]

    out_copy.wait()
    wait_bytes(psend.at[pl.ds(oc, far_row + nx - oc)], p_ss)
    wait_bytes(bsend.at[pl.ds(0, own_slot + (nx - 1) * oc)], b_ss)
    wait_bytes(qsend, q_ss)
    wait_bytes(ssend, s_ss)
    wait_bytes(grecv, g_ss)
    wait_bytes(nsend, n_ss)
    wait_bytes(wrecv, w_ss)
    wait_bytes(erecv, e_ss)
    wait_bytes(yrecv, y_ss)
    wait_bytes(vrecv, v_ss)
    if cores > 1:
        wait_bytes(red_c.at[pl.ds(0, 1)], red_c_ss)
    wait_bytes(red_p.at[pl.ds(0, chips - 1)], red_p_ss)
    wait_bytes(red_z.at[pl.ds(0, nz - 1)], red_z_ss)


def shards(ng, nx, nz, tiles, owner, tile_rows, tile_cols, ghost_rows, rhs, start, diag):
    tcount, block = tiles.shape[1], tiles.shape[2]
    width = rhs.shape[1]
    nk = nz // 4
    f32, bf16, i32, i16 = jnp.float32, jnp.bfloat16, jnp.int32, jnp.int16
    vmem, smem, dma = pltpu.VMEM, pltpu.SMEM, pltpu.SemaphoreType.DMA
    whole = pl.BlockSpec(memory_space=pltpu.VMEM)
    smoothed, rms = pl.pallas_call(
        functools.partial(kernel, ng, nx, nz),
        out_shape=(
            jax.ShapeDtypeStruct((1, width, 128), f32),
            jax.ShapeDtypeStruct((1, width), f32),
        ),
        in_specs=[pl.BlockSpec(memory_space=pltpu.HBM)] * 8,
        out_specs=(pl.BlockSpec(memory_space=pltpu.HBM), whole),
        scratch_shapes=[
            smem((1, tcount), i32),
            smem((1, tcount), i32),
            smem((1, tcount), i32),
            smem((1, 2), i32),
            vmem((tcount, block, block), bf16),
            vmem((width, 128), f32),
            vmem((width, 128), f32),
            vmem((1, 128), f32),
            vmem((8, 128), i32),
            smem((8, 128), i32),
            vmem((nx * (4 * nk), 1, 128), i32),
            vmem((nx * (4 * nk), 1, 128), i32),
            vmem((nx * 4 * nk, 64, 128), bf16),
            vmem((nx, 2 * nk - 1, 64, 128), bf16),
            vmem((2, nk, nx, 64, 128), bf16),
            vmem((nx, 64, 128), bf16),
            vmem((2, CH, 64, 128), f32),
            vmem((2, nk - 1, 2, 2, 64, 128), i16),
            vmem((2, nk - 1, 2, 2, 64, 128), i16),
            vmem((2, nk - 1, 2, 2, 128), f32),
            vmem((2, nk - 1, 2, 2, 128), f32),
            vmem((256, 256), bf16),
            vmem((2, width, 128), bf16),
            vmem((6, width, 128), bf16),
            vmem((2, 128, 128), bf16),
            vmem((2, 128, 128), bf16),
            vmem((width + 8, 128), f32),
            vmem((2, width + 8, 128), f32),
            vmem((width + 16, 256), bf16),
            vmem((2, width + 16, 256), bf16),
            vmem((2, 256, 256), bf16),
            vmem((2, width, 128), f32),
            vmem((2, 2, width, 128), f32),
            vmem((width + 8, 128), f32),
            vmem((2, width + 8, 128), f32),
            vmem((2, 1, 128), f32),
            vmem((ng * nx, 1, 128), f32),
            vmem((nz, 1, 128), f32),
            vmem((width, 128), f32),
            dma((8,)),
            dma,
            dma,
            dma,
            dma,
            dma,
            dma((nk,)),
            dma((2, nk)),
            dma((2,)),
            dma,
            dma((2, nk - 1, 2)),
            dma,
            dma((2, nk - 1, 2)),
            dma,
            dma((3,)),
            dma,
            dma,
            dma,
            dma,
            dma,
            dma,
            dma,
            dma,
            dma,
            dma,
            dma,
            dma,
            dma,
            dma,
            dma,
            dma,
        ],
        compiler_params=pltpu.CompilerParams(
            collective_id=0, has_side_effects=True, vmem_limit_bytes=60 * 1024 * 1024
        ),
    )(owner.reshape(1, tcount), tile_rows, tile_cols, ghost_rows, tiles, rhs, start, diag)
    return smoothed, rms.reshape(width)


def solution(mesh):
    ng = mesh.shape["grp"]
    nx = mesh.shape["dev"] // NZ
    return jax.shard_map(
        functools.partial(shards, ng, nx, NZ),
        mesh=mesh,
        in_specs=(
            P("grp", "dev", None, None),
            P("grp", "dev", None),
            P("grp", "dev"),
            P("grp", "dev"),
            P("grp", "dev"),
            P("grp", None, "dev"),
            P("grp", None, "dev"),
            P("grp", "dev"),
        ),
        out_specs=(P("grp", None, "dev"), P()),
        check_vma=False,
    )
```

```python
import functools

import jax
import jax.numpy as jnp
from jax import lax
from jax.experimental import pallas as pl
from jax.experimental.pallas import tpu as pltpu
from jax.sharding import PartitionSpec as P

STEPS = 3
THETA = (2.0 + 0.2) / 2.0
DELTA = (2.0 - 0.2) / 2.0
SIGMA = THETA / DELTA
NZ = 16
CH = 4
MESH = pl.DeviceIdType.MESH


def kernel(
    ng, nx, nz,
    owner_h, rows_h, cols_h, ghost_h, tiles_h, rhs_h, start_h, diag_h,
    out_ref, rms_ref,
    owner_s, rows_s, cols_s, ghost_s, tiles_v, rhs_v, start_v, diag_v,
    tab_v, tab_s, psend, precv, bsend, xown, lrecv, frecv, dmat,
    qsend, qrecv, ssend, srecv, wmat, gsend, grecv, nsend, nrecv, wsend, wrecv,
    esend, erecv, pmat, ysend, yrecv, vsend, vrecv, red_c, red_p, red_z, out_v, in_sem, tab_sem, out_sem, p_ss, p_rs, b_ss, o_rs, l_rs, f_rs,
    q_ss, q_rs, s_ss, s_rs, g_ss, g_rs, n_ss, n_rs, w_ss, w_rs,
    e_ss, e_rs, y_ss, y_rs, v_ss, v_rs, red_c_ss, red_c_rs, red_p_ss, red_p_rs, red_z_ss, red_z_rs,
):
    half = nz // 2
    nk = half // 2
    ndev = nx * nz
    tcount = tiles_v.shape[0]
    width = rhs_v.shape[0]
    dev = lax.axis_index("dev")
    grp = lax.axis_index("grp")
    x = lax.div(dev, nz)
    z = lax.rem(dev, nz)

    def at(j, k):
        return {"dev": lax.rem(x + j, nx) * nz + lax.rem(z + k + nz, nz)}

    cores = 2 if ng % 2 == 0 else 1
    core = lax.rem(grp, cores)
    chips = ng // cores * nx
    plane = lax.div(grp, cores) * nx + x

    def core_peer(n):
        return {"grp": grp + 1 - 2 * core}

    def plane_peer(n):
        there = lax.rem(plane + n, chips)
        return {"grp": lax.div(there, nx) * cores + core, "dev": lax.rem(there, nx) * nz + z}

    def z_peer(n):
        return at(0, n)

    upper = {"dev": lax.rem(dev + 1, ndev)}
    lower = {"dev": lax.rem(dev + ndev - 1, ndev)}
    upper2 = {"dev": lax.rem(dev + 2, ndev)}
    lower2 = {"dev": lax.rem(dev + ndev - 2, ndev)}

    barrier = pltpu.get_barrier_semaphore()
    def ring_hops(n, count):
        return min(n % count, count - n % count)

    peers = [(ring_hops(j, nx) + 1, at(j, k)) for j in range(nx) for k in (-1, 1)]
    peers += [(ring_hops(j, nx), at(j, 0)) for j in range(1, nx)]
    peers += [(2, at(0, -2)), (2, at(0, 2))]
    peers += [(ring_hops(j, nx) + 2, at(nx - j, 4 * (j % 2) - 2)) for j in range(1, nx)]
    peers += [(2, upper), (2, lower), (3, upper2), (3, lower2)]
    peers += [(0, core_peer(n)) for n in range(1, cores)]
    peers += [
        (ring_hops(n, nx) + ring_hops(n // nx, chips // nx), plane_peer(n))
        for n in range(1, chips)
    ]
    peers = [peer for _, peer in sorted(peers, key=lambda entry: -entry[0])]

    def greet(some):
        for peer in some:
            pl.semaphore_signal(barrier, inc=1, device_id=peer, device_id_type=MESH)

    greet(peers[:10])
    fetches = [
        pltpu.make_async_copy(src, dst, in_sem.at[n])
        for n, (src, dst) in enumerate((
            (owner_h, owner_s), (rows_h, rows_s), (cols_h, cols_s), (ghost_h, ghost_s),
            (tiles_h.at[0], tiles_v), (start_h.at[0], start_v), (rhs_h.at[0], rhs_v),
            (diag_h, diag_v),
        ))
    ]
    for fetch in fetches:
        fetch.start()

    greet(peers[10:])

    lane = lax.broadcasted_iota(jnp.int32, (1, 128), 1)
    none = jnp.full((1, 128), -1, jnp.int32)
    for fetch in fetches[:4]:
        fetch.wait()

    def find(t, held):
        i0, i1, p0, p1 = held
        hit = lane == owner_s[0, t]
        place = rows_s[0, t] * 4 + cols_s[0, t]
        first = jnp.logical_and(hit, i0 < 0)
        second = jnp.logical_and(hit, i0 >= 0)
        return (
            jnp.where(first, t, i0), jnp.where(second, t, i1),
            jnp.where(first, place, p0), jnp.where(second, place, p1),
        )

    i0, i1, p0, p1 = lax.fori_loop(0, tcount, find, (none,) * 4, unroll=True)
    tab_v[0:1, :] = jnp.maximum(i0, 0)
    tab_v[1:2, :] = jnp.maximum(i1, 0)
    tab_v[2:3, :] = p0
    tab_v[3:4, :] = p1
    tab_copy = pltpu.make_async_copy(tab_v, tab_s, tab_sem)
    tab_copy.start()

    wide = lax.broadcasted_iota(jnp.int32, (width, 128), 1)
    left = wide < 64
    stay = jnp.where(left, ghost_s[0, 1], 1 - ghost_s[0, 0]) == 0

    def pack_ghosts(vec):
        return jnp.where(stay[:vec.shape[0]], vec, pltpu.roll(vec, 64, 1))

    def remote(src, dst, ss, rs, peer):
        return pltpu.make_async_remote_copy(
            src_ref=src, dst_ref=dst, send_sem=ss, recv_sem=rs,
            device_id=peer, device_id_type=MESH,
        )

    def wait_bytes(ref, sem):
        pltpu.make_async_copy(ref, ref, sem).wait()

    def send_ghosts(n, vec):
        gsend[n] = pack_ghosts(vec).astype(jnp.bfloat16)
        for way, peer in enumerate((upper, lower)):
            remote(gsend.at[n], grecv.at[2 * n + way], g_ss, g_rs.at[n], peer).start()

    def owner_of(j, step):
        return lax.rem(x + j, nx) * nz + lax.rem(z + step + nz, nz)

    def own_step(fam, k):
        if k == 0:
            return 0
        return half - 2 * k if fam == 0 else 2 * k - half

    def leaf_step(way, k):
        return half - 1 - 2 * k if way == 0 else 2 * k + 1 - half

    def pair(o):
        return jnp.concatenate([tiles_v[tab_s[0, o]], tiles_v[tab_s[1, o]]], axis=1)

    def place(o):
        return jnp.where(lane < 64, tab_s[2, o], tab_s[3, o])

    oc = 2 * nk - 1
    leaf_row, far_row = nx * oc, nx * oc + 2 * nx * nk
    leaf_slot, own_slot = nx, nx + 2 * nk * nx

    def own_index(k, fam):
        return oc - 1 if k == 0 else 2 * (k - 1) + fam

    def over_x(body, count=nx):
        def turn(i, _):
            body(lax.rem(i + 1, nx))
            return 0

        lax.fori_loop(0, count, turn, 0)

    def far_hops(j):
        return 2 - 4 * lax.rem(j, 2)

    def own_slots(j):
        return own_slot + lax.rem(j + nx - 1, nx) * oc

    def send_rows(first, count, peer):
        rows = pl.ds(first, count)
        remote(psend.at[rows], precv.at[rows], p_ss, p_rs, peer).start()

    def send_places():
        def body(j):
            for way in range(2):
                send_rows(leaf_row + (way * nx + j) * nk, nk, at(j, 1 - 2 * way))
            send_rows(far_row + j, 1, at(j, far_hops(j)))

        over_x(body)
        over_x(lambda j: send_rows(j * oc, oc, at(j, 0)), nx - 1)

    def send_far():
        def body(j):
            remote(
                bsend.at[j], frecv.at[j], b_ss, f_rs.at[lax.rem(j, 2)], at(j, far_hops(j))
            ).start()

        over_x(body)

    def send_leaf(k):
        def body(j):
            for way in range(2):
                slot = leaf_slot + (way * nk + k) * nx + j
                remote(
                    bsend.at[slot], lrecv.at[way, k, j], b_ss, l_rs.at[way, k],
                    at(j, 1 - 2 * way),
                ).start()

        over_x(body)

    def send_own(k):
        def body(j):
            count = 1 if k == 0 else 2
            remote(
                bsend.at[pl.ds(own_slots(j) + own_index(k, 0), count)],
                xown.at[j, pl.ds(own_index(k, 0), count)], b_ss, o_rs.at[k], at(j, 0),
            ).start()

        over_x(body, nx - 1)

    tab_copy.wait()
    fetches[4].wait()
    fetches[5].wait()
    start = start_v[...]
    def pack(j):
        o = owner_of(j, half)
        psend[far_row + j] = place(o)
        bsend[j] = pair(o)
        for k in range(nk):
            for way in range(2):
                o = owner_of(j, leaf_step(way, k))
                psend[leaf_row + (way * nx + j) * nk + k] = place(o)
                bsend[leaf_slot + (way * nk + k) * nx + j] = pair(o)
            for fam in range(1 if k == 0 else 2):
                o = owner_of(j, own_step(fam, k))
                psend[j * oc + own_index(k, fam)] = place(o)
                bsend[own_slots(j) + own_index(k, fam)] = pair(o)

    over_x(pack)
    precv[0:oc] = psend[0:oc]
    xown[0] = bsend[own_slot + (nx - 1) * oc:own_slot + nx * oc]

    pl.semaphore_wait(barrier, len(peers))
    send_ghosts(0, start)
    send_far()
    send_leaf(0)
    send_own(1)
    send_places()
    send_leaf(1)
    send_own(2 % nk)

    right_half = (lane >= 64).astype(jnp.int32)

    def add_pair(acc, both, row):
        both = both.astype(jnp.float32)
        swapped = pltpu.roll(both, 64, 1)
        row_swapped = pltpu.roll(row, 64, 1)
        out = []
        for c in range(CH):
            target = (c // 2) * 4 + (c % 2) * 2 + right_half
            value = acc[c] + jnp.where(row == target, both, 0.0)
            out.append(value + jnp.where(row_swapped == target, swapped, 0.0))
        return tuple(out)

    def own_arrived(k):
        count = 1 if k == 0 else 2
        wait_bytes(xown.at[pl.ds(1, nx - 1), pl.ds(own_index(k, 0), count)], o_rs.at[k])

    def dense(n, k, fam, leaves, far):
        acc = tuple(jnp.zeros((64, 128), jnp.float32) for _ in range(CH))
        if far:
            wait_bytes(frecv.at[pl.ds(0, nx // 2)], f_rs.at[fam])
            for i in range(nx // 2):
                acc = add_pair(acc, frecv[2 * i + fam], precv[far_row + 2 * i + fam])
        for way, kk in leaves:
            wait_bytes(lrecv.at[way, kk], l_rs.at[way, kk])
            for j in range(nx):
                row = leaf_row + (way * nx + j) * nk + kk
                acc = add_pair(acc, lrecv[way, kk, j], precv[row])
        for j in range(nx):
            i = own_index(k, fam)
            acc = add_pair(acc, xown[j, i], precv[j * oc + i])
        for c in range(CH):
            dmat[n, c] = acc[c]

    def both_ways(body):
        def turn(way, _):
            body(way)
            return 0

        lax.fori_loop(0, 2, turn, 0)

    def chain_copies(way, s, h, cp):
        peer = z_peer(2 - 4 * way)
        at_n = (way, s - 1, h, cp)
        return (
            remote(ssend.at[at_n], srecv.at[at_n], s_ss, s_rs.at[at_n], peer),
            remote(qsend.at[at_n], qrecv.at[at_n], q_ss, q_rs.at[at_n], peer),
        )

    def send_chunk(way, s, h, cp, value):
        most = jnp.maximum(jnp.max(jnp.abs(value), axis=0, keepdims=True), 1e-30)
        scaled = jnp.round(value * (32767.0 / most))
        qsend[way, s - 1, h, cp] = scaled.astype(jnp.int32).astype(jnp.int16)
        ssend[way, s - 1, h, cp] = most * (1.0 / 32767.0)
        for copy in chain_copies(way, s, h, cp):
            copy.start()

    def arrived(way, s, h, cp):
        for copy in chain_copies(way, s, h, cp):
            copy.wait_recv()
        whole = qrecv[way, s - 1, h, cp].astype(jnp.int32).astype(jnp.float32)
        return whole * srecv[way, s - 1, h, cp]

    wait_bytes(precv.at[pl.ds(oc, far_row + nx - oc)], p_rs)

    def split(matrix, h, cp, value):
        high = value.astype(jnp.bfloat16)
        low = (value - high.astype(jnp.float32)).astype(jnp.bfloat16)
        matrix[h * 64:h * 64 + 64, cp * 128:cp * 128 + 128] = high
        matrix[128 + h * 64:192 + h * 64, cp * 128:cp * 128 + 128] = low

    def times(vec, matrix):
        both = lax.dot_general(
            vec, matrix, (((1,), (1,)), ((), ())), preferred_element_type=jnp.float32
        )
        return both[:, :128] + both[:, 128:]

    from_lower = jnp.logical_and(left, dev > 0)
    from_upper = jnp.logical_and(jnp.logical_not(left), dev < ndev - 1)

    def ghosts_of(n):
        wait_bytes(grecv.at[pl.ds(2 * n, 2)], g_rs.at[n])
        ghosts = jnp.where(from_lower, grecv[2 * n].astype(jnp.float32), 0.0)
        return jnp.where(from_upper, grecv[2 * n + 1].astype(jnp.float32), ghosts)

    for s in range(1, nk):
        def form(way):
            dense(way, s, way, [(way, s - 1)], s == 1)

        def pass_on(way, h, cp):
            value = dmat[way, h * 2 + cp]
            if s > 1:
                value = value + arrived(way, s - 1, h, cp)
            send_chunk(way, s, h, cp, value)
            if s == nk - 1:
                split(pmat.at[way], h, cp, value)

        def first(way):
            form(way)
            for c in range(CH):
                pass_on(way, c // 2, c % 2)

        own_arrived(s)
        if s == 1:
            both_ways(first)
        else:
            both_ways(form)
            for c in range(CH):
                both_ways(functools.partial(pass_on, h=c // 2, cp=c % 2))
        if s == 1:
            ghosts = ghosts_of(0)
            esend[0:width, 0:128] = start.astype(jnp.bfloat16)
            esend[0:width, 128:256] = ghosts.astype(jnp.bfloat16)
            turned = jnp.broadcast_to(stay[0:1].astype(jnp.float32), (16, 128))
            esend[width:width + 16, 0:128] = turned.astype(jnp.bfloat16)
            esend[width:width + 16, 128:256] = turned.astype(jnp.bfloat16)
            for way in range(2):
                remote(esend, erecv.at[way], e_ss, e_rs, z_peer(2 * (2 * way - 1))).start()
        if s + 1 < nk:
            send_leaf(s + 1)
            send_own((s + 2) % nk)
    wait_bytes(erecv, e_rs)
    def pass_products(way):
        part = times(erecv[way, 0:width, :], pmat[way])
        turned = erecv[way, width:width + 16, 0:128].astype(jnp.float32)[0:1]
        ysend[way] = jnp.where(turned > 0.5, part, pltpu.roll(part, 64, 1))
        first = lax.rem(z + 2 - 4 * way + nz, nz) + x * nz
        for side in range(2):
            remote(
                ysend.at[way], yrecv.at[side, way], y_ss, y_rs,
                {"dev": lax.rem(first + 1 - 2 * side + ndev, ndev)},
            ).start()

    both_ways(pass_products)
    own_arrived(0)
    dense(0, 0, 0, [(0, nk - 1), (1, nk - 1)], [])
    fetches[6].wait()
    fetches[7].wait()
    diag = diag_v[...]
    inverse = 1.0 / diag
    for c in range(CH):
        split(wmat, c // 2, c % 2, dmat[0, c])
    base = rhs_v[...] - diag * start
    vsend[0:width, :] = pack_ghosts(base - times(esend[0:width, :], wmat[...]))
    vsend[width:width + 8, :] = pack_ghosts(jnp.broadcast_to(inverse * (1.0 / THETA), (8, 128)))
    for way, peer in enumerate((upper, lower)):
        remote(vsend, vrecv.at[way], v_ss, v_rs, peer).start()

    ghost_rows = []
    for h in range(2):
        values = [dmat[0, h * 2 + cp] for cp in range(2)]
        for way in range(2):
            values = [values[cp] + arrived(way, nk - 1, h, cp) for cp in range(2)]
        for cp in range(2):
            split(wmat, h, cp, values[cp])
        ghost_rows.append(values[1])

    for way, peer in enumerate((upper, lower)):
        chosen = jnp.where(ghost_s[0, 1 - way] == 0, ghost_rows[0], ghost_rows[1])
        high = chosen.astype(jnp.bfloat16)
        nsend[way, 0:64, :] = high
        nsend[way, 64:128, :] = (chosen - high.astype(jnp.float32)).astype(jnp.bfloat16)
        remote(nsend.at[way], nrecv.at[way], n_ss, n_rs, peer).start()

    def product(vec, columns):
        return times(vec.astype(jnp.bfloat16), wmat[:, columns:columns + 128])

    def own_part(vec):
        return diag * vec + product(vec, 0)

    def mixed(ref):
        return jnp.where(left, ref[0, 0:width, :], ref[1, 0:width, :])

    def mixed_scale(ref):
        return jnp.where(left[:8], ref[0, width:width + 8, :], ref[1, width:width + 8, :])[0:1]

    def inside(ghosts):
        return jnp.where(jnp.logical_or(from_lower, from_upper), ghosts, 0.0)

    def first_ghosts():
        wait_bytes(vrecv, v_rs)
        wait_bytes(yrecv, y_rs)
        parts = jnp.where(left, yrecv[0, 0] + yrecv[0, 1], yrecv[1, 0] + yrecv[1, 1])
        return inside(mixed_scale(vrecv) * (mixed(vrecv) - parts))

    def neighbour_part(vec, way):
        both = lax.dot_general(
            vec.astype(jnp.bfloat16), nrecv[way], (((1,), (1,)), ((), ())),
            preferred_element_type=jnp.float32,
        )
        return both + pltpu.roll(both, 64, 1)

    def next_ghosts(mine):
        far = jnp.where(jnp.logical_and(left, dev > 1), grecv[4].astype(jnp.float32), 0.0)
        below = jnp.where(left, far, mine)
        far = jnp.where(
            jnp.logical_and(jnp.logical_not(left), dev < ndev - 2),
            grecv[5].astype(jnp.float32), 0.0,
        )
        above = jnp.where(left, mine, far)
        summed = jnp.where(left, neighbour_part(below, 0), neighbour_part(above, 1))
        return inside(mixed(wrecv) - mixed_scale(wrecv) * summed)

    rho = 1.0 / SIGMA
    iterate = start
    residual = base - times(esend[0:width, :], wmat[...])
    direction = residual * (inverse * (1.0 / THETA))
    for step in range(1, STEPS):
        last = step == STEPS - 1
        if last:
            send_ghosts(1, direction)
            remote(gsend.at[1], grecv.at[4], g_ss, g_rs.at[2], upper2).start()
            remote(gsend.at[1], grecv.at[5], g_ss, g_rs.at[2], lower2).start()
        iterate = iterate + direction
        rest = residual - own_part(direction)
        rho_new = 1.0 / (2.0 * SIGMA - rho)
        gain = (2.0 * rho_new / DELTA) * inverse
        kept = (rho_new * rho) * direction + gain * rest
        if last:
            wsend[0:width, :] = pack_ghosts(kept)
            wsend[width:width + 8, :] = pack_ghosts(jnp.broadcast_to(gain, (8, 128)))
            for way, peer in enumerate((upper, lower)):
                remote(wsend, wrecv.at[way], w_ss, w_rs, peer).start()
        ghosts = product(ghosts_of(1) if last else first_ghosts(), 128)
        direction = kept - gain * ghosts
        residual = rest - ghosts
        rho = rho_new
    out_v[...] = iterate + direction
    out_copy = pltpu.make_async_copy(out_v, out_ref.at[0], out_sem)
    out_copy.start()
    rest = residual - own_part(direction)
    wait_bytes(nrecv, n_rs)
    wait_bytes(grecv.at[pl.ds(4, 2)], g_rs.at[2])
    wait_bytes(wrecv, w_rs)
    residual = rest - product(next_ghosts(gsend[1].astype(jnp.float32)), 128)

    squares = jnp.sum((residual * residual).T, axis=0, keepdims=True)
    part = jnp.concatenate([squares, jnp.zeros((1, 128 - width), jnp.float32)], axis=1)
    for buf, ss, rs, here, count, peer in (
        (red_c, red_c_ss, red_c_rs, core, cores, core_peer),
        (red_p, red_p_ss, red_p_rs, plane, chips, plane_peer),
        (red_z, red_z_ss, red_z_rs, z, nz, z_peer),
    ):
        if count == 1:
            continue
        buf[here] = part
        for n in range(1, count):
            remote(buf.at[here], buf.at[here], ss, rs, peer(n)).start()
        wait_bytes(buf.at[pl.ds(0, count - 1)], rs)
        part = buf[0]
        for n in range(1, count):
            part = part + buf[n]
    rms_ref[...] = jnp.sqrt(part * (1.0 / (ng * ndev * 128)))[:, :width]

    out_copy.wait()
    wait_bytes(psend.at[pl.ds(oc, far_row + nx - oc)], p_ss)
    wait_bytes(bsend.at[pl.ds(0, own_slot + (nx - 1) * oc)], b_ss)
    wait_bytes(qsend, q_ss)
    wait_bytes(ssend, s_ss)
    wait_bytes(grecv, g_ss)
    wait_bytes(nsend, n_ss)
    wait_bytes(wrecv, w_ss)
    wait_bytes(erecv, e_ss)
    wait_bytes(yrecv, y_ss)
    wait_bytes(vrecv, v_ss)
    if cores > 1:
        wait_bytes(red_c.at[pl.ds(0, 1)], red_c_ss)
    wait_bytes(red_p.at[pl.ds(0, chips - 1)], red_p_ss)
    wait_bytes(red_z.at[pl.ds(0, nz - 1)], red_z_ss)


def shards(ng, nx, nz, tiles, owner, tile_rows, tile_cols, ghost_rows, rhs, start, diag):
    tcount, block = tiles.shape[1], tiles.shape[2]
    width = rhs.shape[1]
    nk = nz // 4
    f32, bf16, i32, i16 = jnp.float32, jnp.bfloat16, jnp.int32, jnp.int16
    vmem, smem, dma = pltpu.VMEM, pltpu.SMEM, pltpu.SemaphoreType.DMA
    whole = pl.BlockSpec(memory_space=pltpu.VMEM)
    smoothed, rms = pl.pallas_call(
        functools.partial(kernel, ng, nx, nz),
        out_shape=(
            jax.ShapeDtypeStruct((1, width, 128), f32),
            jax.ShapeDtypeStruct((1, width), f32),
        ),
        in_specs=[pl.BlockSpec(memory_space=pltpu.HBM)] * 8,
        out_specs=(pl.BlockSpec(memory_space=pltpu.HBM), whole),
        scratch_shapes=[
            smem((1, tcount), i32),
            smem((1, tcount), i32),
            smem((1, tcount), i32),
            smem((1, 2), i32),
            vmem((tcount, block, block), bf16),
            vmem((width, 128), f32),
            vmem((width, 128), f32),
            vmem((1, 128), f32),
            vmem((8, 128), i32),
            smem((8, 128), i32),
            vmem((nx * (4 * nk), 1, 128), i32),
            vmem((nx * (4 * nk), 1, 128), i32),
            vmem((nx * 4 * nk, 64, 128), bf16),
            vmem((nx, 2 * nk - 1, 64, 128), bf16),
            vmem((2, nk, nx, 64, 128), bf16),
            vmem((nx, 64, 128), bf16),
            vmem((2, CH, 64, 128), f32),
            vmem((2, nk - 1, 2, 2, 64, 128), i16),
            vmem((2, nk - 1, 2, 2, 64, 128), i16),
            vmem((2, nk - 1, 2, 2, 1, 128), f32),
            vmem((2, nk - 1, 2, 2, 1, 128), f32),
            vmem((256, 256), bf16),
            vmem((2, width, 128), bf16),
            vmem((6, width, 128), bf16),
            vmem((2, 128, 128), bf16),
            vmem((2, 128, 128), bf16),
            vmem((width + 8, 128), f32),
            vmem((2, width + 8, 128), f32),
            vmem((width + 16, 256), bf16),
            vmem((2, width + 16, 256), bf16),
            vmem((2, 256, 256), bf16),
            vmem((2, width, 128), f32),
            vmem((2, 2, width, 128), f32),
            vmem((width + 8, 128), f32),
            vmem((2, width + 8, 128), f32),
            vmem((2, 1, 128), f32),
            vmem((ng * nx, 1, 128), f32),
            vmem((nz, 1, 128), f32),
            vmem((width, 128), f32),
            dma((8,)),
            dma,
            dma,
            dma,
            dma,
            dma,
            dma((nk,)),
            dma((2, nk)),
            dma((2,)),
            dma,
            dma((2, nk - 1, 2, 2)),
            dma,
            dma((2, nk - 1, 2, 2)),
            dma,
            dma((3,)),
            dma,
            dma,
            dma,
            dma,
            dma,
            dma,
            dma,
            dma,
            dma,
            dma,
            dma,
            dma,
            dma,
            dma,
            dma,
            dma,
        ],
        compiler_params=pltpu.CompilerParams(
            collective_id=0, has_side_effects=True, vmem_limit_bytes=60 * 1024 * 1024
        ),
    )(owner.reshape(1, tcount), tile_rows, tile_cols, ghost_rows, tiles, rhs, start, diag)
    return smoothed, rms.reshape(width)


def solution(mesh):
    ng = mesh.shape["grp"]
    nx = mesh.shape["dev"] // NZ
    return jax.shard_map(
        functools.partial(shards, ng, nx, NZ),
        mesh=mesh,
        in_specs=(
            P("grp", "dev", None, None),
            P("grp", "dev", None),
            P("grp", "dev"),
            P("grp", "dev"),
            P("grp", "dev"),
            P("grp", None, "dev"),
            P("grp", None, "dev"),
            P("grp", "dev"),
        ),
        out_specs=(P("grp", None, "dev"), P()),
        check_vma=False,
    )
```
